32 devices in a mesh: groups: 2 (over x), mset: 16 (over z, y, core).
Axes of the slice: x: 2, y: 2, z: 4, core: 2. Of those that a mesh axis runs over, the one named last changes fastest.
Arguments:
- m_list: int32 [16], replicated, may hold values from 1536 to 3071, as said below
- coeff: bfloat16 [32, 32, 1536], P(('groups', 'mset')), parts along dimension 0, may hold values from -6 to 6
- blocks: bfloat16 [32, 1536, 1536], P(('groups', 'mset')), parts along dimension 0, may hold values from -0.15625 to 0.15625
- legendre: bfloat16 [512, 16, 1536], P(('groups', 'mset')), parts along dimension 0, may hold values from -0.15625 to 0.15625
Outputs:
- sky_map: bfloat16 [512, 16, 8192], P(('groups', 'mset')), parts along dimension 0
The draws below stay inside these ranges and needn't reach their ends.
There are 2 independent parts, one for each index of `groups`. The reference program is written for one: setup_inputs(seed, part) draws one part's arguments, and reference() takes and returns one part's arrays. A program takes and returns all parts, laid end to end along the dimension named above; an argument that names none is the same for every part. Nothing has to cross between parts.
Inputs may be any that keep to these rules, and one draw needn't show every extreme that they name: `m_list`: 16 distinct values; the value 3072 - 1536, a block of full order 1536, is always among them.
All inputs are finite; a program needn't handle non-finite values.
Results may differ from the reference program's by a relative error of at most 0.0062.
Values may be sent and summed in bfloat16 or wider, within the bound.
No kernel may reach another device: no remote copies, remote signals or barrier semaphores. Data moves between devices by JAX's collectives and lax.ppermute only.
A program may use at most 64 MiB of HBM per device.

```python
import math
import jax
import jax.numpy as jnp
from jax import lax

LL = 3072
LB = 1536
REAL = 16
COLS = 32
NPHI = 8192
M_SUB = 16
CYCLES = 256


def draw_m_list(key, part):
    shuffled = jax.random.permutation(jax.random.fold_in(key, 11), LB).astype(jnp.int32)
    target = jax.random.randint(jax.random.fold_in(key, 12), (), 0, M_SUB).astype(jnp.int32)
    zero_pos = jnp.argmax(shuffled == 0).astype(jnp.int32)
    moved_value = shuffled[target]
    shuffled = shuffled.at[zero_pos].set(moved_value)
    shuffled = shuffled.at[target].set(jnp.int32(0))
    return (LL - LB + shuffled[:M_SUB]).astype(jnp.int32)


def shard_levels(rng, shape, shards, least, high):
    def one(dim, parts):
        heights = jax.random.uniform(jax.random.fold_in(jax.random.fold_in(rng, 6), dim), (parts,), jnp.float32, least / len(shards), high / len(shards))
        return jnp.repeat(jnp.exp(heights), shape[dim] // parts).reshape((-1,) + (1,) * (len(shape) - dim - 1))

    level = one(*shards[0])
    for cut in shards[1:]:
        level = level * one(*cut)
    return level


def scatter_about(own_key, dims, scale, bound, pieces=(), kind=jnp.bfloat16):
    gain = shard_levels(own_key, dims, pieces, -0.22, 0.18) if pieces else 1.0
    array = jax.random.normal(own_key, dims, jnp.float32) * scale * gain
    return jnp.minimum(jnp.maximum(array, -bound), bound).astype(kind)


def setup_inputs(seed: int = 0, part: int = 0) -> dict:
    arg_keys = jax.random.split(jax.random.key(seed), 5)
    part_keys = jax.random.split(jax.random.fold_in(arg_keys[4], part), 5)
    return {
        "m_list": draw_m_list(jax.random.fold_in(arg_keys[4], 71), part),
        "coeff": scatter_about(part_keys[1], (M_SUB, COLS, LB), 1.0, 6.0, ((0, 16),)),
        "blocks": scatter_about(part_keys[2], (M_SUB, LB, LB), LB ** -0.5, 0.15625, ((0, 16),)),
        "legendre": scatter_about(part_keys[3], (CYCLES, M_SUB, LB), LB ** -0.5, 0.15625, ((0, 16),)),
    }


def fourier_table(m_values, pixels):
    pixel_index = jnp.arange(pixels, dtype=jnp.int32)
    phases = m_values.astype(jnp.int32)[:, None] * pixel_index[None, :] % pixels
    angles = phases.astype(jnp.float32) * (2.0 * math.pi / pixels)
    cos_part = jnp.cos(angles).astype(jnp.bfloat16)
    sin_part = jnp.sin(angles).astype(jnp.bfloat16)
    return jnp.concatenate([cos_part, -sin_part], axis=0)

def reference(m_list, coeff, blocks, legendre):
    orders = (LL - m_list).astype(jnp.int32)
    valid_mask = jnp.arange(LB, dtype=jnp.int32)[None, :] < orders[:, None]

    def block_apply(items):
        column_block, inverse, valid_row = items
        masked = jnp.where(valid_row[None, :], column_block, jnp.zeros_like(column_block))
        products = jnp.dot(masked.astype(jnp.float32), inverse.astype(jnp.float32), preferred_element_type=jnp.float32)
        return jnp.where(valid_row[None, :], products, jnp.zeros_like(products)).astype(jnp.bfloat16)
    filtered = lax.map(block_apply, (coeff, blocks, valid_mask))
    filtered_wide = filtered.astype(jnp.float32)

    def cycle_sum(cycle_table):
        return jnp.einsum('mj,mcj->mc', cycle_table.astype(jnp.float32), filtered_wide).astype(jnp.bfloat16)
    harmonics = lax.map(cycle_sum, legendre)
    real_part = harmonics[:, :, :REAL]
    imag_part = harmonics[:, :, REAL:]
    stacked = jnp.concatenate([real_part, imag_part], axis=1)
    flattened = jnp.transpose(stacked, (0, 2, 1)).reshape(CYCLES * REAL, 2 * M_SUB)
    trig_table = fourier_table(m_list, NPHI)
    summed = jnp.dot(flattened.astype(jnp.float32), trig_table.astype(jnp.float32), preferred_element_type=jnp.float32)
    scaled = summed * (1.0 / math.sqrt(M_SUB))
    return scaled.astype(jnp.bfloat16).reshape(CYCLES, REAL, NPHI)
```

```python
import math

import jax
import jax.numpy as jnp
from jax import lax
from jax.sharding import PartitionSpec as P

LL = 3072
REAL = 16
NPHI = 8192


def fourier_table(m_values, pixels):
    pixel_index = jnp.arange(pixels, dtype=jnp.int32)
    phases = m_values[:, None] * pixel_index[None, :] % pixels
    angles = phases.astype(jnp.float32) * (2.0 * math.pi / pixels)
    cos_part = jnp.cos(angles).astype(jnp.bfloat16)
    sin_part = jnp.sin(angles).astype(jnp.bfloat16)
    return jnp.concatenate([cos_part, -sin_part], axis=0)


def body(m_list, coeff, blocks, legendre):
    per_device = coeff.shape[0]
    order_max = coeff.shape[2]
    first_slot = lax.axis_index("mset") * per_device
    own_m = lax.dynamic_slice_in_dim(m_list, first_slot, per_device)
    orders = LL - own_m
    valid_mask = jnp.arange(order_max, dtype=jnp.int32)[None, :] < orders[:, None]
    masked = jnp.where(valid_mask[:, None, :], coeff, jnp.zeros_like(coeff))
    products = jnp.einsum("mcj,mjk->mck", masked, blocks, preferred_element_type=jnp.float32)
    filtered = jnp.where(valid_mask[:, None, :], products, jnp.zeros_like(products)).astype(
        jnp.bfloat16
    )
    gathered = lax.all_gather(filtered, "mset", axis=0, tiled=True)
    harmonics = jnp.einsum(
        "rij,icj->irc", legendre, gathered, preferred_element_type=jnp.float32
    ).astype(jnp.bfloat16)
    subset_size, cycle_count, _ = harmonics.shape
    parts = harmonics.reshape(subset_size, cycle_count, 2, REAL)
    flattened = jnp.transpose(parts, (1, 3, 2, 0)).reshape(cycle_count * REAL, 2 * subset_size)
    trig_table = fourier_table(m_list, NPHI)
    summed_map = jnp.dot(flattened, trig_table, preferred_element_type=jnp.float32)
    scaled = summed_map * (1.0 / math.sqrt(subset_size))
    return scaled.astype(jnp.bfloat16).reshape(cycle_count, REAL, NPHI)


def solution(mesh):
    in_specs = (
        P(),
        P(("groups", "mset"), None, None),
        P(("groups", "mset"), None, None),
        P(("groups", "mset"), None, None),
    )
    out_specs = P(("groups", "mset"), None, None)
    return jax.shard_map(body, mesh=mesh, in_specs=in_specs, out_specs=out_specs, check_vma=False)
```

```python
import functools
import math

import jax
import jax.numpy as jnp
from jax import lax
from jax.experimental import pallas as pl
from jax.experimental.pallas import tpu as pltpu
from jax.sharding import PartitionSpec as P

LL = 3072
REAL = 16
NPHI = 8192
LANES = 128
BF16 = jnp.bfloat16
F32 = jnp.float32


def filter_kernel(per_device, m_ref, coeff_ref, block_ref, out_ref):
    slot, tile = pl.program_id(0), pl.program_id(1)
    order = LL - m_ref[lax.axis_index("mset") * per_device + slot]
    coeff = coeff_ref[...]
    rows = lax.broadcasted_iota(jnp.int32, coeff.shape, 1)
    masked = jnp.where(rows < order, coeff, jnp.zeros_like(coeff))
    product = jnp.dot(masked, block_ref[...], preferred_element_type=F32)
    width = product.shape[1]
    cols = lax.broadcasted_iota(jnp.int32, product.shape, 1) + tile * width
    out_ref[...] = jnp.where(cols < order, product, 0.0).astype(BF16)


def filter_blocks(m_list, coeff, blocks):
    per_device, columns, order_max = coeff.shape
    width = min(256, order_max)
    return pl.pallas_call(
        functools.partial(filter_kernel, per_device),
        out_shape=jax.ShapeDtypeStruct(coeff.shape, BF16),
        grid=(per_device, order_max // width),
        in_specs=[
            pl.BlockSpec(memory_space=pltpu.SMEM),
            pl.BlockSpec((None, columns, order_max), lambda s, t: (s, 0, 0)),
            pl.BlockSpec((None, order_max, width), lambda s, t: (s, 0, t)),
        ],
        out_specs=pl.BlockSpec((None, columns, width), lambda s, t: (s, 0, t)),
        compiler_params=pltpu.CompilerParams(vmem_limit_bytes=16 << 20),
        cost_estimate=pl.CostEstimate(
            flops=2 * coeff.size * order_max,
            bytes_accessed=2 * (blocks.size + 2 * coeff.size),
            transcendentals=0,
        ),
        name="filter_blocks",
    )(m_list, coeff, blocks)


def trig_kernel(m_ref, out_ref):
    n = out_ref.shape[0] // 2
    me = lax.axis_index("mset")
    per_device = n // lax.axis_size("mset")
    steps = NPHI // LANES

    def m_columns(width):
        index = lax.broadcasted_iota(jnp.int32, (n, width), 0)
        values = jnp.zeros((n, width), jnp.int32)
        for k in range(n):
            source = (me ^ (k // per_device)) * per_device + k % per_device
            values = jnp.where(index == k, m_ref[source], values)
        return values

    def angle(phase):
        phase = phase & (NPHI - 1)
        phase = jnp.where(phase >= NPHI // 2, phase - NPHI, phase)
        return phase.astype(F32) * (2.0 * math.pi / NPHI)

    values = m_columns(LANES)
    lane = lax.broadcasted_iota(jnp.int32, (n, LANES), 1)
    fine = angle(values * lane)
    coarse = angle(values * lane * LANES)
    cos_f, sin_f = jnp.cos(fine), jnp.sin(fine)
    cos_c, sin_c = jnp.cos(coarse), jnp.sin(coarse)
    for a in range(steps):
        ca, sa = cos_c[:, a : a + 1], sin_c[:, a : a + 1]
        span = slice(a * LANES, (a + 1) * LANES)
        out_ref[:n, span] = (ca * cos_f - sa * sin_f).astype(BF16)
        out_ref[n:, span] = (-(sa * cos_f + ca * sin_f)).astype(BF16)


def trig_table(m_list):
    rows = 2 * m_list.shape[0]
    return pl.pallas_call(
        trig_kernel,
        out_shape=jax.ShapeDtypeStruct((rows, NPHI), BF16),
        in_specs=[pl.BlockSpec(memory_space=pltpu.SMEM)],
        out_specs=pl.BlockSpec(memory_space=pltpu.VMEM),
        compiler_params=pltpu.CompilerParams(vmem_limit_bytes=16 << 20),
        cost_estimate=pl.CostEstimate(
            flops=8 * rows * NPHI, bytes_accessed=2 * rows * NPHI, transcendentals=0
        ),
        name="trig_table",
    )(m_list)


def synthesis_kernel(shards, chunk, tiles, *refs):
    leg_ref, table_ref = refs[0], refs[1]
    shard_refs = refs[2 : 2 + shards]
    out_ref, held, sems = refs[2 + shards :]
    me = lax.axis_index("mset")
    rows = leg_ref.shape[0]
    per_device, columns, _ = shard_refs[0].shape
    n = shards * per_device
    cycles = rows // n
    out_rows = cycles * REAL
    wide = chunk * per_device * columns
    legendre = leg_ref[...]

    row_m = lax.rem(lax.broadcasted_iota(jnp.int32, (rows, wide), 0), n)
    local = lax.broadcasted_iota(jnp.int32, (rows, wide), 1) // columns
    same_cycle = (
        lax.broadcasted_iota(jnp.int32, (out_rows, rows), 0) // REAL
        == lax.broadcasted_iota(jnp.int32, (out_rows, rows), 1) // n
    ).astype(BF16)
    same_real = lax.rem(lax.broadcasted_iota(jnp.int32, (out_rows, wide), 0), REAL) == lax.rem(
        lax.broadcasted_iota(jnp.int32, (out_rows, wide), 1), REAL
    )
    pick_row = lax.broadcasted_iota(jnp.int32, (wide, 2 * n), 0)
    pick_col = lax.broadcasted_iota(jnp.int32, (wide, 2 * n), 1)
    part = lax.rem(pick_row, columns) // REAL

    flat = jnp.zeros((out_rows, 2 * n), F32)
    for q in range(shards // chunk):
        piece = jnp.concatenate(
            [shard_refs[q * chunk + k][...].reshape(per_device * columns, -1) for k in range(chunk)],
            axis=0,
        )
        cross = lax.dot_general(
            legendre, piece, (((1,), (1,)), ((), ())), preferred_element_type=F32
        )
        slot = q * chunk + local // per_device
        source = (me ^ slot) * per_device + lax.rem(local, per_device)
        own = jnp.where(row_m == source, cross, 0.0).astype(BF16)
        spread = jnp.dot(same_cycle, own, preferred_element_type=F32)
        chosen = jnp.where(same_real, spread, 0.0).astype(BF16)
        pick = (part * n + q * chunk * per_device + pick_row // columns == pick_col).astype(BF16)
        flat += jnp.dot(chosen, pick, preferred_element_type=F32)
    flat = flat.astype(BF16)

    width = NPHI // tiles
    copies = []
    for t in range(tiles):
        span = pl.ds(t * width, width)
        summed = jnp.dot(flat, table_ref[:, span], preferred_element_type=F32)
        held[:, span] = (summed * (1.0 / math.sqrt(n))).astype(BF16)
        copy = pltpu.make_async_copy(held.at[:, span], out_ref.at[:, span], sems.at[t])
        copy.start()
        copies.append(copy)
    for copy in copies:
        copy.wait()


def synthesize(legendre, table, shards):
    cycles, n, order_max = legendre.shape
    count = len(shards)
    chunk = min(8, count)
    tiles = 8
    out_rows = cycles * REAL
    return pl.pallas_call(
        functools.partial(synthesis_kernel, count, chunk, tiles),
        out_shape=jax.ShapeDtypeStruct((out_rows, NPHI), BF16),
        in_specs=[pl.BlockSpec(memory_space=pltpu.VMEM)] * (2 + count),
        out_specs=pl.BlockSpec(memory_space=pl.ANY),
        scratch_shapes=[pltpu.VMEM((out_rows, NPHI), BF16), pltpu.SemaphoreType.DMA((tiles,))],
        compiler_params=pltpu.CompilerParams(vmem_limit_bytes=48 << 20),
        cost_estimate=pl.CostEstimate(
            flops=4 * out_rows * n * NPHI,
            bytes_accessed=2 * (out_rows * NPHI + legendre.size + table.size),
            transcendentals=0,
        ),
        name="legendre_synthesis",
    )(legendre.reshape(cycles * n, order_max), table, *shards)


def exchange(value, size, mask):
    return lax.ppermute(value, "mset", [(d, d ^ mask) for d in range(size)])


def gather_xor(value):
    size = lax.axis_size("mset")
    shards = {0: value}
    bits = size.bit_length() - 1
    stages = [[1 << b] for b in range(min(2, bits))]
    rest = list(range(2, bits))
    for low in range(0, len(rest), 2):
        pair = [1 << b for b in rest[low : low + 2]]
        masks = pair if len(pair) == 1 else [pair[0], pair[1], pair[0] | pair[1]]
        stages.append(masks)
    for masks in reversed(stages):
        fresh = {}
        for mask in masks:
            for k, shard in shards.items():
                fresh[k | mask] = exchange(shard, size, mask)
        shards.update(fresh)
    return [shards[k] for k in range(size)]


def body(m_list, coeff, blocks, legendre):
    filtered = filter_blocks(m_list, coeff, blocks)
    shards = gather_xor(filtered)
    table = trig_table(m_list)
    sky_map = synthesize(legendre, table, shards)
    return sky_map.reshape(legendre.shape[0], REAL, NPHI)


def solution(mesh):
    in_specs = (
        P(),
        P(("groups", "mset"), None, None),
        P(("groups", "mset"), None, None),
        P(("groups", "mset"), None, None),
    )
    out_specs = P(("groups", "mset"), None, None)
    return jax.shard_map(body, mesh=mesh, in_specs=in_specs, out_specs=out_specs, check_vma=False)
```

```python
import functools
import math

import jax
import jax.numpy as jnp
from jax import lax
from jax.experimental import pallas as pl
from jax.experimental.pallas import tpu as pltpu
from jax.sharding import PartitionSpec as P

LL = 3072
REAL = 16
NPHI = 8192
LANES = 128
BF16 = jnp.bfloat16
F32 = jnp.float32
VMEM = pl.BlockSpec(memory_space=pltpu.VMEM)
HBM = pl.BlockSpec(memory_space=pltpu.HBM)


def iota(shape, dim):
    return lax.broadcasted_iota(jnp.int32, shape, dim)


def insert_bit(value, bit, at):
    low = (1 << at) - 1
    return (value & low) | (bit << at) | ((value >> at) << (at + 1))


def remove_bit(value, at):
    low = (1 << at) - 1
    return (value & low) | ((value >> (at + 1)) << at)


def angle(phase):
    phase = phase & (NPHI - 1)
    phase = jnp.where(phase >= NPHI // 2, phase - NPHI, phase)
    return phase.astype(F32) * (2.0 * math.pi / NPHI)


def write_table(table_ref, m_smem, me, at):
    n = table_ref.shape[0] // 2
    index = iota((n, LANES), 0)
    lane = iota((n, LANES), 1)
    values = jnp.zeros((n, LANES), jnp.int32)
    for j in range(n):
        source = me ^ insert_bit(j % (n // 2), j // (n // 2), at)
        values = jnp.where(index == j, m_smem[source], values)
    fine = angle(values * lane)
    coarse = angle(values * lane * LANES)
    cos_f, sin_f = jnp.cos(fine), jnp.sin(fine)
    cos_c, sin_c = jnp.cos(coarse), jnp.sin(coarse)
    for a in range(NPHI // LANES):
        ca, sa = cos_c[:, a : a + 1], sin_c[:, a : a + 1]
        span = slice(a * LANES, (a + 1) * LANES)
        table_ref[:n, span] = (ca * cos_f - sa * sin_f).astype(BF16)
        table_ref[n:, span] = (-(sa * cos_f + ca * sin_f)).astype(BF16)


def prepare_kernel(
    at, m_ref, coeff_ref, block_ref, leg_ref, filtered_ref, keep_ref, send_ref, table_ref,
    m_smem, coeff_vmem, block_vmem, leg_vmem, sems,
):
    me = lax.axis_index("mset")
    columns, order_max = coeff_ref.shape
    pieces = block_vmem.shape[0]
    depth = order_max // pieces
    copy_m = pltpu.make_async_copy(m_ref, m_smem, sems.at[0])
    copy_leg = pltpu.make_async_copy(leg_ref, leg_vmem, sems.at[1])
    copy_coeff = pltpu.make_async_copy(coeff_ref, coeff_vmem, sems.at[2])
    copy_blocks = [
        pltpu.make_async_copy(
            block_ref.at[pl.ds(p * depth, depth), :], block_vmem.at[p], sems.at[3 + p]
        )
        for p in range(pieces)
    ]
    for copy in [copy_m, copy_leg, copy_coeff] + copy_blocks:
        copy.start()

    copy_m.wait()
    write_table(table_ref, m_smem, me, at)

    rows = leg_ref.shape[0]
    n = m_ref.shape[0]
    half = rows // 2
    own_bit = (me >> at) & 1
    row, col = iota((half, rows), 0), iota((half, rows), 1)
    same_cycle = row // (n // 2) == col // n
    slot = lax.rem(row, n // 2)
    copy_leg.wait()
    for ref, bit in ((keep_ref, own_bit), (send_ref, 1 - own_bit)):
        pick = same_cycle & (insert_bit(slot, bit, at) == lax.rem(col, n))
        ref[...] = jnp.dot(
            pick.astype(BF16), leg_vmem[...], preferred_element_type=F32
        ).astype(BF16)

    order = LL - m_smem[me]
    copy_coeff.wait()
    coeff = coeff_vmem[...]
    coeff = jnp.where(iota(coeff.shape, 1) < order, coeff, jnp.zeros_like(coeff))
    total = jnp.zeros((columns, order_max), F32)
    for p in range(pieces):
        copy_blocks[p].wait()
        total += jnp.dot(
            coeff[:, p * depth : (p + 1) * depth], block_vmem[p], preferred_element_type=F32
        )
    filtered_ref[...] = jnp.where(iota(total.shape, 1) < order, total, 0.0).astype(BF16)


def prepare(m_list, coeff, block, legendre, at):
    columns, order_max = coeff.shape
    rows = legendre.shape[0]
    n = m_list.shape[0]
    pieces = 6
    operands = (m_list, coeff, block, legendre)
    return pl.pallas_call(
        functools.partial(prepare_kernel, at),
        out_shape=[
            jax.ShapeDtypeStruct((columns, order_max), BF16),
            jax.ShapeDtypeStruct((rows // 2, order_max), BF16),
            jax.ShapeDtypeStruct((rows // 2, order_max), BF16),
            jax.ShapeDtypeStruct((2 * n, NPHI), BF16),
        ],
        in_specs=[HBM] * 4,
        out_specs=[VMEM] * 4,
        scratch_shapes=[
            pltpu.SMEM((n,), jnp.int32),
            pltpu.VMEM((columns, order_max), BF16),
            pltpu.VMEM((pieces, order_max // pieces, order_max), BF16),
            pltpu.VMEM((rows, order_max), BF16),
            pltpu.SemaphoreType.DMA((3 + pieces,)),
        ],
        compiler_params=pltpu.CompilerParams(vmem_limit_bytes=32 << 20),
        cost_estimate=pl.CostEstimate(
            flops=2 * (columns * order_max * order_max + rows * rows * order_max),
            bytes_accessed=2 * (block.size + legendre.size),
            transcendentals=0,
        ),
        name="prepare",
    )(*[pltpu.with_memory_space_constraint(x, pltpu.HBM) for x in operands])


def cross_kernel(at, n, shards, chunk, *refs):
    keep_ref, got_ref = refs[:2]
    shard_refs = refs[2 : 2 + shards]
    own_ref, back_ref = refs[2 + shards :]
    rest = remove_bit(lax.axis_index("mset"), at)
    half = keep_ref.shape[0]
    columns = shard_refs[0].shape[0]
    cycles = own_ref.shape[0]
    wide = chunk * columns
    slot = lax.rem(iota((half, wide), 0), shards)
    local = iota((half, wide), 1) // columns
    fold = (iota((cycles, half), 0) == iota((cycles, half), 1) // shards).astype(BF16)
    for q in range(shards // chunk):
        piece = jnp.concatenate(
            [shard_refs[q * chunk + k][...] for k in range(chunk)], axis=0
        )
        own = slot == (rest ^ (local + q * chunk))
        for source, target in ((keep_ref, own_ref), (got_ref, back_ref)):
            cross = lax.dot_general(
                source[...], piece, (((1,), (1,)), ((), ())), preferred_element_type=F32
            )
            chosen = jnp.where(own, cross, 0.0).astype(BF16)
            target[:, q * wide : (q + 1) * wide] = jnp.dot(
                fold, chosen, preferred_element_type=F32
            ).astype(BF16)


def cross(keep, got, shards, n, at):
    half, order_max = keep.shape
    columns = shards[0].shape[0]
    count = len(shards)
    cycles = half // count
    shape = jax.ShapeDtypeStruct((cycles, count * columns), BF16)
    return pl.pallas_call(
        functools.partial(cross_kernel, at, n, count, min(8, count)),
        out_shape=[shape, shape],
        in_specs=[VMEM] * (2 + count),
        out_specs=[VMEM] * 2,
        compiler_params=pltpu.CompilerParams(vmem_limit_bytes=32 << 20),
        cost_estimate=pl.CostEstimate(
            flops=4 * half * order_max * count * columns,
            bytes_accessed=2 * (2 * keep.size + count * shards[0].size),
            transcendentals=0,
        ),
        name="cross",
    )(keep, got, *shards)


def synthesis_kernel(tiles, columns, own_ref, got_ref, table_ref, out_ref, held, sems):
    cycles, half = own_ref.shape
    wide = 2 * half
    n = wide // columns
    out_rows = cycles * REAL
    joined = jnp.concatenate([own_ref[...], got_ref[...]], axis=1)
    repeat = (iota((out_rows, cycles), 0) // REAL == iota((out_rows, cycles), 1)).astype(BF16)
    spread = jnp.dot(repeat, joined, preferred_element_type=F32)
    same_real = lax.rem(iota((out_rows, wide), 0), REAL) == lax.rem(
        iota((out_rows, wide), 1), REAL
    )
    chosen = jnp.where(same_real, spread, 0.0).astype(BF16)
    row, col = iota((wide, 2 * n), 0), iota((wide, 2 * n), 1)
    pick = (lax.rem(row, columns) // REAL * n + row // columns == col).astype(BF16)
    flat = jnp.dot(chosen, pick, preferred_element_type=F32).astype(BF16)

    width = NPHI // tiles
    copies = []
    for t in range(tiles):
        span = pl.ds(t * width, width)
        summed = jnp.dot(flat, table_ref[:, span], preferred_element_type=F32)
        held[:, span] = (summed * (1.0 / math.sqrt(n))).astype(BF16)
        copy = pltpu.make_async_copy(held.at[:, span], out_ref.at[:, span], sems.at[t])
        copy.start()
        copies.append(copy)
    for copy in copies:
        copy.wait()


def synthesize(own, got, table, columns):
    cycles = own.shape[0]
    tiles = 8
    out_rows = cycles * REAL
    return pl.pallas_call(
        functools.partial(synthesis_kernel, tiles, columns),
        out_shape=jax.ShapeDtypeStruct((out_rows, NPHI), BF16),
        in_specs=[VMEM] * 3,
        out_specs=HBM,
        scratch_shapes=[pltpu.VMEM((out_rows, NPHI), BF16), pltpu.SemaphoreType.DMA((tiles,))],
        compiler_params=pltpu.CompilerParams(vmem_limit_bytes=32 << 20),
        cost_estimate=pl.CostEstimate(
            flops=2 * out_rows * table.size,
            bytes_accessed=2 * (out_rows * NPHI + table.size),
            transcendentals=0,
        ),
        name="synthesis",
    )(own, got, table)


def exchange(value, size, mask):
    return lax.ppermute(value, "mset", [(d, d ^ mask) for d in range(size)])


def gather_xor(value, size, at):
    shards = {0: value}
    bits = [b for b in range(size.bit_length() - 1) if b != at]
    for b in reversed(bits):
        shards.update({k | 1 << b: exchange(v, size, 1 << b) for k, v in shards.items()})
    return [shards[k] for k in sorted(shards)]


def body(m_list, coeff, blocks, legendre):
    size = lax.axis_size("mset")
    per_device, columns, order_max = coeff.shape
    if per_device != 1 or size & (size - 1):
        raise ValueError("unsupported mesh")
    cycles, n, _ = legendre.shape
    at = min(2, size.bit_length() - 2)
    filtered, keep, send, table = prepare(
        m_list, coeff[0], blocks[0], legendre.reshape(cycles * n, order_max), at
    )
    got = exchange(send, size, 1 << at)
    shards = gather_xor(filtered, size, at)
    own, back = cross(keep, got, shards, n, at)
    other = exchange(back, size, 1 << at)
    sky_map = synthesize(own, other, table, columns)
    return sky_map.reshape(cycles, REAL, NPHI)


def solution(mesh):
    in_specs = (
        P(),
        P(("groups", "mset"), None, None),
        P(("groups", "mset"), None, None),
        P(("groups", "mset"), None, None),
    )
    out_specs = P(("groups", "mset"), None, None)
    return jax.shard_map(body, mesh=mesh, in_specs=in_specs, out_specs=out_specs, check_vma=False)
```

```python
import functools
import math

import jax
import jax.numpy as jnp
from jax import lax
from jax.experimental import pallas as pl
from jax.experimental.pallas import tpu as pltpu
from jax.sharding import PartitionSpec as P

LL = 3072
REAL = 16
NPHI = 8192
LANES = 128
BF16 = jnp.bfloat16
F32 = jnp.float32
VMEM = pl.BlockSpec(memory_space=pltpu.VMEM)
HBM = pl.BlockSpec(memory_space=pltpu.HBM)


def iota(shape, dim):
    return lax.broadcasted_iota(jnp.int32, shape, dim)


def angle(phase):
    phase = phase & (NPHI - 1)
    phase = jnp.where(phase >= NPHI // 2, phase - NPHI, phase)
    return phase.astype(F32) * (2.0 * math.pi / NPHI)


def write_table(table_ref, m_smem, quad):
    n = table_ref.shape[0] // 2
    line = n // quad
    index = iota((n, LANES), 0)
    lane = iota((n, LANES), 1)
    values = jnp.zeros((n, LANES), jnp.int32)
    for j in range(n):
        values = jnp.where(index == j, m_smem[j % line * quad + j // line], values)
    fine = angle(values * lane)
    coarse = angle(values * lane * LANES)
    cos_f, sin_f = jnp.cos(fine), jnp.sin(fine)
    cos_c, sin_c = jnp.cos(coarse), jnp.sin(coarse)
    for a in range(NPHI // LANES):
        ca, sa = cos_c[:, a : a + 1], sin_c[:, a : a + 1]
        span = slice(a * LANES, (a + 1) * LANES)
        table_ref[:n, span] = (ca * cos_f - sa * sin_f).astype(BF16)
        table_ref[n:, span] = (-(sa * cos_f + ca * sin_f)).astype(BF16)


def prepare_kernel(
    quad, m_ref, coeff_ref, block_ref, leg_ref, filtered_ref, send_ref, table_ref,
    m_smem, coeff_vmem, block_vmem, leg_vmem, sems,
):
    me = lax.axis_index("mset")
    columns, order_max = coeff_ref.shape
    pieces = block_vmem.shape[0]
    depth = order_max // pieces
    copy_m = pltpu.make_async_copy(m_ref, m_smem, sems.at[0])
    copy_leg = pltpu.make_async_copy(leg_ref, leg_vmem, sems.at[1])
    copy_coeff = pltpu.make_async_copy(coeff_ref, coeff_vmem, sems.at[2])
    copy_blocks = [
        pltpu.make_async_copy(
            block_ref.at[pl.ds(p * depth, depth), :], block_vmem.at[p], sems.at[3 + p]
        )
        for p in range(pieces)
    ]
    for copy in [copy_m, copy_leg, copy_coeff] + copy_blocks:
        copy.start()

    copy_m.wait()
    write_table(table_ref, m_smem, quad)

    rows = leg_ref.shape[0]
    n = m_ref.shape[0]
    line = n // quad
    share = rows // quad
    row, col = iota((share, rows), 0), iota((share, rows), 1)
    wanted = row // line * n + lax.rem(row, line) * quad
    copy_leg.wait()
    for low in range(quad):
        pick = (wanted + low == col).astype(BF16)
        send_ref[low] = jnp.dot(pick, leg_vmem[...], preferred_element_type=F32).astype(BF16)

    order = LL - m_smem[me]
    copy_coeff.wait()
    coeff = coeff_vmem[...]
    coeff = jnp.where(iota(coeff.shape, 1) < order, coeff, jnp.zeros_like(coeff))
    total = jnp.zeros((columns, order_max), F32)
    for p in range(pieces):
        copy_blocks[p].wait()
        total += jnp.dot(
            coeff[:, p * depth : (p + 1) * depth], block_vmem[p], preferred_element_type=F32
        )
    filtered = jnp.where(iota(total.shape, 1) < order, total, 0.0).astype(BF16)
    for z in range(line):
        filtered_ref[z] = filtered


def prepare(m_list, coeff, block, legendre, quad):
    columns, order_max = coeff.shape
    rows = legendre.shape[0]
    n = m_list.shape[0]
    pieces = 6
    operands = (m_list, coeff, block, legendre)
    return pl.pallas_call(
        functools.partial(prepare_kernel, quad),
        out_shape=[
            jax.ShapeDtypeStruct((n // quad, columns, order_max), BF16),
            jax.ShapeDtypeStruct((quad, rows // quad, order_max), BF16),
            jax.ShapeDtypeStruct((2 * n, NPHI), BF16),
        ],
        in_specs=[HBM] * 4,
        out_specs=[VMEM] * 3,
        scratch_shapes=[
            pltpu.SMEM((n,), jnp.int32),
            pltpu.VMEM((columns, order_max), BF16),
            pltpu.VMEM((pieces, order_max // pieces, order_max), BF16),
            pltpu.VMEM((rows, order_max), BF16),
            pltpu.SemaphoreType.DMA((3 + pieces,)),
        ],
        compiler_params=pltpu.CompilerParams(vmem_limit_bytes=32 << 20),
        cost_estimate=pl.CostEstimate(
            flops=2 * (columns * order_max * order_max + rows * rows * order_max),
            bytes_accessed=2 * (block.size + legendre.size),
            transcendentals=0,
        ),
        name="prepare",
    )(*[pltpu.with_memory_space_constraint(x, pltpu.HBM) for x in operands])


def cross_kernel(chunk, leg_ref, filtered_ref, out_ref):
    quad, share, order_max = leg_ref.shape
    line, columns, _ = filtered_ref.shape
    cycles = share // line
    rows = quad * share
    wide = chunk * columns
    legendre = leg_ref[...].reshape(rows, order_max)
    slot = lax.rem(iota((rows, wide), 0), line)
    local = iota((rows, wide), 1) // columns
    fold = (iota((quad * cycles, rows), 0) == iota((quad * cycles, rows), 1) // line).astype(BF16)
    for q in range(line // chunk):
        piece = filtered_ref[q * chunk : (q + 1) * chunk].reshape(wide, order_max)
        product = lax.dot_general(
            legendre, piece, (((1,), (1,)), ((), ())), preferred_element_type=F32
        )
        chosen = jnp.where(slot == local + q * chunk, product, 0.0).astype(BF16)
        folded = jnp.dot(fold, chosen, preferred_element_type=F32).astype(BF16)
        out_ref[:, :, q * wide : (q + 1) * wide] = folded.reshape(quad, cycles, wide)


def cross(legendre, filtered):
    quad, share, order_max = legendre.shape
    line, columns, _ = filtered.shape
    return pl.pallas_call(
        functools.partial(cross_kernel, min(8, line)),
        out_shape=jax.ShapeDtypeStruct((quad, share // line, line * columns), BF16),
        in_specs=[VMEM] * 2,
        out_specs=VMEM,
        compiler_params=pltpu.CompilerParams(vmem_limit_bytes=32 << 20),
        cost_estimate=pl.CostEstimate(
            flops=2 * legendre.size * line * columns,
            bytes_accessed=2 * (legendre.size + filtered.size),
            transcendentals=0,
        ),
        name="cross",
    )(legendre, filtered)


def synthesis_kernel(tiles, columns, parts_ref, table_ref, out_ref, held, sems):
    quad, cycles, part = parts_ref.shape
    wide = quad * part
    n = wide // columns
    out_rows = cycles * REAL
    joined = jnp.concatenate([parts_ref[low] for low in range(quad)], axis=1)
    repeat = (iota((out_rows, cycles), 0) // REAL == iota((out_rows, cycles), 1)).astype(BF16)
    spread = jnp.dot(repeat, joined, preferred_element_type=F32)
    same_real = lax.rem(iota((out_rows, wide), 0), REAL) == lax.rem(
        iota((out_rows, wide), 1), REAL
    )
    chosen = jnp.where(same_real, spread, 0.0).astype(BF16)
    row, col = iota((wide, 2 * n), 0), iota((wide, 2 * n), 1)
    pick = (lax.rem(row, columns) // REAL * n + row // columns == col).astype(BF16)
    flat = jnp.dot(chosen, pick, preferred_element_type=F32).astype(BF16)

    width = NPHI // tiles
    copies = []
    for t in range(tiles):
        span = pl.ds(t * width, width)
        summed = jnp.dot(flat, table_ref[:, span], preferred_element_type=F32)
        held[:, span] = (summed * (1.0 / math.sqrt(n))).astype(BF16)
        copy = pltpu.make_async_copy(held.at[:, span], out_ref.at[:, span], sems.at[t])
        copy.start()
        copies.append(copy)
    for copy in copies:
        copy.wait()


def synthesize(parts, table, columns):
    cycles = parts.shape[1]
    tiles = 8
    out_rows = cycles * REAL
    return pl.pallas_call(
        functools.partial(synthesis_kernel, tiles, columns),
        out_shape=jax.ShapeDtypeStruct((out_rows, NPHI), BF16),
        in_specs=[VMEM] * 2,
        out_specs=HBM,
        scratch_shapes=[pltpu.VMEM((out_rows, NPHI), BF16), pltpu.SemaphoreType.DMA((tiles,))],
        compiler_params=pltpu.CompilerParams(vmem_limit_bytes=32 << 20),
        cost_estimate=pl.CostEstimate(
            flops=2 * out_rows * table.size,
            bytes_accessed=2 * (out_rows * NPHI + table.size),
            transcendentals=0,
        ),
        name="synthesis",
    )(parts, table)


def swap(value, groups):
    return lax.all_to_all(
        value, "mset", split_axis=0, concat_axis=0, axis_index_groups=groups, tiled=True
    )


def body(m_list, coeff, blocks, legendre):
    size = lax.axis_size("mset")
    per_device, columns, order_max = coeff.shape
    quad = min(4, size)
    if per_device != 1 or size % quad:
        raise ValueError("unsupported mesh")
    cycles, n, _ = legendre.shape
    quads = [list(range(d, d + quad)) for d in range(0, size, quad)]
    lines = [list(range(low, size, quad)) for low in range(quad)]
    filtered, send, table = prepare(
        m_list, coeff[0], blocks[0], legendre.reshape(cycles * n, order_max), quad
    )
    shared = swap(send, quads)
    shards = swap(filtered, lines)
    parts = swap(cross(shared, shards), quads)
    sky_map = synthesize(parts, table, columns)
    return sky_map.reshape(cycles, REAL, NPHI)


def solution(mesh):
    in_specs = (
        P(),
        P(("groups", "mset"), None, None),
        P(("groups", "mset"), None, None),
        P(("groups", "mset"), None, None),
    )
    out_specs = P(("groups", "mset"), None, None)
    return jax.shard_map(body, mesh=mesh, in_specs=in_specs, out_specs=out_specs, check_vma=False)
```

```python
import functools
import math

import jax
import jax.numpy as jnp
from jax import lax
from jax.experimental import pallas as pl
from jax.experimental.pallas import tpu as pltpu
from jax.sharding import PartitionSpec as P

LL = 3072
REAL = 16
NPHI = 8192
LANES = 128
BF16 = jnp.bfloat16
F32 = jnp.float32
VMEM = pl.BlockSpec(memory_space=pltpu.VMEM)
HBM = pl.BlockSpec(memory_space=pltpu.HBM)


def iota(shape, dim):
    return lax.broadcasted_iota(jnp.int32, shape, dim)


def insert_bit(value, bit, at):
    low = (1 << at) - 1
    return (value & low) | (bit << at) | ((value >> at) << (at + 1))


def remove_bit(value, at):
    low = (1 << at) - 1
    return (value & low) | ((value >> (at + 1)) << at)


def angle(phase):
    phase = phase & (NPHI - 1)
    phase = jnp.where(phase >= NPHI // 2, phase - NPHI, phase)
    return phase.astype(F32) * (2.0 * math.pi / NPHI)


def write_table(table_ref, m_smem, me, at):
    n = table_ref.shape[0] // 2
    index = iota((n, LANES), 0)
    lane = iota((n, LANES), 1)
    values = jnp.zeros((n, LANES), jnp.int32)
    for j in range(n):
        source = me ^ insert_bit(j % (n // 2), j // (n // 2), at)
        values = jnp.where(index == j, m_smem[source], values)
    fine = angle(values * lane)
    coarse = angle(values * lane * LANES)
    cos_f, sin_f = jnp.cos(fine), jnp.sin(fine)
    cos_c, sin_c = jnp.cos(coarse), jnp.sin(coarse)
    for a in range(NPHI // LANES):
        ca, sa = cos_c[:, a : a + 1], sin_c[:, a : a + 1]
        span = slice(a * LANES, (a + 1) * LANES)
        table_ref[:n, span] = (ca * cos_f - sa * sin_f).astype(BF16)
        table_ref[n:, span] = (-(sa * cos_f + ca * sin_f)).astype(BF16)


def prepare_kernel(
    at, m_ref, coeff_ref, block_ref, leg_ref, filtered_ref, keep_ref, send_ref, table_ref,
    m_smem, coeff_vmem, block_vmem, leg_vmem, sems,
):
    me = lax.axis_index("mset")
    columns, order_max = coeff_ref.shape
    pieces = block_vmem.shape[0]
    depth = order_max // pieces
    copy_m = pltpu.make_async_copy(m_ref, m_smem, sems.at[0])
    copy_leg = pltpu.make_async_copy(leg_ref, leg_vmem, sems.at[1])
    copy_coeff = pltpu.make_async_copy(coeff_ref, coeff_vmem, sems.at[2])
    copy_blocks = [
        pltpu.make_async_copy(
            block_ref.at[pl.ds(p * depth, depth), :], block_vmem.at[p], sems.at[3 + p]
        )
        for p in range(pieces)
    ]
    for copy in [copy_m, copy_leg, copy_coeff] + copy_blocks:
        copy.start()

    copy_m.wait()
    write_table(table_ref, m_smem, me, at)

    rows = leg_ref.shape[0]
    n = m_ref.shape[0]
    half = rows // 2
    own_bit = (me >> at) & 1
    row, col = iota((half, rows), 0), iota((half, rows), 1)
    same_cycle = row // (n // 2) == col // n
    slot = lax.rem(row, n // 2)
    copy_leg.wait()
    for ref, bit in ((keep_ref, own_bit), (send_ref, 1 - own_bit)):
        pick = same_cycle & (insert_bit(slot, bit, at) == lax.rem(col, n))
        ref[...] = jnp.dot(
            pick.astype(BF16), leg_vmem[...], preferred_element_type=F32
        ).astype(BF16)

    order = LL - m_smem[me]
    copy_coeff.wait()
    coeff = coeff_vmem[...]
    coeff = jnp.where(iota(coeff.shape, 1) < order, coeff, jnp.zeros_like(coeff))
    total = jnp.zeros((columns, order_max), F32)
    for p in range(pieces):
        copy_blocks[p].wait()
        total += jnp.dot(
            coeff[:, p * depth : (p + 1) * depth], block_vmem[p], preferred_element_type=F32
        )
    filtered_ref[...] = jnp.where(iota(total.shape, 1) < order, total, 0.0).astype(BF16)


def prepare(m_list, coeff, block, legendre, at):
    columns, order_max = coeff.shape
    rows = legendre.shape[0]
    n = m_list.shape[0]
    pieces = 6
    operands = (m_list, coeff, block, legendre)
    return pl.pallas_call(
        functools.partial(prepare_kernel, at),
        out_shape=[
            jax.ShapeDtypeStruct((columns, order_max), BF16),
            jax.ShapeDtypeStruct((rows // 2, order_max), BF16),
            jax.ShapeDtypeStruct((rows // 2, order_max), BF16),
            jax.ShapeDtypeStruct((2 * n, NPHI), BF16),
        ],
        in_specs=[HBM] * 4,
        out_specs=[VMEM] * 4,
        scratch_shapes=[
            pltpu.SMEM((n,), jnp.int32),
            pltpu.VMEM((columns, order_max), BF16),
            pltpu.VMEM((pieces, order_max // pieces, order_max), BF16),
            pltpu.VMEM((rows, order_max), BF16),
            pltpu.SemaphoreType.DMA((3 + pieces,)),
        ],
        compiler_params=pltpu.CompilerParams(vmem_limit_bytes=32 << 20),
        cost_estimate=pl.CostEstimate(
            flops=2 * (columns * order_max * order_max + rows * rows * order_max),
            bytes_accessed=2 * (block.size + legendre.size),
            transcendentals=0,
        ),
        name="prepare",
    )(*[pltpu.with_memory_space_constraint(x, pltpu.HBM) for x in operands])


def cross_kernel(at, n, shards, chunk, *refs):
    keep_ref, got_ref = refs[:2]
    shard_refs = refs[2 : 2 + shards]
    own_ref, back_ref = refs[2 + shards :]
    rest = remove_bit(lax.axis_index("mset"), at)
    half = keep_ref.shape[0]
    columns = shard_refs[0].shape[0]
    cycles = own_ref.shape[0]
    wide = chunk * columns
    slot = lax.rem(iota((half, wide), 0), shards)
    local = iota((half, wide), 1) // columns
    fold = (iota((cycles, half), 0) == iota((cycles, half), 1) // shards).astype(BF16)
    for q in range(shards // chunk):
        piece = jnp.concatenate(
            [shard_refs[q * chunk + k][...] for k in range(chunk)], axis=0
        )
        own = slot == (rest ^ (local + q * chunk))
        for source, target in ((keep_ref, own_ref), (got_ref, back_ref)):
            cross = lax.dot_general(
                source[...], piece, (((1,), (1,)), ((), ())), preferred_element_type=F32
            )
            chosen = jnp.where(own, cross, 0.0).astype(BF16)
            target[:, q * wide : (q + 1) * wide] = jnp.dot(
                fold, chosen, preferred_element_type=F32
            ).astype(BF16)


def cross(keep, got, shards, n, at):
    half, order_max = keep.shape
    columns = shards[0].shape[0]
    count = len(shards)
    cycles = half // count
    shape = jax.ShapeDtypeStruct((cycles, count * columns), BF16)
    return pl.pallas_call(
        functools.partial(cross_kernel, at, n, count, min(8, count)),
        out_shape=[shape, shape],
        in_specs=[VMEM] * (2 + count),
        out_specs=[VMEM] * 2,
        compiler_params=pltpu.CompilerParams(vmem_limit_bytes=32 << 20),
        cost_estimate=pl.CostEstimate(
            flops=4 * half * order_max * count * columns,
            bytes_accessed=2 * (2 * keep.size + count * shards[0].size),
            transcendentals=0,
        ),
        name="cross",
    )(keep, got, *shards)


def synthesis_kernel(tiles, columns, own_ref, got_ref, table_ref, out_ref, held, sems):
    cycles, half = own_ref.shape
    wide = 2 * half
    n = wide // columns
    out_rows = cycles * REAL
    joined = jnp.concatenate([own_ref[...], got_ref[...]], axis=1)
    repeat = (iota((out_rows, cycles), 0) // REAL == iota((out_rows, cycles), 1)).astype(BF16)
    spread = jnp.dot(repeat, joined, preferred_element_type=F32)
    same_real = lax.rem(iota((out_rows, wide), 0), REAL) == lax.rem(
        iota((out_rows, wide), 1), REAL
    )
    chosen = jnp.where(same_real, spread, 0.0).astype(BF16)
    row, col = iota((wide, 2 * n), 0), iota((wide, 2 * n), 1)
    pick = (lax.rem(row, columns) // REAL * n + row // columns == col).astype(BF16)
    flat = jnp.dot(chosen, pick, preferred_element_type=F32).astype(BF16)

    width = NPHI // tiles
    copies = []
    for t in range(tiles):
        span = pl.ds(t * width, width)
        summed = jnp.dot(flat, table_ref[:, span], preferred_element_type=F32)
        held[:, span] = (summed * (1.0 / math.sqrt(n))).astype(BF16)
        copy = pltpu.make_async_copy(held.at[:, span], out_ref.at[:, span], sems.at[t])
        copy.start()
        copies.append(copy)
    for copy in copies:
        copy.wait()


def synthesize(own, got, table, columns):
    cycles = own.shape[0]
    tiles = 8
    out_rows = cycles * REAL
    return pl.pallas_call(
        functools.partial(synthesis_kernel, tiles, columns),
        out_shape=jax.ShapeDtypeStruct((out_rows, NPHI), BF16),
        in_specs=[VMEM] * 3,
        out_specs=HBM,
        scratch_shapes=[pltpu.VMEM((out_rows, NPHI), BF16), pltpu.SemaphoreType.DMA((tiles,))],
        compiler_params=pltpu.CompilerParams(vmem_limit_bytes=32 << 20),
        cost_estimate=pl.CostEstimate(
            flops=2 * out_rows * table.size,
            bytes_accessed=2 * (out_rows * NPHI + table.size),
            transcendentals=0,
        ),
        name="synthesis",
    )(own, got, table)


def exchange(value, size, mask):
    return lax.ppermute(value, "mset", [(d, d ^ mask) for d in range(size)])


def gather_xor(value, size, at):
    shards = {0: value}
    top = size.bit_length() - 1
    stages = [[b, b + 1] if b + 1 < top else [b] for b in range(2, top, 2)]
    stages = [[b] for b in range(min(2, top)) if b != at] + stages
    for bits in reversed(stages):
        masks = [sum(1 << b for e, b in enumerate(bits) if m >> e & 1) for m in range(1, 1 << len(bits))]
        shards.update({k | m: exchange(v, size, m) for m in masks for k, v in list(shards.items())})
    return [shards[k] for k in sorted(shards)]


def body(m_list, coeff, blocks, legendre):
    size = lax.axis_size("mset")
    per_device, columns, order_max = coeff.shape
    if per_device != 1 or size & (size - 1):
        raise ValueError("unsupported mesh")
    cycles, n, _ = legendre.shape
    at = min(1, size.bit_length() - 2)
    filtered, keep, send, table = prepare(
        m_list, coeff[0], blocks[0], legendre.reshape(cycles * n, order_max), at
    )
    shards = gather_xor(filtered, size, at)
    got = exchange(send, size, 1 << at)
    own, back = cross(keep, got, shards, n, at)
    other = exchange(back, size, 1 << at)
    sky_map = synthesize(own, other, table, columns)
    return sky_map.reshape(cycles, REAL, NPHI)


def solution(mesh):
    in_specs = (
        P(),
        P(("groups", "mset"), None, None),
        P(("groups", "mset"), None, None),
        P(("groups", "mset"), None, None),
    )
    out_specs = P(("groups", "mset"), None, None)
    return jax.shard_map(body, mesh=mesh, in_specs=in_specs, out_specs=out_specs, check_vma=False)
```

```python
import functools
import math

import jax
import jax.numpy as jnp
from jax import lax
from jax.experimental import pallas as pl
from jax.experimental.pallas import tpu as pltpu
from jax.sharding import PartitionSpec as P

LL = 3072
REAL = 16
NPHI = 8192
LANES = 128
BF16 = jnp.bfloat16
F32 = jnp.float32
VMEM = pl.BlockSpec(memory_space=pltpu.VMEM)
HBM = pl.BlockSpec(memory_space=pltpu.HBM)


def iota(shape, dim):
    return lax.broadcasted_iota(jnp.int32, shape, dim)


def insert_bit(value, bit, at):
    low = (1 << at) - 1
    return (value & low) | (bit << at) | ((value >> at) << (at + 1))


def remove_bit(value, at):
    low = (1 << at) - 1
    return (value & low) | ((value >> (at + 1)) << at)


def angle(phase):
    phase = phase & (NPHI - 1)
    phase = jnp.where(phase >= NPHI // 2, phase - NPHI, phase)
    return phase.astype(F32) * (2.0 * math.pi / NPHI)


def write_table(table_ref, m_smem, me, at):
    n = table_ref.shape[0] // 2
    index = iota((n, LANES), 0)
    lane = iota((n, LANES), 1)
    values = jnp.zeros((n, LANES), jnp.int32)
    for j in range(n):
        source = me ^ insert_bit(j % (n // 2), j // (n // 2), at)
        values = jnp.where(index == j, m_smem[source], values)
    fine = angle(values * lane)
    coarse = angle(values * lane * LANES)
    cos_f, sin_f = jnp.cos(fine), jnp.sin(fine)
    cos_c, sin_c = jnp.cos(coarse), jnp.sin(coarse)
    for a in range(NPHI // LANES):
        ca, sa = cos_c[:, a : a + 1], sin_c[:, a : a + 1]
        span = slice(a * LANES, (a + 1) * LANES)
        table_ref[:n, span] = (ca * cos_f - sa * sin_f).astype(BF16)
        table_ref[n:, span] = (-(sa * cos_f + ca * sin_f)).astype(BF16)


def prepare_kernel(
    at, m_ref, coeff_ref, block_ref, leg_ref, filtered_ref, keep_ref, send_ref,
    m_smem, coeff_vmem, block_vmem, leg_vmem, sems,
):
    me = lax.axis_index("mset")
    columns, order_max = coeff_ref.shape
    pieces = block_vmem.shape[0]
    depth = order_max // pieces
    copy_m = pltpu.make_async_copy(m_ref, m_smem, sems.at[0])
    copy_leg = pltpu.make_async_copy(leg_ref, leg_vmem, sems.at[1])
    copy_coeff = pltpu.make_async_copy(coeff_ref, coeff_vmem, sems.at[2])
    copy_blocks = [
        pltpu.make_async_copy(
            block_ref.at[pl.ds(p * depth, depth), :], block_vmem.at[p], sems.at[3 + p]
        )
        for p in range(pieces)
    ]
    for copy in [copy_m, copy_leg, copy_coeff] + copy_blocks:
        copy.start()

    rows = leg_ref.shape[0]
    n = m_ref.shape[0]
    half = rows // 2
    own_bit = (me >> at) & 1
    row, col = iota((half, rows), 0), iota((half, rows), 1)
    same_cycle = row // (n // 2) == col // n
    slot = lax.rem(row, n // 2)
    copy_leg.wait()
    for ref, bit in ((keep_ref, own_bit), (send_ref, 1 - own_bit)):
        pick = same_cycle & (insert_bit(slot, bit, at) == lax.rem(col, n))
        ref[...] = jnp.dot(
            pick.astype(BF16), leg_vmem[...], preferred_element_type=F32
        ).astype(BF16)

    copy_m.wait()
    order = LL - m_smem[me]
    copy_coeff.wait()
    coeff = coeff_vmem[...]
    coeff = jnp.where(iota(coeff.shape, 1) < order, coeff, jnp.zeros_like(coeff))
    total = jnp.zeros((columns, order_max), F32)
    for p in range(pieces):
        copy_blocks[p].wait()
        total += jnp.dot(
            coeff[:, p * depth : (p + 1) * depth], block_vmem[p], preferred_element_type=F32
        )
    filtered_ref[...] = jnp.where(iota(total.shape, 1) < order, total, 0.0).astype(BF16)


def prepare(m_list, coeff, block, legendre, at):
    columns, order_max = coeff.shape
    rows = legendre.shape[0]
    n = m_list.shape[0]
    pieces = 6
    operands = (m_list, coeff, block, legendre)
    return pl.pallas_call(
        functools.partial(prepare_kernel, at),
        out_shape=[
            jax.ShapeDtypeStruct((columns, order_max), BF16),
            jax.ShapeDtypeStruct((rows // 2, order_max), BF16),
            jax.ShapeDtypeStruct((rows // 2, order_max), BF16),
        ],
        in_specs=[HBM] * 4,
        out_specs=[VMEM] * 3,
        scratch_shapes=[
            pltpu.SMEM((n,), jnp.int32),
            pltpu.VMEM((columns, order_max), BF16),
            pltpu.VMEM((pieces, order_max // pieces, order_max), BF16),
            pltpu.VMEM((rows, order_max), BF16),
            pltpu.SemaphoreType.DMA((3 + pieces,)),
        ],
        compiler_params=pltpu.CompilerParams(vmem_limit_bytes=32 << 20),
        cost_estimate=pl.CostEstimate(
            flops=2 * (columns * order_max * order_max + rows * rows * order_max),
            bytes_accessed=2 * (block.size + legendre.size),
            transcendentals=0,
        ),
        name="prepare",
    )(*[pltpu.with_memory_space_constraint(x, pltpu.HBM) for x in operands])


def trig_kernel(at, m_ref, after_ref, table_ref):
    write_table(table_ref, m_ref, lax.axis_index("mset"), at)


def trig_table(m_list, after, at):
    rows = 2 * m_list.shape[0]
    return pl.pallas_call(
        functools.partial(trig_kernel, at),
        out_shape=jax.ShapeDtypeStruct((rows, NPHI), BF16),
        in_specs=[pl.BlockSpec(memory_space=pltpu.SMEM), pl.BlockSpec(memory_space=pl.ANY)],
        out_specs=VMEM,
        compiler_params=pltpu.CompilerParams(vmem_limit_bytes=16 << 20),
        cost_estimate=pl.CostEstimate(
            flops=8 * rows * NPHI, bytes_accessed=2 * rows * NPHI, transcendentals=0
        ),
        name="trig_table",
    )(m_list, after)


def cross_kernel(at, shards, chunk, *refs):
    keep_ref, got_ref = refs[:2]
    shard_refs = refs[2 : 2 + shards]
    own_ref, back_ref = refs[2 + shards :]
    rest = remove_bit(lax.axis_index("mset"), at)
    half = keep_ref.shape[0]
    columns = shard_refs[0].shape[0]
    cycles = own_ref.shape[0]
    wide = chunk * columns
    legendre = jnp.concatenate([keep_ref[...], got_ref[...]], axis=0)
    slot = lax.rem(iota((2 * half, wide), 0), shards)
    local = iota((2 * half, wide), 1) // columns
    fold = iota((2 * cycles, 2 * half), 0) == iota((2 * cycles, 2 * half), 1) // shards
    fold = fold.astype(BF16)
    for q in range(shards // chunk):
        piece = jnp.concatenate(
            [shard_refs[q * chunk + k][...] for k in range(chunk)], axis=0
        )
        product = lax.dot_general(
            legendre, piece, (((1,), (1,)), ((), ())), preferred_element_type=F32
        )
        own = slot == (rest ^ (local + q * chunk))
        chosen = jnp.where(own, product, 0.0).astype(BF16)
        folded = jnp.dot(fold, chosen, preferred_element_type=F32).astype(BF16)
        own_ref[:, q * wide : (q + 1) * wide] = folded[:cycles]
        back_ref[:, q * wide : (q + 1) * wide] = folded[cycles:]


def cross(keep, got, shards, at):
    half, order_max = keep.shape
    columns = shards[0].shape[0]
    count = len(shards)
    cycles = half // count
    shape = jax.ShapeDtypeStruct((cycles, count * columns), BF16)
    return pl.pallas_call(
        functools.partial(cross_kernel, at, count, min(8, count)),
        out_shape=[shape, shape],
        in_specs=[VMEM] * (2 + count),
        out_specs=[VMEM] * 2,
        compiler_params=pltpu.CompilerParams(vmem_limit_bytes=32 << 20),
        cost_estimate=pl.CostEstimate(
            flops=4 * half * order_max * count * columns,
            bytes_accessed=2 * (2 * keep.size + count * shards[0].size),
            transcendentals=0,
        ),
        name="cross",
    )(keep, got, *shards)


def synthesis_kernel(tiles, columns, own_ref, got_ref, table_ref, out_ref, held, sems):
    cycles, half = own_ref.shape
    wide = 2 * half
    n = wide // columns
    out_rows = cycles * REAL
    joined = jnp.concatenate([own_ref[...], got_ref[...]], axis=1)
    repeat = (iota((out_rows, cycles), 0) // REAL == iota((out_rows, cycles), 1)).astype(BF16)
    spread = jnp.dot(repeat, joined, preferred_element_type=F32)
    same_real = lax.rem(iota((out_rows, wide), 0), REAL) == lax.rem(
        iota((out_rows, wide), 1), REAL
    )
    chosen = jnp.where(same_real, spread, 0.0).astype(BF16)
    row, col = iota((wide, 2 * n), 0), iota((wide, 2 * n), 1)
    pick = (lax.rem(row, columns) // REAL * n + row // columns == col).astype(BF16)
    flat = jnp.dot(chosen, pick, preferred_element_type=F32).astype(BF16)

    width = NPHI // tiles
    copies = []
    for t in range(tiles):
        span = pl.ds(t * width, width)
        summed = jnp.dot(flat, table_ref[:, span], preferred_element_type=F32)
        held[:, span] = (summed * (1.0 / math.sqrt(n))).astype(BF16)
        copy = pltpu.make_async_copy(held.at[:, span], out_ref.at[:, span], sems.at[t])
        copy.start()
        copies.append(copy)
    for copy in copies:
        copy.wait()


def synthesize(own, got, table, columns):
    cycles = own.shape[0]
    tiles = 8
    out_rows = cycles * REAL
    return pl.pallas_call(
        functools.partial(synthesis_kernel, tiles, columns),
        out_shape=jax.ShapeDtypeStruct((out_rows, NPHI), BF16),
        in_specs=[VMEM] * 3,
        out_specs=HBM,
        scratch_shapes=[pltpu.VMEM((out_rows, NPHI), BF16), pltpu.SemaphoreType.DMA((tiles,))],
        compiler_params=pltpu.CompilerParams(vmem_limit_bytes=32 << 20),
        cost_estimate=pl.CostEstimate(
            flops=2 * out_rows * table.size,
            bytes_accessed=2 * (out_rows * NPHI + table.size),
            transcendentals=0,
        ),
        name="synthesis",
    )(own, got, table)


def exchange(value, size, mask):
    return lax.ppermute(value, "mset", [(d, d ^ mask) for d in range(size)])


def gather_xor(value, size, at):
    bits = [b for b in range(size.bit_length() - 1) if b != at]
    shards = {0: value}
    for b in reversed(bits):
        shards.update({k | 1 << b: exchange(v, size, 1 << b) for k, v in shards.items()})
    return [shards[k] for k in sorted(shards)]


def body(m_list, coeff, blocks, legendre):
    size = lax.axis_size("mset")
    per_device, columns, order_max = coeff.shape
    if per_device != 1 or size & (size - 1):
        raise ValueError("unsupported mesh")
    cycles, n, _ = legendre.shape
    at = min(1, size.bit_length() - 2)
    filtered, keep, send = prepare(
        m_list, coeff[0], blocks[0], legendre.reshape(cycles * n, order_max), at
    )
    shards = gather_xor(filtered, size, at)
    got = exchange(send, size, 1 << at)
    own, back = cross(keep, got, shards, at)
    other = exchange(back, size, 1 << at)
    table = trig_table(m_list, own, at)
    sky_map = synthesize(own, other, table, columns)
    return sky_map.reshape(cycles, REAL, NPHI)


def solution(mesh):
    in_specs = (
        P(),
        P(("groups", "mset"), None, None),
        P(("groups", "mset"), None, None),
        P(("groups", "mset"), None, None),
    )
    out_specs = P(("groups", "mset"), None, None)
    return jax.shard_map(body, mesh=mesh, in_specs=in_specs, out_specs=out_specs, check_vma=False)
```

```python
import functools
import math

import jax
import jax.numpy as jnp
from jax import lax
from jax.experimental import pallas as pl
from jax.experimental.pallas import tpu as pltpu
from jax.sharding import PartitionSpec as P

LL = 3072
REAL = 16
NPHI = 8192
LANES = 128
BF16 = jnp.bfloat16
F32 = jnp.float32
VMEM = pl.BlockSpec(memory_space=pltpu.VMEM)
HBM = pl.BlockSpec(memory_space=pltpu.HBM)


def iota(shape, dim):
    return lax.broadcasted_iota(jnp.int32, shape, dim)


def insert_bit(value, bit, at):
    low = (1 << at) - 1
    return (value & low) | (bit << at) | ((value >> at) << (at + 1))


def remove_bit(value, at):
    low = (1 << at) - 1
    return (value & low) | ((value >> (at + 1)) << at)


def angle(phase):
    phase = phase & (NPHI - 1)
    phase = jnp.where(phase >= NPHI // 2, phase - NPHI, phase)
    return phase.astype(F32) * (2.0 * math.pi / NPHI)


def write_table(table_ref, m_ref, me, at):
    n = table_ref.shape[0] // 2
    half = n // 2
    index = iota((n, LANES), 0)
    lane = iota((n, LANES), 1)
    values = jnp.zeros((n, LANES), jnp.int32)
    for j in range(n):
        source = me ^ insert_bit(j % half, j // half, at)
        values = jnp.where(index == j, m_ref[source], values)
    scale = 1.0 / math.sqrt(n)
    fine = angle(values * lane)
    coarse = angle(values * lane * LANES)
    cos_f, sin_f = jnp.cos(fine), jnp.sin(fine)
    cos_c, sin_c = jnp.cos(coarse), jnp.sin(coarse)
    for a in range(NPHI // LANES):
        ca, sa = cos_c[:, a : a + 1], sin_c[:, a : a + 1]
        span = slice(a * LANES, (a + 1) * LANES)
        cos_part = ((ca * cos_f - sa * sin_f).astype(BF16) * scale).astype(BF16)
        sin_part = ((-(sa * cos_f + ca * sin_f)).astype(BF16) * scale).astype(BF16)
        for h in range(2):
            rows = slice(h * half, (h + 1) * half)
            table_ref[2 * h * half : (2 * h + 1) * half, span] = cos_part[rows]
            table_ref[(2 * h + 1) * half : (2 * h + 2) * half, span] = sin_part[rows]


def prepare_kernel(
    at, m_ref, coeff_ref, block_ref, leg_ref, filtered_ref, keep_ref, send_ref,
    m_smem, coeff_vmem, block_vmem, leg_vmem, sems,
):
    me = lax.axis_index("mset")
    columns, order_max = coeff_ref.shape
    pieces = block_vmem.shape[0]
    depth = order_max // pieces
    copy_m = pltpu.make_async_copy(m_ref, m_smem, sems.at[0])
    copy_leg = pltpu.make_async_copy(leg_ref, leg_vmem, sems.at[1])
    copy_coeff = pltpu.make_async_copy(coeff_ref, coeff_vmem, sems.at[2])
    copy_blocks = [
        pltpu.make_async_copy(
            block_ref.at[pl.ds(p * depth, depth), :], block_vmem.at[p], sems.at[3 + p]
        )
        for p in range(pieces)
    ]
    for copy in [copy_m, copy_leg, copy_coeff] + copy_blocks:
        copy.start()

    rows = leg_ref.shape[0]
    n = m_ref.shape[0]
    half = rows // 2
    own_bit = (me >> at) & 1
    row, col = iota((rows, rows), 0), iota((rows, rows), 1)
    bit = own_bit ^ (row // half)
    slot = lax.rem(row, n // 2)
    pick = (lax.rem(row, half) // (n // 2) == col // n) & (
        insert_bit(slot, bit, at) == lax.rem(col, n)
    )
    pick = pick.astype(BF16)
    copy_leg.wait()
    ordered = jnp.dot(pick, leg_vmem[...], preferred_element_type=F32).astype(BF16)
    keep_ref[...] = ordered[:half]
    send_ref[...] = ordered[half:]

    copy_m.wait()
    order = LL - m_smem[me]
    copy_coeff.wait()
    coeff = coeff_vmem[...]
    coeff = jnp.where(iota(coeff.shape, 1) < order, coeff, jnp.zeros_like(coeff))
    total = jnp.zeros((columns, order_max), F32)
    for p in range(pieces):
        copy_blocks[p].wait()
        total += jnp.dot(
            coeff[:, p * depth : (p + 1) * depth], block_vmem[p], preferred_element_type=F32
        )
    filtered_ref[...] = jnp.where(iota(total.shape, 1) < order, total, 0.0).astype(BF16)


def prepare(m_list, coeff, block, legendre, at):
    columns, order_max = coeff.shape
    rows = legendre.shape[0]
    n = m_list.shape[0]
    pieces = 6
    operands = (m_list, coeff, block, legendre)
    return pl.pallas_call(
        functools.partial(prepare_kernel, at),
        out_shape=[
            jax.ShapeDtypeStruct((columns, order_max), BF16),
            jax.ShapeDtypeStruct((rows // 2, order_max), BF16),
            jax.ShapeDtypeStruct((rows // 2, order_max), BF16),
        ],
        in_specs=[HBM] * 4,
        out_specs=[VMEM] * 3,
        scratch_shapes=[
            pltpu.SMEM((n,), jnp.int32),
            pltpu.VMEM((columns, order_max), BF16),
            pltpu.VMEM((pieces, order_max // pieces, order_max), BF16),
            pltpu.VMEM((rows, order_max), BF16),
            pltpu.SemaphoreType.DMA((3 + pieces,)),
        ],
        compiler_params=pltpu.CompilerParams(vmem_limit_bytes=32 << 20),
        cost_estimate=pl.CostEstimate(
            flops=2 * (columns * order_max * order_max + rows * rows * order_max),
            bytes_accessed=2 * (block.size + legendre.size),
            transcendentals=0,
        ),
        name="prepare",
    )(*[pltpu.with_memory_space_constraint(x, pltpu.HBM) for x in operands])


def trig_kernel(at, m_ref, after_ref, table_ref):
    write_table(table_ref, m_ref, lax.axis_index("mset"), at)


def trig_table(m_list, after, at):
    rows = 2 * m_list.shape[0]
    return pl.pallas_call(
        functools.partial(trig_kernel, at),
        out_shape=jax.ShapeDtypeStruct((rows, NPHI), BF16),
        in_specs=[pl.BlockSpec(memory_space=pltpu.SMEM), pl.BlockSpec(memory_space=pl.ANY)],
        out_specs=VMEM,
        compiler_params=pltpu.CompilerParams(vmem_limit_bytes=16 << 20),
        cost_estimate=pl.CostEstimate(
            flops=8 * rows * NPHI, bytes_accessed=2 * rows * NPHI, transcendentals=0
        ),
        name="trig_table",
    )(m_list, after)


def cross_kernel(at, shards, chunk, *refs):
    keep_ref, got_ref = refs[:2]
    shard_refs = refs[2 : 2 + shards]
    own_ref, back_ref = refs[2 + shards :]
    rest = remove_bit(lax.axis_index("mset"), at)
    half = keep_ref.shape[0]
    columns = shard_refs[0].shape[0]
    out_rows = own_ref.shape[1]
    wide = chunk * columns
    legendre = jnp.concatenate([keep_ref[...], got_ref[...]], axis=0)
    slot = lax.rem(iota((2 * half, wide), 0), shards)
    local = iota((2 * half, wide), 1) // columns
    spread = iota((out_rows, half), 0) // REAL == iota((out_rows, half), 1) // shards
    spread = spread.astype(BF16)
    same_real = lax.rem(iota((out_rows, wide), 0), REAL) == lax.rem(
        iota((out_rows, wide), 1), REAL
    )
    row, col = iota((2 * shards, wide), 0), iota((2 * shards, wide), 1)
    totals = [jnp.zeros(own_ref.shape, F32) for _ in range(2)]
    for q in range(shards // chunk):
        piece = jnp.concatenate(
            [shard_refs[q * chunk + k][...] for k in range(chunk)], axis=0
        )
        product = lax.dot_general(
            legendre, piece, (((1,), (1,)), ((), ())), preferred_element_type=F32
        )
        own = slot == (rest ^ (local + q * chunk))
        chosen = jnp.where(own, product, 0.0).astype(BF16)
        pick = lax.rem(col, columns) // REAL * shards + q * chunk + col // columns == row
        pick = pick.astype(BF16)
        for h in range(2):
            wider = jnp.dot(
                spread, chosen[h * half : (h + 1) * half], preferred_element_type=F32
            )
            wider = jnp.where(same_real, wider, 0.0).astype(BF16)
            totals[h] += lax.dot_general(
                pick, wider, (((1,), (1,)), ((), ())), preferred_element_type=F32
            )
    own_ref[...] = totals[0].astype(BF16)
    back_ref[...] = totals[1].astype(BF16)


def cross(keep, got, shards, at):
    half, order_max = keep.shape
    columns = shards[0].shape[0]
    count = len(shards)
    shape = jax.ShapeDtypeStruct((2 * count, half // count * REAL), BF16)
    return pl.pallas_call(
        functools.partial(cross_kernel, at, count, min(8, count)),
        out_shape=[shape, shape],
        in_specs=[VMEM] * (2 + count),
        out_specs=[VMEM] * 2,
        compiler_params=pltpu.CompilerParams(vmem_limit_bytes=32 << 20),
        cost_estimate=pl.CostEstimate(
            flops=4 * half * order_max * count * columns,
            bytes_accessed=2 * (2 * keep.size + count * shards[0].size),
            transcendentals=0,
        ),
        name="cross",
    )(keep, got, *shards)


def synthesis_kernel(tiles, own_ref, got_ref, table_ref, out_ref, held, sems):
    flat = jnp.concatenate([own_ref[...], got_ref[...]], axis=0)
    width = NPHI // tiles
    copies = []
    for t in range(tiles):
        span = pl.ds(t * width, width)
        summed = lax.dot_general(
            flat, table_ref[:, span], (((0,), (0,)), ((), ())), preferred_element_type=F32
        )
        held[:, span] = summed.astype(BF16)
        copy = pltpu.make_async_copy(held.at[:, span], out_ref.at[:, span], sems.at[t])
        copy.start()
        copies.append(copy)
    for copy in copies:
        copy.wait()


def synthesize(own, got, table):
    tiles = 16
    out_rows = own.shape[1]
    return pl.pallas_call(
        functools.partial(synthesis_kernel, tiles),
        out_shape=jax.ShapeDtypeStruct((out_rows, NPHI), BF16),
        in_specs=[VMEM] * 3,
        out_specs=HBM,
        scratch_shapes=[pltpu.VMEM((out_rows, NPHI), BF16), pltpu.SemaphoreType.DMA((tiles,))],
        compiler_params=pltpu.CompilerParams(vmem_limit_bytes=32 << 20),
        cost_estimate=pl.CostEstimate(
            flops=2 * out_rows * table.size,
            bytes_accessed=2 * (out_rows * NPHI + table.size),
            transcendentals=0,
        ),
        name="synthesis",
    )(own, got, table)


def exchange(value, size, mask):
    return lax.ppermute(value, "mset", [(d, d ^ mask) for d in range(size)])


def gather_xor(value, size, at):
    shards = {0: value}
    top = size.bit_length() - 1
    stages = [[b, b + 1] if b + 1 < top else [b] for b in range(2, top, 2)]
    stages = [[b] for b in range(min(2, top)) if b != at] + stages
    for bits in reversed(stages):
        masks = [sum(1 << b for e, b in enumerate(bits) if m >> e & 1) for m in range(1, 1 << len(bits))]
        shards.update({k | m: exchange(v, size, m) for m in masks for k, v in list(shards.items())})
    return [shards[k] for k in sorted(shards)]


def body(m_list, coeff, blocks, legendre):
    size = lax.axis_size("mset")
    per_device, columns, order_max = coeff.shape
    if per_device != 1 or size & (size - 1):
        raise ValueError("unsupported mesh")
    cycles, n, _ = legendre.shape
    at = min(1, size.bit_length() - 2)
    filtered, keep, send = prepare(
        m_list, coeff[0], blocks[0], legendre.reshape(cycles * n, order_max), at
    )
    shards = gather_xor(filtered, size, at)
    got = exchange(send, size, 1 << at)
    own, back = cross(keep, got, shards, at)
    other = exchange(back, size, 1 << at)
    table = trig_table(m_list, own, at)
    sky_map = synthesize(own, other, table)
    return sky_map.reshape(cycles, REAL, NPHI)


def solution(mesh):
    in_specs = (
        P(),
        P(("groups", "mset"), None, None),
        P(("groups", "mset"), None, None),
        P(("groups", "mset"), None, None),
    )
    out_specs = P(("groups", "mset"), None, None)
    return jax.shard_map(body, mesh=mesh, in_specs=in_specs, out_specs=out_specs, check_vma=False)
```

```python
import functools
import math

import jax
import jax.numpy as jnp
from jax import lax
from jax.experimental import pallas as pl
from jax.experimental.pallas import tpu as pltpu
from jax.sharding import PartitionSpec as P

LL = 3072
REAL = 16
NPHI = 8192
LANES = 128
BF16 = jnp.bfloat16
F32 = jnp.float32
VMEM = pl.BlockSpec(memory_space=pltpu.VMEM)
HBM = pl.BlockSpec(memory_space=pltpu.HBM)


def iota(shape, dim):
    return lax.broadcasted_iota(jnp.int32, shape, dim)


def insert_bit(value, bit, at):
    low = (1 << at) - 1
    return (value & low) | (bit << at) | ((value >> at) << (at + 1))


def shard_source(position, me, at, line):
    z, other = me >> (at + 1), me & ((1 << at) - 1)
    turn, flip = position >> at, position & ((1 << at) - 1)
    return (((z - turn) & (line - 1)) << at) | (other ^ flip)


def angle(phase):
    phase = phase & (NPHI - 1)
    phase = jnp.where(phase >= NPHI // 2, phase - NPHI, phase)
    return phase.astype(F32) * (2.0 * math.pi / NPHI)


def write_table(table_ref, m_ref, me, at, line):
    n = table_ref.shape[0] // 2
    half = n // 2
    index = iota((n, LANES), 0)
    lane = iota((n, LANES), 1)
    own_bit = (me >> at) & 1
    values = jnp.zeros((n, LANES), jnp.int32)
    for j in range(n):
        source = insert_bit(shard_source(j % half, me, at, line), own_bit ^ (j // half), at)
        values = jnp.where(index == j, m_ref[source], values)
    scale = 1.0 / math.sqrt(n)
    fine = angle(values * lane)
    coarse = angle(values * lane * LANES)
    cos_f, sin_f = jnp.cos(fine), jnp.sin(fine)
    cos_c, sin_c = jnp.cos(coarse), jnp.sin(coarse)
    for a in range(NPHI // LANES):
        ca, sa = cos_c[:, a : a + 1], sin_c[:, a : a + 1]
        span = slice(a * LANES, (a + 1) * LANES)
        table_ref[:n, span] = ((ca * cos_f - sa * sin_f).astype(BF16) * scale).astype(BF16)
        table_ref[n:, span] = ((-(sa * cos_f + ca * sin_f)).astype(BF16) * scale).astype(BF16)


def map_rows(half_ref, first, total):
    cycles, wide = half_ref.shape
    rows = cycles * REAL
    repeat = (iota((rows, cycles), 0) // REAL == iota((rows, cycles), 1)).astype(BF16)
    spread = jnp.dot(repeat, half_ref[...], preferred_element_type=F32)
    same_real = lax.rem(iota((rows, wide), 0), REAL) == lax.rem(iota((rows, wide), 1), REAL)
    chosen = jnp.where(same_real, spread, 0.0).astype(BF16)
    row, col = iota((wide, 2 * total), 0), iota((wide, 2 * total), 1)
    pick = lax.rem(row, 2 * REAL) // REAL * total + first + row // (2 * REAL) == col
    return jnp.dot(chosen, pick.astype(BF16), preferred_element_type=F32)


def prepare_kernel(
    at, m_ref, coeff_ref, block_ref, leg_ref, filtered_ref, keep_ref, send_ref,
    m_smem, coeff_vmem, block_vmem, leg_vmem, sems,
):
    me = lax.axis_index("mset")
    columns, order_max = coeff_ref.shape
    pieces = block_vmem.shape[0]
    depth = order_max // pieces
    copy_m = pltpu.make_async_copy(m_ref, m_smem, sems.at[0])
    copy_leg = pltpu.make_async_copy(leg_ref, leg_vmem, sems.at[1])
    copy_coeff = pltpu.make_async_copy(coeff_ref, coeff_vmem, sems.at[2])
    copy_blocks = [
        pltpu.make_async_copy(
            block_ref.at[pl.ds(p * depth, depth), :], block_vmem.at[p], sems.at[3 + p]
        )
        for p in range(pieces)
    ]
    for copy in [copy_m, copy_leg, copy_coeff] + copy_blocks:
        copy.start()

    rows = leg_ref.shape[0]
    n = m_ref.shape[0]
    half = rows // 2
    own_bit = (me >> at) & 1
    row, col = iota((rows, rows), 0), iota((rows, rows), 1)
    bit = own_bit ^ (row // half)
    slot = lax.rem(row, n // 2)
    pick = (lax.rem(row, half) // (n // 2) == col // n) & (
        insert_bit(slot, bit, at) == lax.rem(col, n)
    )
    pick = pick.astype(BF16)
    copy_leg.wait()
    ordered = jnp.dot(pick, leg_vmem[...], preferred_element_type=F32).astype(BF16)
    keep_ref[...] = ordered[:half]
    send_ref[...] = ordered[half:]

    copy_m.wait()
    order = LL - m_smem[me]
    copy_coeff.wait()
    coeff = coeff_vmem[...]
    coeff = jnp.where(iota(coeff.shape, 1) < order, coeff, jnp.zeros_like(coeff))
    total = jnp.zeros((columns, order_max), F32)
    for p in range(pieces):
        copy_blocks[p].wait()
        total += jnp.dot(
            coeff[:, p * depth : (p + 1) * depth], block_vmem[p], preferred_element_type=F32
        )
    filtered_ref[...] = jnp.where(iota(total.shape, 1) < order, total, 0.0).astype(BF16)


def prepare(m_list, coeff, block, legendre, at):
    columns, order_max = coeff.shape
    rows = legendre.shape[0]
    n = m_list.shape[0]
    pieces = 6
    operands = (m_list, coeff, block, legendre)
    return pl.pallas_call(
        functools.partial(prepare_kernel, at),
        out_shape=[
            jax.ShapeDtypeStruct((columns, order_max), BF16),
            jax.ShapeDtypeStruct((rows // 2, order_max), BF16),
            jax.ShapeDtypeStruct((rows // 2, order_max), BF16),
        ],
        in_specs=[HBM] * 4,
        out_specs=[VMEM] * 3,
        scratch_shapes=[
            pltpu.SMEM((n,), jnp.int32),
            pltpu.VMEM((columns, order_max), BF16),
            pltpu.VMEM((pieces, order_max // pieces, order_max), BF16),
            pltpu.VMEM((rows, order_max), BF16),
            pltpu.SemaphoreType.DMA((3 + pieces,)),
        ],
        compiler_params=pltpu.CompilerParams(vmem_limit_bytes=32 << 20),
        cost_estimate=pl.CostEstimate(
            flops=2 * (columns * order_max * order_max + rows * rows * order_max),
            bytes_accessed=2 * (block.size + legendre.size),
            transcendentals=0,
        ),
        name="prepare",
    )(*[pltpu.with_memory_space_constraint(x, pltpu.HBM) for x in operands])


def table_kernel(at, line, m_ref, own_ref, table_ref, rows_ref):
    write_table(table_ref, m_ref, lax.axis_index("mset"), at, line)
    rows_ref[...] = map_rows(own_ref, 0, m_ref.shape[0]).astype(BF16)


def table_and_own(m_list, own, at, line):
    n = m_list.shape[0]
    out_rows = own.shape[0] * REAL
    return pl.pallas_call(
        functools.partial(table_kernel, at, line),
        out_shape=[
            jax.ShapeDtypeStruct((2 * n, NPHI), BF16),
            jax.ShapeDtypeStruct((out_rows, 2 * n), BF16),
        ],
        in_specs=[pl.BlockSpec(memory_space=pltpu.SMEM), VMEM],
        out_specs=[VMEM] * 2,
        compiler_params=pltpu.CompilerParams(vmem_limit_bytes=16 << 20),
        cost_estimate=pl.CostEstimate(
            flops=16 * n * NPHI, bytes_accessed=4 * n * NPHI, transcendentals=0
        ),
        name="table_and_own",
    )(m_list, own)


def cross_kernel(at, line, order, chunk, *refs):
    shards = len(order)
    shard_refs = dict(zip(order, refs[:shards]))
    keep_ref, got_ref, own_ref, back_ref = refs[shards:]
    half = keep_ref.shape[0]
    columns = shard_refs[0].shape[0]
    cycles = own_ref.shape[0]
    wide = chunk * columns
    legendre = jnp.concatenate([keep_ref[...], got_ref[...]], axis=0)
    slot = lax.rem(iota((2 * half, wide), 0), shards)
    local = iota((2 * half, wide), 1) // columns
    fold = iota((2 * cycles, 2 * half), 0) == iota((2 * cycles, 2 * half), 1) // shards
    fold = fold.astype(BF16)
    me = lax.axis_index("mset")
    for q in range(shards // chunk):
        piece = jnp.concatenate(
            [shard_refs[q * chunk + k][...] for k in range(chunk)], axis=0
        )
        product = lax.dot_general(
            legendre, piece, (((1,), (1,)), ((), ())), preferred_element_type=F32
        )
        own = slot == shard_source(local + q * chunk, me, at, line)
        chosen = jnp.where(own, product, 0.0).astype(BF16)
        folded = jnp.dot(fold, chosen, preferred_element_type=F32).astype(BF16)
        own_ref[:, q * wide : (q + 1) * wide] = folded[:cycles]
        back_ref[:, q * wide : (q + 1) * wide] = folded[cycles:]


def cross(keep, got, shards, at, line):
    half, order_max = keep.shape
    columns = shards[0].shape[0]
    count = len(shards)
    order = sorted(shards, key=lambda k: -(k >> at) % line)
    shape = jax.ShapeDtypeStruct((half // count, count * columns), BF16)
    return pl.pallas_call(
        functools.partial(cross_kernel, at, line, order, min(8, count)),
        out_shape=[shape, shape],
        in_specs=[VMEM] * (2 + count),
        out_specs=[VMEM] * 2,
        compiler_params=pltpu.CompilerParams(vmem_limit_bytes=32 << 20),
        cost_estimate=pl.CostEstimate(
            flops=4 * half * order_max * count * columns,
            bytes_accessed=2 * (2 * keep.size + count * shards[0].size),
            transcendentals=0,
        ),
        name="cross",
    )(*[shards[k] for k in order], keep, got)


def synthesis_kernel(tiles, own_ref, got_ref, table_ref, out_ref, held, sems):
    n = table_ref.shape[0] // 2
    flat = (map_rows(got_ref, n // 2, n) + own_ref[...].astype(F32)).astype(BF16)
    width = NPHI // tiles
    copies = []
    for t in range(tiles):
        span = pl.ds(t * width, width)
        summed = jnp.dot(flat, table_ref[:, span], preferred_element_type=F32)
        held[:, span] = summed.astype(BF16)
        copy = pltpu.make_async_copy(held.at[:, span], out_ref.at[:, span], sems.at[t])
        copy.start()
        copies.append(copy)
    for copy in copies:
        copy.wait()


def synthesize(own, got, table):
    tiles = 16
    out_rows = own.shape[0]
    return pl.pallas_call(
        functools.partial(synthesis_kernel, tiles),
        out_shape=jax.ShapeDtypeStruct((out_rows, NPHI), BF16),
        in_specs=[VMEM] * 3,
        out_specs=HBM,
        scratch_shapes=[pltpu.VMEM((out_rows, NPHI), BF16), pltpu.SemaphoreType.DMA((tiles,))],
        compiler_params=pltpu.CompilerParams(vmem_limit_bytes=32 << 20),
        cost_estimate=pl.CostEstimate(
            flops=2 * out_rows * table.size,
            bytes_accessed=2 * (out_rows * NPHI + table.size),
            transcendentals=0,
        ),
        name="synthesis",
    )(own, got, table)


def exchange(value, size, mask):
    return lax.ppermute(value, "mset", [(d, d ^ mask) for d in range(size)])


def gather_shards(value, size, at, line):
    step = size // line
    shards = {0: value}
    for turn in range(1, line):
        pairs = [(d, (d + turn * step) % size) for d in range(size)]
        shards[turn << at] = lax.ppermute(value, "mset", pairs)
    for b in range(at):
        shards.update({k | 1 << b: exchange(v, size, 1 << b) for k, v in shards.items()})
    return shards


def body(m_list, coeff, blocks, legendre):
    size = lax.axis_size("mset")
    per_device, columns, order_max = coeff.shape
    if per_device != 1 or size & (size - 1):
        raise ValueError("unsupported mesh")
    cycles, n, _ = legendre.shape
    at = min(1, size.bit_length() - 2)
    line = size >> (at + 1)
    filtered, keep, send = prepare(
        m_list, coeff[0], blocks[0], legendre.reshape(cycles * n, order_max), at
    )
    shards = gather_shards(filtered, size, at, line)
    got = exchange(send, size, 1 << at)
    own, back = cross(keep, got, shards, at, line)
    other = exchange(back, size, 1 << at)
    table, own_rows = table_and_own(m_list, own, at, line)
    sky_map = synthesize(own_rows, other, table)
    return sky_map.reshape(cycles, REAL, NPHI)


def solution(mesh):
    in_specs = (
        P(),
        P(("groups", "mset"), None, None),
        P(("groups", "mset"), None, None),
        P(("groups", "mset"), None, None),
    )
    out_specs = P(("groups", "mset"), None, None)
    return jax.shard_map(body, mesh=mesh, in_specs=in_specs, out_specs=out_specs, check_vma=False)
```

```python
import functools
import math

import jax
import jax.numpy as jnp
from jax import lax
from jax.experimental import pallas as pl
from jax.experimental.pallas import tpu as pltpu
from jax.sharding import PartitionSpec as P

LL = 3072
REAL = 16
NPHI = 8192
LANES = 128
BF16 = jnp.bfloat16
F32 = jnp.float32
VMEM = pl.BlockSpec(memory_space=pltpu.VMEM)
HBM = pl.BlockSpec(memory_space=pltpu.HBM)


def iota(shape, dim):
    return lax.broadcasted_iota(jnp.int32, shape, dim)


def insert_bit(value, bit, at):
    low = (1 << at) - 1
    return (value & low) | (bit << at) | ((value >> at) << (at + 1))


def sends(line):
    if line == 4:
        return [[3, 0, 1, 2], [2, 1, 3, 0], [1, 3, 0, 2], [0, 2, 3, 1]]
    return [[(z - turn) % line for z in range(line)] for turn in range(1, line)]


def slots(line):
    found = []
    for z in range(line):
        seen, own = {z}, []
        for number, sources in enumerate(sends(line)):
            if sources[z] not in seen:
                seen.add(sources[z])
                own.append((number, sources[z]))
        found.append(own)
    return list(zip(*found))


def by_place(values, z):
    result = values[0]
    for place, value in enumerate(values):
        if value != values[0]:
            result = jnp.where(z == place, value, result)
    return result


def shard_ranks(me, at, line):
    z, other = me >> (at + 1), me & ((1 << at) - 1)
    places = [z] + [by_place([source for _, source in slot], z) for slot in slots(line)]
    return [(place << at) | (other ^ flip) for place in places for flip in range(1 << at)]


def angle(phase):
    phase = phase & (NPHI - 1)
    phase = jnp.where(phase >= NPHI // 2, phase - NPHI, phase)
    return phase.astype(F32) * (2.0 * math.pi / NPHI)


def write_table(table_ref, m_ref, me, at, line):
    n = table_ref.shape[0] // 2
    half = n // 2
    index = iota((n, LANES), 0)
    lane = iota((n, LANES), 1)
    own_bit = (me >> at) & 1
    values = jnp.zeros((n, LANES), jnp.int32)
    ranks = shard_ranks(me, at, line)
    for j in range(n):
        source = insert_bit(ranks[j % half], own_bit ^ (j // half), at)
        values = jnp.where(index == j, m_ref[source], values)
    scale = 1.0 / math.sqrt(n)
    fine = angle(values * lane)
    coarse = angle(values * lane * LANES)
    cos_f, sin_f = jnp.cos(fine), jnp.sin(fine)
    cos_c, sin_c = jnp.cos(coarse), jnp.sin(coarse)
    for a in range(NPHI // LANES):
        ca, sa = cos_c[:, a : a + 1], sin_c[:, a : a + 1]
        span = slice(a * LANES, (a + 1) * LANES)
        table_ref[:n, span] = ((ca * cos_f - sa * sin_f).astype(BF16) * scale).astype(BF16)
        table_ref[n:, span] = ((-(sa * cos_f + ca * sin_f)).astype(BF16) * scale).astype(BF16)


def map_rows(half_ref, first, total):
    cycles, wide = half_ref.shape
    rows = cycles * REAL
    repeat = (iota((rows, cycles), 0) // REAL == iota((rows, cycles), 1)).astype(BF16)
    spread = jnp.dot(repeat, half_ref[...], preferred_element_type=F32)
    same_real = lax.rem(iota((rows, wide), 0), REAL) == lax.rem(iota((rows, wide), 1), REAL)
    chosen = jnp.where(same_real, spread, 0.0).astype(BF16)
    row, col = iota((wide, 2 * total), 0), iota((wide, 2 * total), 1)
    pick = lax.rem(row, 2 * REAL) // REAL * total + first + row // (2 * REAL) == col
    return jnp.dot(chosen, pick.astype(BF16), preferred_element_type=F32)


def prepare_kernel(
    at, m_ref, coeff_ref, block_ref, leg_ref, filtered_ref, keep_ref, send_ref,
    m_smem, coeff_vmem, block_vmem, leg_vmem, sems,
):
    me = lax.axis_index("mset")
    columns, order_max = coeff_ref.shape
    pieces = block_vmem.shape[0]
    depth = order_max // pieces
    copy_m = pltpu.make_async_copy(m_ref, m_smem, sems.at[0])
    copy_leg = pltpu.make_async_copy(leg_ref, leg_vmem, sems.at[1])
    copy_coeff = pltpu.make_async_copy(coeff_ref, coeff_vmem, sems.at[2])
    copy_blocks = [
        pltpu.make_async_copy(
            block_ref.at[pl.ds(p * depth, depth), :], block_vmem.at[p], sems.at[3 + p]
        )
        for p in range(pieces)
    ]
    for copy in [copy_m, copy_leg, copy_coeff] + copy_blocks:
        copy.start()

    rows = leg_ref.shape[0]
    n = m_ref.shape[0]
    half = rows // 2
    own_bit = (me >> at) & 1
    row, col = iota((rows, rows), 0), iota((rows, rows), 1)
    bit = own_bit ^ (row // half)
    slot = lax.rem(row, n // 2)
    pick = (lax.rem(row, half) // (n // 2) == col // n) & (
        insert_bit(slot, bit, at) == lax.rem(col, n)
    )
    pick = pick.astype(BF16)
    copy_leg.wait()
    ordered = jnp.dot(pick, leg_vmem[...], preferred_element_type=F32).astype(BF16)
    keep_ref[...] = ordered[:half]
    send_ref[...] = ordered[half:]

    copy_m.wait()
    order = LL - m_smem[me]
    copy_coeff.wait()
    coeff = coeff_vmem[...]
    coeff = jnp.where(iota(coeff.shape, 1) < order, coeff, jnp.zeros_like(coeff))
    total = jnp.zeros((columns, order_max), F32)
    for p in range(pieces):
        copy_blocks[p].wait()
        total += jnp.dot(
            coeff[:, p * depth : (p + 1) * depth], block_vmem[p], preferred_element_type=F32
        )
    filtered_ref[...] = jnp.where(iota(total.shape, 1) < order, total, 0.0).astype(BF16)


def prepare(m_list, coeff, block, legendre, at):
    columns, order_max = coeff.shape
    rows = legendre.shape[0]
    n = m_list.shape[0]
    pieces = 6
    operands = (m_list, coeff, block, legendre)
    return pl.pallas_call(
        functools.partial(prepare_kernel, at),
        out_shape=[
            jax.ShapeDtypeStruct((columns, order_max), BF16),
            jax.ShapeDtypeStruct((rows // 2, order_max), BF16),
            jax.ShapeDtypeStruct((rows // 2, order_max), BF16),
        ],
        in_specs=[HBM] * 4,
        out_specs=[VMEM] * 3,
        scratch_shapes=[
            pltpu.SMEM((n,), jnp.int32),
            pltpu.VMEM((columns, order_max), BF16),
            pltpu.VMEM((pieces, order_max // pieces, order_max), BF16),
            pltpu.VMEM((rows, order_max), BF16),
            pltpu.SemaphoreType.DMA((3 + pieces,)),
        ],
        compiler_params=pltpu.CompilerParams(vmem_limit_bytes=32 << 20),
        cost_estimate=pl.CostEstimate(
            flops=2 * (columns * order_max * order_max + rows * rows * order_max),
            bytes_accessed=2 * (block.size + legendre.size),
            transcendentals=0,
        ),
        name="prepare",
    )(*[pltpu.with_memory_space_constraint(x, pltpu.HBM) for x in operands])


def table_kernel(at, line, m_ref, own_ref, table_ref, rows_ref):
    write_table(table_ref, m_ref, lax.axis_index("mset"), at, line)
    rows_ref[...] = map_rows(own_ref, 0, m_ref.shape[0]).astype(BF16)


def table_and_own(m_list, own, at, line):
    n = m_list.shape[0]
    out_rows = own.shape[0] * REAL
    return pl.pallas_call(
        functools.partial(table_kernel, at, line),
        out_shape=[
            jax.ShapeDtypeStruct((2 * n, NPHI), BF16),
            jax.ShapeDtypeStruct((out_rows, 2 * n), BF16),
        ],
        in_specs=[pl.BlockSpec(memory_space=pltpu.SMEM), VMEM],
        out_specs=[VMEM] * 2,
        compiler_params=pltpu.CompilerParams(vmem_limit_bytes=16 << 20),
        cost_estimate=pl.CostEstimate(
            flops=16 * n * NPHI, bytes_accessed=4 * n * NPHI, transcendentals=0
        ),
        name="table_and_own",
    )(m_list, own)


def cross_kernel(at, line, order, chunk, *refs):
    shard_refs = dict(zip(order, refs[: len(order)]))
    keep_ref, got_ref, own_ref, back_ref = refs[len(order) :]
    shards = line << at
    half = keep_ref.shape[0]
    columns = shard_refs[0].shape[0]
    cycles = own_ref.shape[0]
    wide = chunk * columns
    legendre = jnp.concatenate([keep_ref[...], got_ref[...]], axis=0)
    slot = lax.rem(iota((2 * half, wide), 0), shards)
    local = iota((2 * half, wide), 1) // columns
    fold = iota((2 * cycles, 2 * half), 0) == iota((2 * cycles, 2 * half), 1) // shards
    fold = fold.astype(BF16)
    me = lax.axis_index("mset")
    z = me >> (at + 1)
    ranks = shard_ranks(me, at, line)

    def shard(position):
        turn, flip = position >> at, position & ((1 << at) - 1)
        if turn == 0:
            return shard_refs[flip][...]
        numbers = [number for number, _ in slots(line)[turn - 1]]
        value = shard_refs[(numbers[0] + 1) << at | flip][...]
        for number in sorted(set(numbers) - {numbers[0]}):
            here = by_place([int(k == number) for k in numbers], z)
            value = jnp.where(here == 1, shard_refs[(number + 1) << at | flip][...], value)
        return value

    for q in range(shards // chunk):
        piece = jnp.concatenate([shard(q * chunk + k) for k in range(chunk)], axis=0)
        rank = jnp.zeros_like(local)
        for k in range(chunk):
            rank = jnp.where(local == k, ranks[q * chunk + k], rank)
        product = lax.dot_general(
            legendre, piece, (((1,), (1,)), ((), ())), preferred_element_type=F32
        )
        chosen = jnp.where(slot == rank, product, 0.0).astype(BF16)
        folded = jnp.dot(fold, chosen, preferred_element_type=F32).astype(BF16)
        own_ref[:, q * wide : (q + 1) * wide] = folded[:cycles]
        back_ref[:, q * wide : (q + 1) * wide] = folded[cycles:]


def cross(keep, got, shards, at, line):
    half, order_max = keep.shape
    columns = shards[0].shape[0]
    count = line << at
    order = sorted(shards, key=lambda k: (k >> at != 0, -k))
    shape = jax.ShapeDtypeStruct((half // count, count * columns), BF16)
    return pl.pallas_call(
        functools.partial(cross_kernel, at, line, order, min(8, count)),
        out_shape=[shape, shape],
        in_specs=[VMEM] * (2 + len(order)),
        out_specs=[VMEM] * 2,
        compiler_params=pltpu.CompilerParams(vmem_limit_bytes=32 << 20),
        cost_estimate=pl.CostEstimate(
            flops=4 * half * order_max * count * columns,
            bytes_accessed=2 * (2 * keep.size + count * shards[0].size),
            transcendentals=0,
        ),
        name="cross",
    )(*[shards[k] for k in order], keep, got)


def synthesis_kernel(tiles, own_ref, got_ref, table_ref, out_ref, held, sems):
    n = table_ref.shape[0] // 2
    flat = (map_rows(got_ref, n // 2, n) + own_ref[...].astype(F32)).astype(BF16)
    width = NPHI // tiles
    copies = []
    for t in range(tiles):
        span = pl.ds(t * width, width)
        summed = jnp.dot(flat, table_ref[:, span], preferred_element_type=F32)
        held[:, span] = summed.astype(BF16)
        copy = pltpu.make_async_copy(held.at[:, span], out_ref.at[:, span], sems.at[t])
        copy.start()
        copies.append(copy)
    for copy in copies:
        copy.wait()


def synthesize(own, got, table):
    tiles = 16
    out_rows = own.shape[0]
    return pl.pallas_call(
        functools.partial(synthesis_kernel, tiles),
        out_shape=jax.ShapeDtypeStruct((out_rows, NPHI), BF16),
        in_specs=[VMEM] * 3,
        out_specs=HBM,
        scratch_shapes=[pltpu.VMEM((out_rows, NPHI), BF16), pltpu.SemaphoreType.DMA((tiles,))],
        compiler_params=pltpu.CompilerParams(vmem_limit_bytes=32 << 20),
        cost_estimate=pl.CostEstimate(
            flops=2 * out_rows * table.size,
            bytes_accessed=2 * (out_rows * NPHI + table.size),
            transcendentals=0,
        ),
        name="synthesis",
    )(own, got, table)


def exchange(value, size, mask):
    return lax.ppermute(value, "mset", [(d, d ^ mask) for d in range(size)])


def gather_shards(value, size, at, line):
    step = size // line
    shards = {0: value}
    for number, sources in enumerate(sends(line)):
        pairs = [(s * step + k, z * step + k) for z, s in enumerate(sources) for k in range(step)]
        shards[(number + 1) << at] = lax.ppermute(value, "mset", pairs)
    for b in range(at):
        shards.update({k | 1 << b: exchange(v, size, 1 << b) for k, v in shards.items()})
    return shards


def body(m_list, coeff, blocks, legendre):
    size = lax.axis_size("mset")
    per_device, columns, order_max = coeff.shape
    if per_device != 1 or size & (size - 1):
        raise ValueError("unsupported mesh")
    cycles, n, _ = legendre.shape
    at = min(1, size.bit_length() - 2)
    line = size >> (at + 1)
    filtered, keep, send = prepare(
        m_list, coeff[0], blocks[0], legendre.reshape(cycles * n, order_max), at
    )
    shards = gather_shards(filtered, size, at, line)
    got = exchange(send, size, 1 << at)
    own, back = cross(keep, got, shards, at, line)
    other = exchange(back, size, 1 << at)
    table, own_rows = table_and_own(m_list, own, at, line)
    sky_map = synthesize(own_rows, other, table)
    return sky_map.reshape(cycles, REAL, NPHI)


def solution(mesh):
    in_specs = (
        P(),
        P(("groups", "mset"), None, None),
        P(("groups", "mset"), None, None),
        P(("groups", "mset"), None, None),
    )
    out_specs = P(("groups", "mset"), None, None)
    return jax.shard_map(body, mesh=mesh, in_specs=in_specs, out_specs=out_specs, check_vma=False)
```

```python
import functools
import math

import jax
import jax.numpy as jnp
from jax import lax
from jax.experimental import pallas as pl
from jax.experimental.pallas import tpu as pltpu
from jax.sharding import PartitionSpec as P

LL = 3072
REAL = 16
NPHI = 8192
RELAY_FLOPS = 2_750_000_000
LANES = 128
BF16 = jnp.bfloat16
F32 = jnp.float32
VMEM = pl.BlockSpec(memory_space=pltpu.VMEM)
HBM = pl.BlockSpec(memory_space=pltpu.HBM)


def iota(shape, dim):
    return lax.broadcasted_iota(jnp.int32, shape, dim)


def insert_bit(value, bit, at):
    low = (1 << at) - 1
    return (value & low) | (bit << at) | ((value >> at) << (at + 1))


def shard_source(position, me, at, line):
    z, other = me >> (at + 1), me & ((1 << at) - 1)
    turn, flip = position >> at, position & ((1 << at) - 1)
    return (((z - turn) & (line - 1)) << at) | (other ^ flip)


def angle(phase):
    phase = phase & (NPHI - 1)
    phase = jnp.where(phase >= NPHI // 2, phase - NPHI, phase)
    return phase.astype(F32) * (2.0 * math.pi / NPHI)


def write_table(table_ref, m_ref, me, at, line):
    n = table_ref.shape[0] // 2
    half = n // 2
    index = iota((n, LANES), 0)
    lane = iota((n, LANES), 1)
    own_bit = (me >> at) & 1
    values = jnp.zeros((n, LANES), jnp.int32)
    for j in range(n):
        source = insert_bit(shard_source(j % half, me, at, line), own_bit ^ (j // half), at)
        values = jnp.where(index == j, m_ref[source], values)
    scale = 1.0 / math.sqrt(n)
    fine = angle(values * lane)
    coarse = angle(values * lane * LANES)
    cos_f, sin_f = jnp.cos(fine), jnp.sin(fine)
    cos_c, sin_c = jnp.cos(coarse), jnp.sin(coarse)
    for a in range(NPHI // LANES):
        ca, sa = cos_c[:, a : a + 1], sin_c[:, a : a + 1]
        span = slice(a * LANES, (a + 1) * LANES)
        table_ref[:n, span] = ((ca * cos_f - sa * sin_f).astype(BF16) * scale).astype(BF16)
        table_ref[n:, span] = ((-(sa * cos_f + ca * sin_f)).astype(BF16) * scale).astype(BF16)


def map_rows(half_ref, first, total):
    cycles, wide = half_ref.shape
    rows = cycles * REAL
    repeat = (iota((rows, cycles), 0) // REAL == iota((rows, cycles), 1)).astype(BF16)
    spread = jnp.dot(repeat, half_ref[...], preferred_element_type=F32)
    same_real = lax.rem(iota((rows, wide), 0), REAL) == lax.rem(iota((rows, wide), 1), REAL)
    chosen = jnp.where(same_real, spread, 0.0).astype(BF16)
    row, col = iota((wide, 2 * total), 0), iota((wide, 2 * total), 1)
    pick = lax.rem(row, 2 * REAL) // REAL * total + first + row // (2 * REAL) == col
    return jnp.dot(chosen, pick.astype(BF16), preferred_element_type=F32)


def prepare_kernel(
    at, m_ref, coeff_ref, block_ref, leg_ref, filtered_ref, keep_ref, send_ref,
    m_smem, coeff_vmem, block_vmem, leg_vmem, sems,
):
    me = lax.axis_index("mset")
    columns, order_max = coeff_ref.shape
    pieces = block_vmem.shape[0]
    depth = order_max // pieces
    copy_m = pltpu.make_async_copy(m_ref, m_smem, sems.at[0])
    copy_leg = pltpu.make_async_copy(leg_ref, leg_vmem, sems.at[1])
    copy_coeff = pltpu.make_async_copy(coeff_ref, coeff_vmem, sems.at[2])
    copy_blocks = [
        pltpu.make_async_copy(
            block_ref.at[pl.ds(p * depth, depth), :], block_vmem.at[p], sems.at[3 + p]
        )
        for p in range(pieces)
    ]
    for copy in [copy_m, copy_leg, copy_coeff] + copy_blocks:
        copy.start()

    rows = leg_ref.shape[0]
    n = m_ref.shape[0]
    half = rows // 2
    own_bit = (me >> at) & 1
    row, col = iota((rows, rows), 0), iota((rows, rows), 1)
    bit = own_bit ^ (row // half)
    slot = lax.rem(row, n // 2)
    pick = (lax.rem(row, half) // (n // 2) == col // n) & (
        insert_bit(slot, bit, at) == lax.rem(col, n)
    )
    pick = pick.astype(BF16)
    copy_leg.wait()
    ordered = jnp.dot(pick, leg_vmem[...], preferred_element_type=F32).astype(BF16)
    keep_ref[...] = ordered[:half]
    send_ref[...] = ordered[half:]

    copy_m.wait()
    order = LL - m_smem[me]
    copy_coeff.wait()
    coeff = coeff_vmem[...]
    coeff = jnp.where(iota(coeff.shape, 1) < order, coeff, jnp.zeros_like(coeff))
    total = jnp.zeros((columns, order_max), F32)
    for p in range(pieces):
        copy_blocks[p].wait()
        total += jnp.dot(
            coeff[:, p * depth : (p + 1) * depth], block_vmem[p], preferred_element_type=F32
        )
    filtered_ref[...] = jnp.where(iota(total.shape, 1) < order, total, 0.0).astype(BF16)


def prepare(m_list, coeff, block, legendre, at):
    columns, order_max = coeff.shape
    rows = legendre.shape[0]
    n = m_list.shape[0]
    pieces = 6
    operands = (m_list, coeff, block, legendre)
    return pl.pallas_call(
        functools.partial(prepare_kernel, at),
        out_shape=[
            jax.ShapeDtypeStruct((columns, order_max), BF16),
            jax.ShapeDtypeStruct((rows // 2, order_max), BF16),
            jax.ShapeDtypeStruct((rows // 2, order_max), BF16),
        ],
        in_specs=[HBM] * 4,
        out_specs=[VMEM] * 3,
        scratch_shapes=[
            pltpu.SMEM((n,), jnp.int32),
            pltpu.VMEM((columns, order_max), BF16),
            pltpu.VMEM((pieces, order_max // pieces, order_max), BF16),
            pltpu.VMEM((rows, order_max), BF16),
            pltpu.SemaphoreType.DMA((3 + pieces,)),
        ],
        compiler_params=pltpu.CompilerParams(vmem_limit_bytes=32 << 20),
        cost_estimate=pl.CostEstimate(
            flops=2 * (columns * order_max * order_max + rows * rows * order_max),
            bytes_accessed=2 * (block.size + legendre.size),
            transcendentals=0,
        ),
        name="prepare",
    )(*[pltpu.with_memory_space_constraint(x, pltpu.HBM) for x in operands])


def table_kernel(at, line, m_ref, own_ref, table_ref, rows_ref):
    write_table(table_ref, m_ref, lax.axis_index("mset"), at, line)
    rows_ref[...] = map_rows(own_ref, 0, m_ref.shape[0]).astype(BF16)


def table_and_own(m_list, own, at, line):
    n = m_list.shape[0]
    out_rows = own.shape[0] * REAL
    return pl.pallas_call(
        functools.partial(table_kernel, at, line),
        out_shape=[
            jax.ShapeDtypeStruct((2 * n, NPHI), BF16),
            jax.ShapeDtypeStruct((out_rows, 2 * n), BF16),
        ],
        in_specs=[pl.BlockSpec(memory_space=pltpu.SMEM), VMEM],
        out_specs=[VMEM] * 2,
        compiler_params=pltpu.CompilerParams(vmem_limit_bytes=16 << 20),
        cost_estimate=pl.CostEstimate(
            flops=16 * n * NPHI, bytes_accessed=4 * n * NPHI, transcendentals=0
        ),
        name="table_and_own",
    )(m_list, own)


def relay_kernel(shard_ref, out_ref):
    out_ref[...] = shard_ref[...]


def relay(shard):
    return pl.pallas_call(
        relay_kernel,
        out_shape=jax.ShapeDtypeStruct(shard.shape, BF16),
        in_specs=[VMEM],
        out_specs=VMEM,
        cost_estimate=pl.CostEstimate(
            flops=RELAY_FLOPS, bytes_accessed=4 * shard.size, transcendentals=0
        ),
        name="relay",
    )(shard)


def cross_kernel(at, line, order, chunk, *refs):
    shards = len(order)
    shard_refs = dict(zip(order, refs[:shards]))
    keep_ref, got_ref, own_ref, back_ref = refs[shards:]
    half = keep_ref.shape[0]
    columns = shard_refs[0].shape[0]
    cycles = own_ref.shape[0]
    wide = chunk * columns
    legendre = jnp.concatenate([keep_ref[...], got_ref[...]], axis=0)
    slot = lax.rem(iota((2 * half, wide), 0), shards)
    local = iota((2 * half, wide), 1) // columns
    fold = iota((2 * cycles, 2 * half), 0) == iota((2 * cycles, 2 * half), 1) // shards
    fold = fold.astype(BF16)
    me = lax.axis_index("mset")
    for q in range(shards // chunk):
        piece = jnp.concatenate(
            [shard_refs[q * chunk + k][...] for k in range(chunk)], axis=0
        )
        product = lax.dot_general(
            legendre, piece, (((1,), (1,)), ((), ())), preferred_element_type=F32
        )
        own = slot == shard_source(local + q * chunk, me, at, line)
        chosen = jnp.where(own, product, 0.0).astype(BF16)
        folded = jnp.dot(fold, chosen, preferred_element_type=F32).astype(BF16)
        own_ref[:, q * wide : (q + 1) * wide] = folded[:cycles]
        back_ref[:, q * wide : (q + 1) * wide] = folded[cycles:]


def cross(keep, got, shards, at, line):
    half, order_max = keep.shape
    columns = shards[0].shape[0]
    count = len(shards)
    order = sorted(shards, key=lambda k: -(k >> at) % line)
    shape = jax.ShapeDtypeStruct((half // count, count * columns), BF16)
    return pl.pallas_call(
        functools.partial(cross_kernel, at, line, order, min(8, count)),
        out_shape=[shape, shape],
        in_specs=[VMEM] * (2 + count),
        out_specs=[VMEM] * 2,
        compiler_params=pltpu.CompilerParams(vmem_limit_bytes=32 << 20),
        cost_estimate=pl.CostEstimate(
            flops=4 * half * order_max * count * columns,
            bytes_accessed=2 * (2 * keep.size + count * shards[0].size),
            transcendentals=0,
        ),
        name="cross",
    )(*[shards[k] for k in order], keep, got)


def synthesis_kernel(tiles, own_ref, got_ref, table_ref, out_ref, held, sems):
    n = table_ref.shape[0] // 2
    flat = (map_rows(got_ref, n // 2, n) + own_ref[...].astype(F32)).astype(BF16)
    width = NPHI // tiles
    copies = []
    for t in range(tiles):
        span = pl.ds(t * width, width)
        summed = jnp.dot(flat, table_ref[:, span], preferred_element_type=F32)
        held[:, span] = summed.astype(BF16)
        copy = pltpu.make_async_copy(held.at[:, span], out_ref.at[:, span], sems.at[t])
        copy.start()
        copies.append(copy)
    for copy in copies:
        copy.wait()


def synthesize(own, got, table):
    tiles = 16
    out_rows = own.shape[0]
    return pl.pallas_call(
        functools.partial(synthesis_kernel, tiles),
        out_shape=jax.ShapeDtypeStruct((out_rows, NPHI), BF16),
        in_specs=[VMEM] * 3,
        out_specs=HBM,
        scratch_shapes=[pltpu.VMEM((out_rows, NPHI), BF16), pltpu.SemaphoreType.DMA((tiles,))],
        compiler_params=pltpu.CompilerParams(vmem_limit_bytes=32 << 20),
        cost_estimate=pl.CostEstimate(
            flops=2 * out_rows * table.size,
            bytes_accessed=2 * (out_rows * NPHI + table.size),
            transcendentals=0,
        ),
        name="synthesis",
    )(own, got, table)


def exchange(value, size, mask):
    return lax.ppermute(value, "mset", [(d, d ^ mask) for d in range(size)])


def gather_shards(value, size, at, line):
    step = size // line
    shards = {0: value}
    for turn in range(1, line):
        pairs = [(d, (d + turn * step) % size) for d in range(size)]
        shards[turn << at] = lax.ppermute(value, "mset", pairs)
    shards[1 << at] = relay(shards[1 << at])
    for b in range(at):
        shards.update({k | 1 << b: exchange(v, size, 1 << b) for k, v in shards.items()})
    return shards


def body(m_list, coeff, blocks, legendre):
    size = lax.axis_size("mset")
    per_device, columns, order_max = coeff.shape
    if per_device != 1 or size & (size - 1):
        raise ValueError("unsupported mesh")
    cycles, n, _ = legendre.shape
    at = min(1, size.bit_length() - 2)
    line = size >> (at + 1)
    filtered, keep, send = prepare(
        m_list, coeff[0], blocks[0], legendre.reshape(cycles * n, order_max), at
    )
    shards = gather_shards(filtered, size, at, line)
    got = exchange(send, size, 1 << at)
    own, back = cross(keep, got, shards, at, line)
    other = exchange(back, size, 1 << at)
    table, own_rows = table_and_own(m_list, own, at, line)
    sky_map = synthesize(own_rows, other, table)
    return sky_map.reshape(cycles, REAL, NPHI)


def solution(mesh):
    in_specs = (
        P(),
        P(("groups", "mset"), None, None),
        P(("groups", "mset"), None, None),
        P(("groups", "mset"), None, None),
    )
    out_specs = P(("groups", "mset"), None, None)
    return jax.shard_map(body, mesh=mesh, in_specs=in_specs, out_specs=out_specs, check_vma=False)
```

```python
import functools
import math

import jax
import jax.numpy as jnp
from jax import lax
from jax.experimental import pallas as pl
from jax.experimental.pallas import tpu as pltpu
from jax.sharding import PartitionSpec as P

LL = 3072
REAL = 16
NPHI = 8192
RELAY_FLOPS = 2_750_000_000
LANES = 128
BF16 = jnp.bfloat16
F32 = jnp.float32
VMEM = pl.BlockSpec(memory_space=pltpu.VMEM)
HBM = pl.BlockSpec(memory_space=pltpu.HBM)


def iota(shape, dim):
    return lax.broadcasted_iota(jnp.int32, shape, dim)


def insert_bit(value, bit, at):
    low = (1 << at) - 1
    return (value & low) | (bit << at) | ((value >> at) << (at + 1))


def shard_source(position, me, at, line):
    z, other = me >> (at + 1), me & ((1 << at) - 1)
    turn, flip = position >> at, position & ((1 << at) - 1)
    return (((z - turn) & (line - 1)) << at) | (other ^ flip)


def angle(phase):
    phase = phase & (NPHI - 1)
    phase = jnp.where(phase >= NPHI // 2, phase - NPHI, phase)
    return phase.astype(F32) * (2.0 * math.pi / NPHI)


def write_table(table_ref, m_ref, me, at, line):
    n = table_ref.shape[0] // 2
    half = n // 2
    index = iota((n, LANES), 0)
    lane = iota((n, LANES), 1)
    own_bit = (me >> at) & 1
    values = jnp.zeros((n, LANES), jnp.int32)
    for j in range(n):
        source = insert_bit(shard_source(j % half, me, at, line), own_bit ^ (j // half), at)
        values = jnp.where(index == j, m_ref[source], values)
    scale = 1.0 / math.sqrt(n)
    fine = angle(values * lane)
    coarse = angle(values * lane * LANES)
    cos_f, sin_f = jnp.cos(fine), jnp.sin(fine)
    cos_c, sin_c = jnp.cos(coarse), jnp.sin(coarse)
    for a in range(NPHI // LANES):
        ca, sa = cos_c[:, a : a + 1], sin_c[:, a : a + 1]
        span = slice(a * LANES, (a + 1) * LANES)
        table_ref[:n, span] = ((ca * cos_f - sa * sin_f).astype(BF16) * scale).astype(BF16)
        table_ref[n:, span] = ((-(sa * cos_f + ca * sin_f)).astype(BF16) * scale).astype(BF16)


def map_rows(half_ref, first, total):
    cycles, wide = half_ref.shape
    rows = cycles * REAL
    repeat = (iota((rows, cycles), 0) // REAL == iota((rows, cycles), 1)).astype(BF16)
    spread = jnp.dot(repeat, half_ref[...], preferred_element_type=F32)
    same_real = lax.rem(iota((rows, wide), 0), REAL) == lax.rem(iota((rows, wide), 1), REAL)
    chosen = jnp.where(same_real, spread, 0.0).astype(BF16)
    row, col = iota((wide, 2 * total), 0), iota((wide, 2 * total), 1)
    pick = lax.rem(row, 2 * REAL) // REAL * total + first + row // (2 * REAL) == col
    return jnp.dot(chosen, pick.astype(BF16), preferred_element_type=F32)


def prepare_kernel(
    at, m_ref, coeff_ref, block_ref, leg_ref, filtered_ref, keep_ref, send_ref,
    m_smem, coeff_vmem, block_vmem, leg_vmem, sems,
):
    me = lax.axis_index("mset")
    columns, order_max = coeff_ref.shape
    pieces = block_vmem.shape[0]
    depth = order_max // pieces
    copy_m = pltpu.make_async_copy(m_ref, m_smem, sems.at[0])
    copy_leg = pltpu.make_async_copy(leg_ref, leg_vmem, sems.at[1])
    copy_coeff = pltpu.make_async_copy(coeff_ref, coeff_vmem, sems.at[2])
    copy_blocks = [
        pltpu.make_async_copy(
            block_ref.at[pl.ds(p * depth, depth), :], block_vmem.at[p], sems.at[3 + p]
        )
        for p in range(pieces)
    ]
    for copy in [copy_m, copy_leg, copy_coeff] + copy_blocks:
        copy.start()

    rows = leg_ref.shape[0]
    n = m_ref.shape[0]
    half = rows // 2
    own_bit = (me >> at) & 1
    row, col = iota((rows, rows), 0), iota((rows, rows), 1)
    bit = own_bit ^ (row // half)
    slot = lax.rem(row, n // 2)
    pick = (lax.rem(row, half) // (n // 2) == col // n) & (
        insert_bit(slot, bit, at) == lax.rem(col, n)
    )
    pick = pick.astype(BF16)
    copy_leg.wait()
    ordered = jnp.dot(pick, leg_vmem[...], preferred_element_type=F32).astype(BF16)
    keep_ref[...] = ordered[:half]
    send_ref[...] = ordered[half:]

    copy_m.wait()
    order = LL - m_smem[me]
    copy_coeff.wait()
    coeff = coeff_vmem[...]
    coeff = jnp.where(iota(coeff.shape, 1) < order, coeff, jnp.zeros_like(coeff))
    total = jnp.zeros((columns, order_max), F32)
    for p in range(pieces):
        copy_blocks[p].wait()
        total += jnp.dot(
            coeff[:, p * depth : (p + 1) * depth], block_vmem[p], preferred_element_type=F32
        )
    filtered_ref[...] = jnp.where(iota(total.shape, 1) < order, total, 0.0).astype(BF16)


def prepare(m_list, coeff, block, legendre, at):
    columns, order_max = coeff.shape
    rows = legendre.shape[0]
    n = m_list.shape[0]
    pieces = 6
    operands = (m_list, coeff, block, legendre)
    return pl.pallas_call(
        functools.partial(prepare_kernel, at),
        out_shape=[
            jax.ShapeDtypeStruct((columns, order_max), BF16),
            jax.ShapeDtypeStruct((rows // 2, order_max), BF16),
            jax.ShapeDtypeStruct((rows // 2, order_max), BF16),
        ],
        in_specs=[HBM] * 4,
        out_specs=[VMEM] * 3,
        scratch_shapes=[
            pltpu.SMEM((n,), jnp.int32),
            pltpu.VMEM((columns, order_max), BF16),
            pltpu.VMEM((pieces, order_max // pieces, order_max), BF16),
            pltpu.VMEM((rows, order_max), BF16),
            pltpu.SemaphoreType.DMA((3 + pieces,)),
        ],
        compiler_params=pltpu.CompilerParams(vmem_limit_bytes=32 << 20),
        cost_estimate=pl.CostEstimate(
            flops=2 * (columns * order_max * order_max + rows * rows * order_max),
            bytes_accessed=2 * (block.size + legendre.size),
            transcendentals=0,
        ),
        name="prepare",
    )(*[pltpu.with_memory_space_constraint(x, pltpu.HBM) for x in operands])


def table_kernel(at, line, m_ref, own_ref, table_ref, rows_ref):
    write_table(table_ref, m_ref, lax.axis_index("mset"), at, line)
    rows_ref[...] = map_rows(own_ref, 0, m_ref.shape[0]).astype(BF16)


def table_and_own(m_list, own, at, line):
    n = m_list.shape[0]
    out_rows = own.shape[0] * REAL
    return pl.pallas_call(
        functools.partial(table_kernel, at, line),
        out_shape=[
            jax.ShapeDtypeStruct((2 * n, NPHI), BF16),
            jax.ShapeDtypeStruct((out_rows, 2 * n), BF16),
        ],
        in_specs=[pl.BlockSpec(memory_space=pltpu.SMEM), VMEM],
        out_specs=[VMEM] * 2,
        compiler_params=pltpu.CompilerParams(vmem_limit_bytes=16 << 20),
        cost_estimate=pl.CostEstimate(
            flops=16 * n * NPHI, bytes_accessed=4 * n * NPHI, transcendentals=0
        ),
        name="table_and_own",
    )(m_list, own)


def relay_kernel(shard_ref, out_ref):
    out_ref[...] = shard_ref[...]


def relay(shard):
    return pl.pallas_call(
        relay_kernel,
        out_shape=jax.ShapeDtypeStruct(shard.shape, BF16),
        in_specs=[VMEM],
        out_specs=VMEM,
        compiler_params=pltpu.CompilerParams(vmem_limit_bytes=8 << 20),
        cost_estimate=pl.CostEstimate(
            flops=RELAY_FLOPS, bytes_accessed=4 * shard.size, transcendentals=0
        ),
        name="relay",
    )(shard)


def cross_kernel(at, line, order, chunk, *refs):
    shards = len(order)
    shard_refs = dict(zip(order, refs[:shards]))
    keep_ref, got_ref, own_ref, back_ref = refs[shards:]
    half = keep_ref.shape[0]
    columns = shard_refs[0].shape[0]
    cycles = own_ref.shape[0]
    wide = chunk * columns
    legendre = jnp.concatenate([keep_ref[...], got_ref[...]], axis=0)
    slot = lax.rem(iota((2 * half, wide), 0), shards)
    local = iota((2 * half, wide), 1) // columns
    fold = iota((2 * cycles, 2 * half), 0) == iota((2 * cycles, 2 * half), 1) // shards
    fold = fold.astype(BF16)
    me = lax.axis_index("mset")
    for q in range(shards // chunk):
        piece = jnp.concatenate(
            [shard_refs[q * chunk + k][...] for k in range(chunk)], axis=0
        )
        product = lax.dot_general(
            legendre, piece, (((1,), (1,)), ((), ())), preferred_element_type=F32
        )
        own = slot == shard_source(local + q * chunk, me, at, line)
        chosen = jnp.where(own, product, 0.0).astype(BF16)
        folded = jnp.dot(fold, chosen, preferred_element_type=F32).astype(BF16)
        own_ref[:, q * wide : (q + 1) * wide] = folded[:cycles]
        back_ref[:, q * wide : (q + 1) * wide] = folded[cycles:]


def cross(keep, got, shards, at, line):
    half, order_max = keep.shape
    columns = shards[0].shape[0]
    count = len(shards)
    order = sorted(shards, key=lambda k: -(k >> at) % line)
    shape = jax.ShapeDtypeStruct((half // count, count * columns), BF16)
    return pl.pallas_call(
        functools.partial(cross_kernel, at, line, order, min(8, count)),
        out_shape=[shape, shape],
        in_specs=[VMEM] * (2 + count),
        out_specs=[VMEM] * 2,
        compiler_params=pltpu.CompilerParams(vmem_limit_bytes=32 << 20),
        cost_estimate=pl.CostEstimate(
            flops=4 * half * order_max * count * columns,
            bytes_accessed=2 * (2 * keep.size + count * shards[0].size),
            transcendentals=0,
        ),
        name="cross",
    )(*[shards[k] for k in order], keep, got)


def synthesis_kernel(tiles, own_ref, got_ref, table_ref, out_ref, held, sems):
    n = table_ref.shape[0] // 2
    flat = (map_rows(got_ref, n // 2, n) + own_ref[...].astype(F32)).astype(BF16)
    width = NPHI // tiles
    copies = []
    for t in range(tiles):
        span = pl.ds(t * width, width)
        summed = jnp.dot(flat, table_ref[:, span], preferred_element_type=F32)
        held[:, span] = summed.astype(BF16)
        copy = pltpu.make_async_copy(held.at[:, span], out_ref.at[:, span], sems.at[t])
        copy.start()
        copies.append(copy)
    for copy in copies:
        copy.wait()


def synthesize(own, got, table):
    tiles = 16
    out_rows = own.shape[0]
    return pl.pallas_call(
        functools.partial(synthesis_kernel, tiles),
        out_shape=jax.ShapeDtypeStruct((out_rows, NPHI), BF16),
        in_specs=[VMEM] * 3,
        out_specs=HBM,
        scratch_shapes=[pltpu.VMEM((out_rows, NPHI), BF16), pltpu.SemaphoreType.DMA((tiles,))],
        compiler_params=pltpu.CompilerParams(vmem_limit_bytes=32 << 20),
        cost_estimate=pl.CostEstimate(
            flops=2 * out_rows * table.size,
            bytes_accessed=2 * (out_rows * NPHI + table.size),
            transcendentals=0,
        ),
        name="synthesis",
    )(own, got, table)


def exchange(value, size, mask):
    return lax.ppermute(value, "mset", [(d, d ^ mask) for d in range(size)])


def gather_shards(value, size, at, line):
    step = size // line
    shards = {0: value}
    for turn in range(1, line):
        pairs = [(d, (d + turn * step) % size) for d in range(size)]
        shards[turn << at] = lax.ppermute(value, "mset", pairs)
    shards[1 << at] = relay(shards[1 << at])
    for b in range(at):
        shards.update({k | 1 << b: exchange(v, size, 1 << b) for k, v in shards.items()})
    return shards


def body(m_list, coeff, blocks, legendre):
    size = lax.axis_size("mset")
    per_device, columns, order_max = coeff.shape
    if per_device != 1 or size & (size - 1):
        raise ValueError("unsupported mesh")
    cycles, n, _ = legendre.shape
    at = min(1, size.bit_length() - 2)
    line = size >> (at + 1)
    filtered, keep, send = prepare(
        m_list, coeff[0], blocks[0], legendre.reshape(cycles * n, order_max), at
    )
    shards = gather_shards(filtered, size, at, line)
    got = exchange(send, size, 1 << at)
    own, back = cross(keep, got, shards, at, line)
    other = exchange(back, size, 1 << at)
    table, own_rows = table_and_own(m_list, own, at, line)
    sky_map = synthesize(own_rows, other, table)
    return sky_map.reshape(cycles, REAL, NPHI)


def solution(mesh):
    in_specs = (
        P(),
        P(("groups", "mset"), None, None),
        P(("groups", "mset"), None, None),
        P(("groups", "mset"), None, None),
    )
    out_specs = P(("groups", "mset"), None, None)
    return jax.shard_map(body, mesh=mesh, in_specs=in_specs, out_specs=out_specs, check_vma=False)
```

```python
import functools
import math

import jax
import jax.numpy as jnp
from jax import lax
from jax.experimental import pallas as pl
from jax.experimental.pallas import tpu as pltpu
from jax.sharding import PartitionSpec as P

LL = 3072
REAL = 16
NPHI = 8192
RELAY_FLOPS = 2_750_000_000
LANES = 128
BF16 = jnp.bfloat16
F32 = jnp.float32
VMEM = pl.BlockSpec(memory_space=pltpu.VMEM)
HBM = pl.BlockSpec(memory_space=pltpu.HBM)


def iota(shape, dim):
    return lax.broadcasted_iota(jnp.int32, shape, dim)


def insert_bit(value, bit, at):
    low = (1 << at) - 1
    return (value & low) | (bit << at) | ((value >> at) << (at + 1))


def shard_source(position, me, at, line):
    z, other = me >> (at + 1), me & ((1 << at) - 1)
    turn, flip = position >> at, position & ((1 << at) - 1)
    return (((z - turn) & (line - 1)) << at) | (other ^ flip)


def angle(phase):
    phase = phase & (NPHI - 1)
    phase = jnp.where(phase >= NPHI // 2, phase - NPHI, phase)
    return phase.astype(F32) * (2.0 * math.pi / NPHI)


def write_table(table_ref, m_ref, me, at, line):
    n = table_ref.shape[0] // 2
    half = n // 2
    index = iota((n, LANES), 0)
    lane = iota((n, LANES), 1)
    own_bit = (me >> at) & 1
    values = jnp.zeros((n, LANES), jnp.int32)
    for j in range(n):
        source = insert_bit(shard_source(j % half, me, at, line), own_bit ^ (j // half), at)
        values = jnp.where(index == j, m_ref[source], values)
    scale = 1.0 / math.sqrt(n)
    fine = angle(values * lane)
    coarse = angle(values * lane * LANES)
    cos_f, sin_f = jnp.cos(fine), jnp.sin(fine)
    cos_c, sin_c = jnp.cos(coarse), jnp.sin(coarse)
    for a in range(NPHI // LANES):
        ca, sa = cos_c[:, a : a + 1], sin_c[:, a : a + 1]
        span = slice(a * LANES, (a + 1) * LANES)
        table_ref[:n, span] = ((ca * cos_f - sa * sin_f).astype(BF16) * scale).astype(BF16)
        table_ref[n:, span] = ((-(sa * cos_f + ca * sin_f)).astype(BF16) * scale).astype(BF16)


def map_rows(half_ref, first, total):
    cycles, wide = half_ref.shape
    rows = cycles * REAL
    repeat = (iota((rows, cycles), 0) // REAL == iota((rows, cycles), 1)).astype(BF16)
    spread = jnp.dot(repeat, half_ref[...], preferred_element_type=F32)
    same_real = lax.rem(iota((rows, wide), 0), REAL) == lax.rem(iota((rows, wide), 1), REAL)
    chosen = jnp.where(same_real, spread, 0.0).astype(BF16)
    row, col = iota((wide, 2 * total), 0), iota((wide, 2 * total), 1)
    pick = lax.rem(row, 2 * REAL) // REAL * total + first + row // (2 * REAL) == col
    return jnp.dot(chosen, pick.astype(BF16), preferred_element_type=F32)


def prepare_kernel(
    at, m_ref, coeff_ref, block_ref, leg_ref, filtered_ref, keep_ref, send_ref,
    m_smem, coeff_vmem, block_vmem, leg_vmem, sems,
):
    me = lax.axis_index("mset")
    columns, order_max = coeff_ref.shape
    pieces = block_vmem.shape[0]
    depth = order_max // pieces
    copy_m = pltpu.make_async_copy(m_ref, m_smem, sems.at[0])
    copy_leg = pltpu.make_async_copy(leg_ref, leg_vmem, sems.at[1])
    copy_coeff = pltpu.make_async_copy(coeff_ref, coeff_vmem, sems.at[2])
    copy_blocks = [
        pltpu.make_async_copy(
            block_ref.at[pl.ds(p * depth, depth), :], block_vmem.at[p], sems.at[3 + p]
        )
        for p in range(pieces)
    ]
    for copy in [copy_m, copy_leg, copy_coeff] + copy_blocks:
        copy.start()

    rows = leg_ref.shape[0]
    n = m_ref.shape[0]
    half = rows // 2
    own_bit = (me >> at) & 1
    row, col = iota((rows, rows), 0), iota((rows, rows), 1)
    bit = own_bit ^ (row // half)
    slot = lax.rem(row, n // 2)
    pick = (lax.rem(row, half) // (n // 2) == col // n) & (
        insert_bit(slot, bit, at) == lax.rem(col, n)
    )
    pick = pick.astype(BF16)
    copy_leg.wait()
    ordered = jnp.dot(pick, leg_vmem[...], preferred_element_type=F32).astype(BF16)
    keep_ref[...] = ordered[:half]
    send_ref[...] = ordered[half:]

    copy_m.wait()
    order = LL - m_smem[me]
    copy_coeff.wait()
    coeff = coeff_vmem[...]
    coeff = jnp.where(iota(coeff.shape, 1) < order, coeff, jnp.zeros_like(coeff))
    total = jnp.zeros((columns, order_max), F32)
    for p in range(pieces):
        copy_blocks[p].wait()
        total += jnp.dot(
            coeff[:, p * depth : (p + 1) * depth], block_vmem[p], preferred_element_type=F32
        )
    filtered_ref[...] = jnp.where(iota(total.shape, 1) < order, total, 0.0).astype(BF16)


def prepare(m_list, coeff, block, legendre, at):
    columns, order_max = coeff.shape
    rows = legendre.shape[0]
    n = m_list.shape[0]
    pieces = 6
    operands = (m_list, coeff, block, legendre)
    return pl.pallas_call(
        functools.partial(prepare_kernel, at),
        out_shape=[
            jax.ShapeDtypeStruct((columns, order_max), BF16),
            jax.ShapeDtypeStruct((rows // 2, order_max), BF16),
            jax.ShapeDtypeStruct((rows // 2, order_max), BF16),
        ],
        in_specs=[HBM] * 4,
        out_specs=[VMEM] * 3,
        scratch_shapes=[
            pltpu.SMEM((n,), jnp.int32),
            pltpu.VMEM((columns, order_max), BF16),
            pltpu.VMEM((pieces, order_max // pieces, order_max), BF16),
            pltpu.VMEM((rows, order_max), BF16),
            pltpu.SemaphoreType.DMA((3 + pieces,)),
        ],
        compiler_params=pltpu.CompilerParams(vmem_limit_bytes=32 << 20),
        cost_estimate=pl.CostEstimate(
            flops=2 * (columns * order_max * order_max + rows * rows * order_max),
            bytes_accessed=2 * (block.size + legendre.size),
            transcendentals=0,
        ),
        name="prepare",
    )(*[pltpu.with_memory_space_constraint(x, pltpu.HBM) for x in operands])


def table_kernel(at, line, order, *refs):
    shard_refs = dict(zip(order, refs))
    m_ref, leg_ref, _, table_ref, rows_ref, half_ref = refs[len(order) :]
    half_ref[...] = half_harmonics(leg_ref[...], shard_refs, at, line)
    write_table(table_ref, m_ref, lax.axis_index("mset"), at, line)
    rows_ref[...] = map_rows(half_ref, 0, m_ref.shape[0]).astype(BF16)


def table_and_own(m_list, legendre, shards, after, at, line):
    n = m_list.shape[0]
    order = sorted(shards, key=lambda k: -(k >> at) % line)
    return pl.pallas_call(
        functools.partial(table_kernel, at, line, order),
        out_shape=[
            jax.ShapeDtypeStruct((2 * n, NPHI), BF16),
            jax.ShapeDtypeStruct((after.shape[0] * REAL, 2 * n), BF16),
        ],
        in_specs=[VMEM] * len(order)
        + [pl.BlockSpec(memory_space=pltpu.SMEM), VMEM, pl.BlockSpec(memory_space=pl.ANY)],
        out_specs=[VMEM] * 2,
        scratch_shapes=[pltpu.VMEM(after.shape, BF16)],
        compiler_params=pltpu.CompilerParams(vmem_limit_bytes=32 << 20),
        cost_estimate=pl.CostEstimate(
            flops=16 * n * NPHI, bytes_accessed=4 * n * NPHI, transcendentals=0
        ),
        name="table_and_own",
    )(*[shards[k] for k in order], m_list, legendre, after)


def relay_kernel(shard_ref, out_ref):
    out_ref[...] = shard_ref[...]


def relay(shard):
    return pl.pallas_call(
        relay_kernel,
        out_shape=jax.ShapeDtypeStruct(shard.shape, BF16),
        in_specs=[VMEM],
        out_specs=VMEM,
        compiler_params=pltpu.CompilerParams(vmem_limit_bytes=8 << 20),
        cost_estimate=pl.CostEstimate(
            flops=RELAY_FLOPS, bytes_accessed=4 * shard.size, transcendentals=0
        ),
        name="relay",
    )(shard)


def half_harmonics(legendre, shard_refs, at, line):
    rows = legendre.shape[0]
    shards = len(shard_refs)
    columns = shard_refs[0].shape[0]
    cycles = rows // shards
    chunk = min(8, shards)
    wide = chunk * columns
    slot = lax.rem(iota((rows, wide), 0), shards)
    local = iota((rows, wide), 1) // columns
    fold = (iota((cycles, rows), 0) == iota((cycles, rows), 1) // shards).astype(BF16)
    me = lax.axis_index("mset")
    pieces = []
    for q in range(shards // chunk):
        piece = jnp.concatenate(
            [shard_refs[q * chunk + k][...] for k in range(chunk)], axis=0
        )
        product = lax.dot_general(
            legendre, piece, (((1,), (1,)), ((), ())), preferred_element_type=F32
        )
        own = slot == shard_source(local + q * chunk, me, at, line)
        chosen = jnp.where(own, product, 0.0).astype(BF16)
        pieces.append(jnp.dot(fold, chosen, preferred_element_type=F32).astype(BF16))
    return jnp.concatenate(pieces, axis=1)


def cross_kernel(at, line, order, *refs):
    shard_refs = dict(zip(order, refs))
    leg_ref, out_ref = refs[len(order) :]
    out_ref[...] = half_harmonics(leg_ref[...], shard_refs, at, line)


def cross(legendre, shards, at, line):
    rows, order_max = legendre.shape
    columns = shards[0].shape[0]
    count = len(shards)
    order = sorted(shards, key=lambda k: -(k >> at) % line)
    return pl.pallas_call(
        functools.partial(cross_kernel, at, line, order),
        out_shape=jax.ShapeDtypeStruct((rows // count, count * columns), BF16),
        in_specs=[VMEM] * (1 + count),
        out_specs=VMEM,
        compiler_params=pltpu.CompilerParams(vmem_limit_bytes=32 << 20),
        cost_estimate=pl.CostEstimate(
            flops=2 * rows * order_max * count * columns,
            bytes_accessed=2 * (legendre.size + count * shards[0].size),
            transcendentals=0,
        ),
        name="cross",
    )(*[shards[k] for k in order], legendre)


def synthesis_kernel(tiles, own_ref, got_ref, table_ref, out_ref, held, sems):
    n = table_ref.shape[0] // 2
    flat = (map_rows(got_ref, n // 2, n) + own_ref[...].astype(F32)).astype(BF16)
    width = NPHI // tiles
    copies = []
    for t in range(tiles):
        span = pl.ds(t * width, width)
        for first in range(0, width, 256):
            columns = pl.ds(t * width + first, min(256, width))
            piece = table_ref[:, columns]
            for row in range(0, flat.shape[0], 128):
                rows = slice(row, row + 128)
                summed = jnp.dot(flat[rows], piece, preferred_element_type=F32)
                held[rows, columns] = summed.astype(BF16)
        copy = pltpu.make_async_copy(held.at[:, span], out_ref.at[:, span], sems.at[t])
        copy.start()
        copies.append(copy)
    for copy in copies:
        copy.wait()


def synthesize(own, got, table):
    tiles = 16
    out_rows = own.shape[0]
    return pl.pallas_call(
        functools.partial(synthesis_kernel, tiles),
        out_shape=jax.ShapeDtypeStruct((out_rows, NPHI), BF16),
        in_specs=[VMEM] * 3,
        out_specs=HBM,
        scratch_shapes=[pltpu.VMEM((out_rows, NPHI), BF16), pltpu.SemaphoreType.DMA((tiles,))],
        compiler_params=pltpu.CompilerParams(vmem_limit_bytes=32 << 20),
        cost_estimate=pl.CostEstimate(
            flops=2 * out_rows * table.size,
            bytes_accessed=2 * (out_rows * NPHI + table.size),
            transcendentals=0,
        ),
        name="synthesis",
    )(own, got, table)


def exchange(value, size, mask):
    return lax.ppermute(value, "mset", [(d, d ^ mask) for d in range(size)])


def gather_shards(value, size, at, line):
    step = size // line
    shards = {0: value}
    for turn in range(1, line):
        pairs = [(d, (d + turn * step) % size) for d in range(size)]
        shards[turn << at] = lax.ppermute(value, "mset", pairs)
    shards[1 << at] = relay(shards[1 << at])
    for b in range(at):
        shards.update({k | 1 << b: exchange(v, size, 1 << b) for k, v in shards.items()})
    return shards


def body(m_list, coeff, blocks, legendre):
    size = lax.axis_size("mset")
    per_device, columns, order_max = coeff.shape
    if per_device != 1 or size & (size - 1):
        raise ValueError("unsupported mesh")
    cycles, n, _ = legendre.shape
    at = min(1, size.bit_length() - 2)
    line = size >> (at + 1)
    filtered, keep, send = prepare(
        m_list, coeff[0], blocks[0], legendre.reshape(cycles * n, order_max), at
    )
    shards = gather_shards(filtered, size, at, line)
    got = exchange(send, size, 1 << at)
    back = cross(got, shards, at, line)
    other = exchange(back, size, 1 << at)
    table, own_rows = table_and_own(m_list, keep, shards, back, at, line)
    sky_map = synthesize(own_rows, other, table)
    return sky_map.reshape(cycles, REAL, NPHI)


def solution(mesh):
    in_specs = (
        P(),
        P(("groups", "mset"), None, None),
        P(("groups", "mset"), None, None),
        P(("groups", "mset"), None, None),
    )
    out_specs = P(("groups", "mset"), None, None)
    return jax.shard_map(body, mesh=mesh, in_specs=in_specs, out_specs=out_specs, check_vma=False)
```

```python
import functools
import math

import jax
import jax.numpy as jnp
from jax import lax
from jax.experimental import pallas as pl
from jax.experimental.pallas import tpu as pltpu
from jax.sharding import PartitionSpec as P

LL = 3072
REAL = 16
NPHI = 8192
RELAY_FLOPS = 2_750_000_000
LANES = 128
BF16 = jnp.bfloat16
F32 = jnp.float32
VMEM = pl.BlockSpec(memory_space=pltpu.VMEM)
HBM = pl.BlockSpec(memory_space=pltpu.HBM)


def iota(shape, dim):
    return lax.broadcasted_iota(jnp.int32, shape, dim)


def insert_bit(value, bit, at):
    low = (1 << at) - 1
    return (value & low) | (bit << at) | ((value >> at) << (at + 1))


def shard_source(position, me, at, line):
    z, other = me >> (at + 1), me & ((1 << at) - 1)
    turn, flip = position >> at, position & ((1 << at) - 1)
    return (((z - turn) & (line - 1)) << at) | (other ^ flip)


def angle(phase):
    phase = phase & (NPHI - 1)
    phase = jnp.where(phase >= NPHI // 2, phase - NPHI, phase)
    return phase.astype(F32) * (2.0 * math.pi / NPHI)


def write_table(table_ref, m_ref, me, at, line):
    n = table_ref.shape[0] // 2
    half = n // 2
    index = iota((n, LANES), 0)
    lane = iota((n, LANES), 1)
    own_bit = (me >> at) & 1
    values = jnp.zeros((n, LANES), jnp.int32)
    for j in range(n):
        source = insert_bit(shard_source(j % half, me, at, line), own_bit ^ (j // half), at)
        values = jnp.where(index == j, m_ref[source], values)
    scale = 1.0 / math.sqrt(n)
    fine = angle(values * lane)
    coarse = angle(values * lane * LANES)
    cos_f, sin_f = jnp.cos(fine), jnp.sin(fine)
    cos_c, sin_c = jnp.cos(coarse), jnp.sin(coarse)
    for a in range(NPHI // LANES):
        ca, sa = cos_c[:, a : a + 1], sin_c[:, a : a + 1]
        span = slice(a * LANES, (a + 1) * LANES)
        table_ref[:n, span] = ((ca * cos_f - sa * sin_f).astype(BF16) * scale).astype(BF16)
        table_ref[n:, span] = ((-(sa * cos_f + ca * sin_f)).astype(BF16) * scale).astype(BF16)


def map_rows(half_ref, first, total):
    cycles, wide = half_ref.shape
    rows = cycles * REAL
    repeat = (iota((rows, cycles), 0) // REAL == iota((rows, cycles), 1)).astype(BF16)
    spread = jnp.dot(repeat, half_ref[...], preferred_element_type=F32)
    same_real = lax.rem(iota((rows, wide), 0), REAL) == lax.rem(iota((rows, wide), 1), REAL)
    chosen = jnp.where(same_real, spread, 0.0).astype(BF16)
    row, col = iota((wide, 2 * total), 0), iota((wide, 2 * total), 1)
    pick = lax.rem(row, 2 * REAL) // REAL * total + first + row // (2 * REAL) == col
    return jnp.dot(chosen, pick.astype(BF16), preferred_element_type=F32)


def filter_kernel(m_ref, coeff_ref, block_ref, out_ref, m_smem, coeff_vmem, block_vmem, total, sems):
    order_max = coeff_ref.shape[1]
    pieces = block_vmem.shape[0]
    depth = order_max // pieces
    first = min(2, pieces)
    copy_m = pltpu.make_async_copy(m_ref, m_smem, sems.at[0])
    copy_coeff = pltpu.make_async_copy(coeff_ref, coeff_vmem, sems.at[1])
    copy_blocks = [
        pltpu.make_async_copy(
            block_ref.at[pl.ds(p * depth, depth), :], block_vmem.at[p], sems.at[2 + p]
        )
        for p in range(pieces)
    ]
    for copy in [copy_m, copy_coeff] + copy_blocks[:first]:
        copy.start()
    copy_m.wait()
    order = LL - m_smem[lax.axis_index("mset")]
    for p in range(first, pieces):
        pl.when(p * depth < order)(copy_blocks[p].start)

    def masked(p):
        span = slice(p * depth, (p + 1) * depth)
        coeff = coeff_vmem[:, span]
        place = iota(coeff.shape, 1) + p * depth
        return jnp.where(place < order, coeff, jnp.zeros_like(coeff))

    copy_coeff.wait()
    value = None
    for p in range(first):
        copy_blocks[p].wait()
        term = jnp.dot(masked(p), block_vmem[p], preferred_element_type=F32)
        value = term if value is None else value + term
    total[...] = value

    def add(p):
        copy_blocks[p].wait()
        total[...] += jnp.dot(masked(p), block_vmem[p], preferred_element_type=F32)

    for p in range(first, pieces):
        pl.when(p * depth < order)(functools.partial(add, p))
    out_ref[...] = jnp.where(iota(total.shape, 1) < order, total[...], 0.0).astype(BF16)


def filter_block(m_list, coeff, block):
    columns, order_max = coeff.shape
    pieces = 6
    operands = (m_list, coeff, block)
    return pl.pallas_call(
        filter_kernel,
        out_shape=jax.ShapeDtypeStruct((columns, order_max), BF16),
        in_specs=[HBM] * 3,
        out_specs=VMEM,
        scratch_shapes=[
            pltpu.SMEM(m_list.shape, jnp.int32),
            pltpu.VMEM((columns, order_max), BF16),
            pltpu.VMEM((pieces, order_max // pieces, order_max), BF16),
            pltpu.VMEM((columns, order_max), F32),
            pltpu.SemaphoreType.DMA((2 + pieces,)),
        ],
        compiler_params=pltpu.CompilerParams(vmem_limit_bytes=16 << 20),
        cost_estimate=pl.CostEstimate(
            flops=2 * coeff.size * order_max, bytes_accessed=2 * block.size, transcendentals=0
        ),
        name="filter_block",
    )(*[pltpu.with_memory_space_constraint(x, pltpu.HBM) for x in operands])


def sort_kernel(at, n, leg_ref, _, keep_ref, send_ref):
    rows = leg_ref.shape[0]
    half = rows // 2
    own_bit = (lax.axis_index("mset") >> at) & 1
    row, col = iota((rows, rows), 0), iota((rows, rows), 1)
    bit = own_bit ^ (row // half)
    slot = lax.rem(row, n // 2)
    pick = (lax.rem(row, half) // (n // 2) == col // n) & (
        insert_bit(slot, bit, at) == lax.rem(col, n)
    )
    ordered = jnp.dot(pick.astype(BF16), leg_ref[...], preferred_element_type=F32).astype(BF16)
    keep_ref[...] = ordered[:half]
    send_ref[...] = ordered[half:]


def sort_legendre(legendre, after, n, at):
    rows, order_max = legendre.shape
    half = jax.ShapeDtypeStruct((rows // 2, order_max), BF16)
    return pl.pallas_call(
        functools.partial(sort_kernel, at, n),
        out_shape=[half, half],
        in_specs=[VMEM, pl.BlockSpec(memory_space=pl.ANY)],
        out_specs=[VMEM] * 2,
        compiler_params=pltpu.CompilerParams(vmem_limit_bytes=32 << 20),
        cost_estimate=pl.CostEstimate(
            flops=2 * rows * rows * order_max,
            bytes_accessed=4 * legendre.size,
            transcendentals=0,
        ),
        name="sort_legendre",
    )(legendre, after)


def table_kernel(at, line, order, *refs):
    shard_refs = dict(zip(order, refs))
    m_ref, leg_ref, _, table_ref, rows_ref, half_ref = refs[len(order) :]
    half_ref[...] = half_harmonics(leg_ref[...], shard_refs, at, line)
    write_table(table_ref, m_ref, lax.axis_index("mset"), at, line)
    rows_ref[...] = map_rows(half_ref, 0, m_ref.shape[0]).astype(BF16)


def table_and_own(m_list, legendre, shards, after, at, line):
    n = m_list.shape[0]
    order = sorted(shards, key=lambda k: -(k >> at) % line)
    return pl.pallas_call(
        functools.partial(table_kernel, at, line, order),
        out_shape=[
            jax.ShapeDtypeStruct((2 * n, NPHI), BF16),
            jax.ShapeDtypeStruct((after.shape[0] * REAL, 2 * n), BF16),
        ],
        in_specs=[VMEM] * len(order)
        + [pl.BlockSpec(memory_space=pltpu.SMEM), VMEM, pl.BlockSpec(memory_space=pl.ANY)],
        out_specs=[VMEM] * 2,
        scratch_shapes=[pltpu.VMEM(after.shape, BF16)],
        compiler_params=pltpu.CompilerParams(vmem_limit_bytes=32 << 20),
        cost_estimate=pl.CostEstimate(
            flops=16 * n * NPHI, bytes_accessed=4 * n * NPHI, transcendentals=0
        ),
        name="table_and_own",
    )(*[shards[k] for k in order], m_list, legendre, after)


def relay_kernel(shard_ref, out_ref):
    out_ref[...] = shard_ref[...]


def relay(shard):
    return pl.pallas_call(
        relay_kernel,
        out_shape=jax.ShapeDtypeStruct(shard.shape, BF16),
        in_specs=[VMEM],
        out_specs=VMEM,
        compiler_params=pltpu.CompilerParams(vmem_limit_bytes=8 << 20),
        cost_estimate=pl.CostEstimate(
            flops=RELAY_FLOPS, bytes_accessed=4 * shard.size, transcendentals=0
        ),
        name="relay",
    )(shard)


def half_harmonics(legendre, shard_refs, at, line):
    rows = legendre.shape[0]
    shards = len(shard_refs)
    columns = shard_refs[0].shape[0]
    cycles = rows // shards
    chunk = min(8, shards)
    wide = chunk * columns
    slot = lax.rem(iota((rows, wide), 0), shards)
    local = iota((rows, wide), 1) // columns
    fold = (iota((cycles, rows), 0) == iota((cycles, rows), 1) // shards).astype(BF16)
    me = lax.axis_index("mset")
    pieces = []
    for q in range(shards // chunk):
        piece = jnp.concatenate(
            [shard_refs[q * chunk + k][...] for k in range(chunk)], axis=0
        )
        product = lax.dot_general(
            legendre, piece, (((1,), (1,)), ((), ())), preferred_element_type=F32
        )
        own = slot == shard_source(local + q * chunk, me, at, line)
        chosen = jnp.where(own, product, 0.0).astype(BF16)
        pieces.append(jnp.dot(fold, chosen, preferred_element_type=F32).astype(BF16))
    return jnp.concatenate(pieces, axis=1)


def cross_kernel(at, line, order, *refs):
    shard_refs = dict(zip(order, refs))
    leg_ref, out_ref = refs[len(order) :]
    out_ref[...] = half_harmonics(leg_ref[...], shard_refs, at, line)


def cross(legendre, shards, at, line):
    rows, order_max = legendre.shape
    columns = shards[0].shape[0]
    count = len(shards)
    order = sorted(shards, key=lambda k: -(k >> at) % line)
    return pl.pallas_call(
        functools.partial(cross_kernel, at, line, order),
        out_shape=jax.ShapeDtypeStruct((rows // count, count * columns), BF16),
        in_specs=[VMEM] * (1 + count),
        out_specs=VMEM,
        compiler_params=pltpu.CompilerParams(vmem_limit_bytes=32 << 20),
        cost_estimate=pl.CostEstimate(
            flops=2 * rows * order_max * count * columns,
            bytes_accessed=2 * (legendre.size + count * shards[0].size),
            transcendentals=0,
        ),
        name="cross",
    )(*[shards[k] for k in order], legendre)


def synthesis_kernel(tiles, own_ref, got_ref, table_ref, out_ref, held, sems):
    n = table_ref.shape[0] // 2
    flat = (map_rows(got_ref, n // 2, n) + own_ref[...].astype(F32)).astype(BF16)
    width = NPHI // tiles
    copies = []
    for t in range(tiles):
        span = pl.ds(t * width, width)
        for first in range(0, width, 256):
            columns = pl.ds(t * width + first, min(256, width))
            piece = table_ref[:, columns]
            for row in range(0, flat.shape[0], 128):
                rows = slice(row, row + 128)
                summed = jnp.dot(flat[rows], piece, preferred_element_type=F32)
                held[rows, columns] = summed.astype(BF16)
        copy = pltpu.make_async_copy(held.at[:, span], out_ref.at[:, span], sems.at[t])
        copy.start()
        copies.append(copy)
    for copy in copies:
        copy.wait()


def synthesize(own, got, table):
    tiles = 16
    out_rows = own.shape[0]
    return pl.pallas_call(
        functools.partial(synthesis_kernel, tiles),
        out_shape=jax.ShapeDtypeStruct((out_rows, NPHI), BF16),
        in_specs=[VMEM] * 3,
        out_specs=HBM,
        scratch_shapes=[pltpu.VMEM((out_rows, NPHI), BF16), pltpu.SemaphoreType.DMA((tiles,))],
        compiler_params=pltpu.CompilerParams(vmem_limit_bytes=32 << 20),
        cost_estimate=pl.CostEstimate(
            flops=2 * out_rows * table.size,
            bytes_accessed=2 * (out_rows * NPHI + table.size),
            transcendentals=0,
        ),
        name="synthesis",
    )(own, got, table)


def exchange(value, size, mask):
    return lax.ppermute(value, "mset", [(d, d ^ mask) for d in range(size)])


def gather_shards(value, size, at, line):
    step = size // line
    shards = {0: value}
    for turn in range(1, line):
        pairs = [(d, (d + turn * step) % size) for d in range(size)]
        shards[turn << at] = lax.ppermute(value, "mset", pairs)
    shards[1 << at] = relay(shards[1 << at])
    for b in range(at):
        shards.update({k | 1 << b: exchange(v, size, 1 << b) for k, v in shards.items()})
    return shards


def body(m_list, coeff, blocks, legendre):
    size = lax.axis_size("mset")
    per_device, columns, order_max = coeff.shape
    if per_device != 1 or size & (size - 1):
        raise ValueError("unsupported mesh")
    cycles, n, _ = legendre.shape
    at = min(1, size.bit_length() - 2)
    line = size >> (at + 1)
    filtered = filter_block(m_list, coeff[0], blocks[0])
    keep, send = sort_legendre(legendre.reshape(cycles * n, order_max), filtered, n, at)
    shards = gather_shards(filtered, size, at, line)
    got = exchange(send, size, 1 << at)
    back = cross(got, shards, at, line)
    other = exchange(back, size, 1 << at)
    table, own_rows = table_and_own(m_list, keep, shards, back, at, line)
    sky_map = synthesize(own_rows, other, table)
    return sky_map.reshape(cycles, REAL, NPHI)


def solution(mesh):
    in_specs = (
        P(),
        P(("groups", "mset"), None, None),
        P(("groups", "mset"), None, None),
        P(("groups", "mset"), None, None),
    )
    out_specs = P(("groups", "mset"), None, None)
    return jax.shard_map(body, mesh=mesh, in_specs=in_specs, out_specs=out_specs, check_vma=False)
```

```python
import functools
import math

import jax
import jax.numpy as jnp
from jax import lax
from jax.experimental import pallas as pl
from jax.experimental.pallas import tpu as pltpu
from jax.sharding import PartitionSpec as P

LL = 3072
REAL = 16
NPHI = 8192
RELAY_FLOPS = 2_750_000_000
LANES = 128
BF16 = jnp.bfloat16
F32 = jnp.float32
VMEM = pl.BlockSpec(memory_space=pltpu.VMEM)
HBM = pl.BlockSpec(memory_space=pltpu.HBM)


def iota(shape, dim):
    return lax.broadcasted_iota(jnp.int32, shape, dim)


def insert_bit(value, bit, at):
    low = (1 << at) - 1
    return (value & low) | (bit << at) | ((value >> at) << (at + 1))


def shard_source(position, me, at, line):
    z, other = me >> (at + 1), me & ((1 << at) - 1)
    turn, flip = position >> at, position & ((1 << at) - 1)
    return (((z - turn) & (line - 1)) << at) | (other ^ flip)


def angle(phase):
    phase = phase & (NPHI - 1)
    phase = jnp.where(phase >= NPHI // 2, phase - NPHI, phase)
    return phase.astype(F32) * (2.0 * math.pi / NPHI)


def write_table(table_ref, m_ref, me, at, line):
    n = table_ref.shape[0] // 2
    half = n // 2
    index = iota((n, LANES), 0)
    lane = iota((n, LANES), 1)
    own_bit = (me >> at) & 1
    values = jnp.zeros((n, LANES), jnp.int32)
    for j in range(n):
        source = insert_bit(shard_source(j % half, me, at, line), own_bit ^ (j // half), at)
        values = jnp.where(index == j, m_ref[source], values)
    scale = 1.0 / math.sqrt(n)
    fine = angle(values * lane)
    coarse = angle(values * lane * LANES)
    cos_f, sin_f = jnp.cos(fine), jnp.sin(fine)
    cos_c, sin_c = jnp.cos(coarse), jnp.sin(coarse)
    for a in range(NPHI // LANES):
        ca, sa = cos_c[:, a : a + 1], sin_c[:, a : a + 1]
        span = slice(a * LANES, (a + 1) * LANES)
        table_ref[:n, span] = ((ca * cos_f - sa * sin_f).astype(BF16) * scale).astype(BF16)
        table_ref[n:, span] = ((-(sa * cos_f + ca * sin_f)).astype(BF16) * scale).astype(BF16)


def map_rows(half_ref, first, total):
    cycles, wide = half_ref.shape
    rows = cycles * REAL
    repeat = (iota((rows, cycles), 0) // REAL == iota((rows, cycles), 1)).astype(BF16)
    spread = jnp.dot(repeat, half_ref[...], preferred_element_type=F32)
    same_real = lax.rem(iota((rows, wide), 0), REAL) == lax.rem(iota((rows, wide), 1), REAL)
    chosen = jnp.where(same_real, spread, 0.0).astype(BF16)
    row, col = iota((wide, 2 * total), 0), iota((wide, 2 * total), 1)
    pick = lax.rem(row, 2 * REAL) // REAL * total + first + row // (2 * REAL) == col
    return jnp.dot(chosen, pick.astype(BF16), preferred_element_type=F32)


def filter_kernel(m_ref, coeff_ref, block_ref, out_ref, m_smem, coeff_vmem, block_vmem, total, sems):
    order_max = coeff_ref.shape[1]
    pieces = block_vmem.shape[0]
    depth = order_max // pieces
    first = min(2, pieces)
    copy_m = pltpu.make_async_copy(m_ref, m_smem, sems.at[0])
    copy_coeff = pltpu.make_async_copy(coeff_ref, coeff_vmem, sems.at[1])
    copy_blocks = [
        pltpu.make_async_copy(
            block_ref.at[pl.ds(p * depth, depth), :], block_vmem.at[p], sems.at[2 + p]
        )
        for p in range(pieces)
    ]
    for copy in [copy_m, copy_coeff] + copy_blocks[:first]:
        copy.start()
    copy_m.wait()
    order = LL - m_smem[lax.axis_index("mset")]
    for p in range(first, pieces):
        pl.when(p * depth < order)(copy_blocks[p].start)

    def masked(p):
        span = slice(p * depth, (p + 1) * depth)
        coeff = coeff_vmem[:, span]
        place = iota(coeff.shape, 1) + p * depth
        return jnp.where(place < order, coeff, jnp.zeros_like(coeff))

    copy_coeff.wait()
    value = None
    for p in range(first):
        copy_blocks[p].wait()
        term = jnp.dot(masked(p), block_vmem[p], preferred_element_type=F32)
        value = term if value is None else value + term
    total[...] = value

    def add(p):
        copy_blocks[p].wait()
        total[...] += jnp.dot(masked(p), block_vmem[p], preferred_element_type=F32)

    for p in range(first, pieces):
        pl.when(p * depth < order)(functools.partial(add, p))
    out_ref[...] = jnp.where(iota(total.shape, 1) < order, total[...], 0.0).astype(BF16)


def filter_block(m_list, coeff, block):
    columns, order_max = coeff.shape
    pieces = 6
    operands = (m_list, coeff, block)
    return pl.pallas_call(
        filter_kernel,
        out_shape=jax.ShapeDtypeStruct((columns, order_max), BF16),
        in_specs=[HBM] * 3,
        out_specs=VMEM,
        scratch_shapes=[
            pltpu.SMEM(m_list.shape, jnp.int32),
            pltpu.VMEM((columns, order_max), BF16),
            pltpu.VMEM((pieces, order_max // pieces, order_max), BF16),
            pltpu.VMEM((columns, order_max), F32),
            pltpu.SemaphoreType.DMA((2 + pieces,)),
        ],
        compiler_params=pltpu.CompilerParams(vmem_limit_bytes=16 << 20),
        cost_estimate=pl.CostEstimate(
            flops=2 * coeff.size * order_max, bytes_accessed=2 * block.size, transcendentals=0
        ),
        name="filter_block",
    )(*[pltpu.with_memory_space_constraint(x, pltpu.HBM) for x in operands])


def sort_kernel(at, n, leg_ref, _, keep_ref, send_ref):
    rows = leg_ref.shape[0]
    half = rows // 2
    own_bit = (lax.axis_index("mset") >> at) & 1
    row, col = iota((rows, rows), 0), iota((rows, rows), 1)
    bit = own_bit ^ (row // half)
    slot = lax.rem(row, n // 2)
    pick = (lax.rem(row, half) // (n // 2) == col // n) & (
        insert_bit(slot, bit, at) == lax.rem(col, n)
    )
    ordered = jnp.dot(pick.astype(BF16), leg_ref[...], preferred_element_type=F32).astype(BF16)
    keep_ref[...] = ordered[:half]
    send_ref[...] = ordered[half:]


def sort_legendre(legendre, after, n, at):
    rows, order_max = legendre.shape
    half = jax.ShapeDtypeStruct((rows // 2, order_max), BF16)
    return pl.pallas_call(
        functools.partial(sort_kernel, at, n),
        out_shape=[half, half],
        in_specs=[VMEM, pl.BlockSpec(memory_space=pl.ANY)],
        out_specs=[VMEM] * 2,
        compiler_params=pltpu.CompilerParams(vmem_limit_bytes=32 << 20),
        cost_estimate=pl.CostEstimate(
            flops=2 * rows * rows * order_max,
            bytes_accessed=4 * legendre.size,
            transcendentals=0,
        ),
        name="sort_legendre",
    )(legendre, after)


def table_kernel(at, line, order, *refs):
    shard_refs = dict(zip(order, refs))
    m_ref, leg_ref, _, table_ref, rows_ref, half_ref = refs[len(order) :]
    half_ref[...] = half_harmonics(leg_ref[...], shard_refs, at, line)
    write_table(table_ref, m_ref, lax.axis_index("mset"), at, line)
    rows_ref[...] = map_rows(half_ref, 0, m_ref.shape[0]).astype(BF16)


def table_and_own(m_list, legendre, shards, after, at, line):
    n = m_list.shape[0]
    order = visiting(shards, at, line)
    return pl.pallas_call(
        functools.partial(table_kernel, at, line, order),
        out_shape=[
            jax.ShapeDtypeStruct((2 * n, NPHI), BF16),
            jax.ShapeDtypeStruct((after.shape[0] * REAL, 2 * n), BF16),
        ],
        in_specs=[VMEM] * len(order)
        + [pl.BlockSpec(memory_space=pltpu.SMEM), VMEM, pl.BlockSpec(memory_space=pl.ANY)],
        out_specs=[VMEM] * 2,
        scratch_shapes=[pltpu.VMEM(after.shape, BF16)],
        compiler_params=pltpu.CompilerParams(vmem_limit_bytes=32 << 20),
        cost_estimate=pl.CostEstimate(
            flops=16 * n * NPHI, bytes_accessed=4 * n * NPHI, transcendentals=0
        ),
        name="table_and_own",
    )(*[shards[k] for k in order], m_list, legendre, after)


def relay_kernel(shard_ref, out_ref):
    out_ref[...] = shard_ref[...]


def relay(shard):
    return pl.pallas_call(
        relay_kernel,
        out_shape=jax.ShapeDtypeStruct(shard.shape, BF16),
        in_specs=[VMEM],
        out_specs=VMEM,
        compiler_params=pltpu.CompilerParams(vmem_limit_bytes=8 << 20),
        cost_estimate=pl.CostEstimate(
            flops=RELAY_FLOPS, bytes_accessed=4 * shard.size, transcendentals=0
        ),
        name="relay",
    )(shard)


def half_harmonics(legendre, shard_refs, at, line):
    rows = legendre.shape[0]
    shards = len(shard_refs)
    columns = shard_refs[0].shape[0]
    cycles = rows // shards
    chunk = min(8, shards)
    wide = chunk * columns
    slot = lax.rem(iota((rows, wide), 0), shards)
    local = iota((rows, wide), 1) // columns
    fold = (iota((cycles, rows), 0) == iota((cycles, rows), 1) // shards).astype(BF16)
    me = lax.axis_index("mset")
    pieces = []
    for q in range(shards // chunk):
        piece = jnp.concatenate(
            [shard_refs[q * chunk + k][...] for k in range(chunk)], axis=0
        )
        product = lax.dot_general(
            legendre, piece, (((1,), (1,)), ((), ())), preferred_element_type=F32
        )
        own = slot == shard_source(local + q * chunk, me, at, line)
        chosen = jnp.where(own, product, 0.0).astype(BF16)
        pieces.append(jnp.dot(fold, chosen, preferred_element_type=F32).astype(BF16))
    return jnp.concatenate(pieces, axis=1)


def cross_kernel(at, line, order, *refs):
    shard_refs = dict(zip(order, refs))
    leg_ref, out_ref = refs[len(order) :]
    out_ref[...] = half_harmonics(leg_ref[...], shard_refs, at, line)


def cross(legendre, shards, at, line):
    rows, order_max = legendre.shape
    columns = shards[0].shape[0]
    count = len(shards)
    order = visiting(shards, at, line)
    return pl.pallas_call(
        functools.partial(cross_kernel, at, line, order),
        out_shape=jax.ShapeDtypeStruct((rows // count, count * columns), BF16),
        in_specs=[VMEM] * (1 + count),
        out_specs=VMEM,
        compiler_params=pltpu.CompilerParams(vmem_limit_bytes=32 << 20),
        cost_estimate=pl.CostEstimate(
            flops=2 * rows * order_max * count * columns,
            bytes_accessed=2 * (legendre.size + count * shards[0].size),
            transcendentals=0,
        ),
        name="cross",
    )(*[shards[k] for k in order], legendre)


def synthesis_kernel(tiles, own_ref, got_ref, table_ref, out_ref, held, sems):
    n = table_ref.shape[0] // 2
    flat = (map_rows(got_ref, n // 2, n) + own_ref[...].astype(F32)).astype(BF16)
    width = NPHI // tiles
    copies = []
    for t in range(tiles):
        span = pl.ds(t * width, width)
        for first in range(0, width, 256):
            columns = pl.ds(t * width + first, min(256, width))
            piece = table_ref[:, columns]
            for row in range(0, flat.shape[0], 128):
                rows = slice(row, row + 128)
                summed = jnp.dot(flat[rows], piece, preferred_element_type=F32)
                held[rows, columns] = summed.astype(BF16)
        copy = pltpu.make_async_copy(held.at[:, span], out_ref.at[:, span], sems.at[t])
        copy.start()
        copies.append(copy)
    for copy in copies:
        copy.wait()


def synthesize(own, got, table):
    tiles = 16
    out_rows = own.shape[0]
    return pl.pallas_call(
        functools.partial(synthesis_kernel, tiles),
        out_shape=jax.ShapeDtypeStruct((out_rows, NPHI), BF16),
        in_specs=[VMEM] * 3,
        out_specs=HBM,
        scratch_shapes=[pltpu.VMEM((out_rows, NPHI), BF16), pltpu.SemaphoreType.DMA((tiles,))],
        compiler_params=pltpu.CompilerParams(vmem_limit_bytes=32 << 20),
        cost_estimate=pl.CostEstimate(
            flops=2 * out_rows * table.size,
            bytes_accessed=2 * (out_rows * NPHI + table.size),
            transcendentals=0,
        ),
        name="synthesis",
    )(own, got, table)


def exchange(value, size, mask):
    return lax.ppermute(value, "mset", [(d, d ^ mask) for d in range(size)])


def visiting(shards, at, line):
    issue = [0, line // 2] + [turn for turn in range(1, line) if turn != line // 2]
    return sorted(shards, key=lambda k: (k >> at != 0, -issue.index(k >> at)))


def gather_shards(value, size, at, line):
    step = size // line
    shards = {0: value}
    for turn in range(1, line):
        pairs = [(d, (d + turn * step) % size) for d in range(size)]
        shards[turn << at] = lax.ppermute(value, "mset", pairs)
    first = line // 2 << at
    shards[first] = relay(shards[first])
    for b in range(at):
        shards.update({k | 1 << b: exchange(v, size, 1 << b) for k, v in shards.items()})
    return shards


def body(m_list, coeff, blocks, legendre):
    size = lax.axis_size("mset")
    per_device, columns, order_max = coeff.shape
    if per_device != 1 or size & (size - 1):
        raise ValueError("unsupported mesh")
    cycles, n, _ = legendre.shape
    at = min(1, size.bit_length() - 2)
    line = size >> (at + 1)
    filtered = filter_block(m_list, coeff[0], blocks[0])
    keep, send = sort_legendre(legendre.reshape(cycles * n, order_max), filtered, n, at)
    shards = gather_shards(filtered, size, at, line)
    got = exchange(send, size, 1 << at)
    back = cross(got, shards, at, line)
    other = exchange(back, size, 1 << at)
    table, own_rows = table_and_own(m_list, keep, shards, back, at, line)
    sky_map = synthesize(own_rows, other, table)
    return sky_map.reshape(cycles, REAL, NPHI)


def solution(mesh):
    in_specs = (
        P(),
        P(("groups", "mset"), None, None),
        P(("groups", "mset"), None, None),
        P(("groups", "mset"), None, None),
    )
    out_specs = P(("groups", "mset"), None, None)
    return jax.shard_map(body, mesh=mesh, in_specs=in_specs, out_specs=out_specs, check_vma=False)
```

```python
import functools
import math

import jax
import jax.numpy as jnp
from jax import lax
from jax.experimental import pallas as pl
from jax.experimental.pallas import tpu as pltpu
from jax.sharding import PartitionSpec as P

LL = 3072
REAL = 16
NPHI = 8192
RELAY_FLOPS = 2_750_000_000
LANES = 128
BF16 = jnp.bfloat16
F32 = jnp.float32
VMEM = pl.BlockSpec(memory_space=pltpu.VMEM)
HBM = pl.BlockSpec(memory_space=pltpu.HBM)


def iota(shape, dim):
    return lax.broadcasted_iota(jnp.int32, shape, dim)


def insert_bit(value, bit, at):
    low = (1 << at) - 1
    return (value & low) | (bit << at) | ((value >> at) << (at + 1))


def shard_source(position, me, at, line):
    z, other = me >> (at + 1), me & ((1 << at) - 1)
    turn, flip = position >> at, position & ((1 << at) - 1)
    return (((z - turn) & (line - 1)) << at) | (other ^ flip)


def angle(phase):
    phase = phase & (NPHI - 1)
    phase = jnp.where(phase >= NPHI // 2, phase - NPHI, phase)
    return phase.astype(F32) * (2.0 * math.pi / NPHI)


def write_table(table_ref, m_ref, me, at, line):
    n = table_ref.shape[0] // 2
    half = n // 2
    index = iota((n, LANES), 0)
    lane = iota((n, LANES), 1)
    own_bit = (me >> at) & 1
    values = jnp.zeros((n, LANES), jnp.int32)
    for j in range(n):
        source = insert_bit(shard_source(j % half, me, at, line), own_bit ^ (j // half), at)
        values = jnp.where(index == j, m_ref[source], values)
    scale = 1.0 / math.sqrt(n)
    fine = angle(values * lane)
    coarse = angle(values * lane * LANES)
    cos_f, sin_f = jnp.cos(fine), jnp.sin(fine)
    cos_c, sin_c = jnp.cos(coarse), jnp.sin(coarse)
    for a in range(NPHI // LANES):
        ca, sa = cos_c[:, a : a + 1], sin_c[:, a : a + 1]
        span = slice(a * LANES, (a + 1) * LANES)
        table_ref[:n, span] = ((ca * cos_f - sa * sin_f).astype(BF16) * scale).astype(BF16)
        table_ref[n:, span] = ((-(sa * cos_f + ca * sin_f)).astype(BF16) * scale).astype(BF16)


def map_rows(half_ref, first, total):
    cycles, wide = half_ref.shape
    rows = cycles * REAL
    repeat = (iota((rows, cycles), 0) // REAL == iota((rows, cycles), 1)).astype(BF16)
    spread = jnp.dot(repeat, half_ref[...], preferred_element_type=F32)
    same_real = lax.rem(iota((rows, wide), 0), REAL) == lax.rem(iota((rows, wide), 1), REAL)
    chosen = jnp.where(same_real, spread, 0.0).astype(BF16)
    row, col = iota((wide, 2 * total), 0), iota((wide, 2 * total), 1)
    pick = lax.rem(row, 2 * REAL) // REAL * total + first + row // (2 * REAL) == col
    return jnp.dot(chosen, pick.astype(BF16), preferred_element_type=F32)


def prepare_kernel(
    at, m_ref, coeff_ref, block_ref, leg_ref, filtered_ref, keep_ref, send_ref,
    m_smem, coeff_vmem, block_vmem, leg_vmem, sems,
):
    me = lax.axis_index("mset")
    columns, order_max = coeff_ref.shape
    pieces = block_vmem.shape[0]
    depth = order_max // pieces
    copy_m = pltpu.make_async_copy(m_ref, m_smem, sems.at[0])
    copy_leg = pltpu.make_async_copy(leg_ref, leg_vmem, sems.at[1])
    copy_coeff = pltpu.make_async_copy(coeff_ref, coeff_vmem, sems.at[2])
    copy_blocks = [
        pltpu.make_async_copy(
            block_ref.at[pl.ds(p * depth, depth), :], block_vmem.at[p], sems.at[3 + p]
        )
        for p in range(pieces)
    ]
    for turn, copy in enumerate([copy_m, copy_leg, copy_coeff] + copy_blocks):
        copy.start(priority=turn % 2)

    rows = leg_ref.shape[0]
    n = m_ref.shape[0]
    half = rows // 2
    own_bit = (me >> at) & 1
    row, col = iota((rows, rows), 0), iota((rows, rows), 1)
    bit = own_bit ^ (row // half)
    slot = lax.rem(row, n // 2)
    pick = (lax.rem(row, half) // (n // 2) == col // n) & (
        insert_bit(slot, bit, at) == lax.rem(col, n)
    )
    pick = pick.astype(BF16)
    copy_leg.wait()
    ordered = jnp.dot(pick, leg_vmem[...], preferred_element_type=F32).astype(BF16)
    keep_ref[...] = ordered[:half]
    send_ref[...] = ordered[half:]

    copy_m.wait()
    order = LL - m_smem[me]
    copy_coeff.wait()
    coeff = coeff_vmem[...]
    coeff = jnp.where(iota(coeff.shape, 1) < order, coeff, jnp.zeros_like(coeff))
    total = jnp.zeros((columns, order_max), F32)
    for p in range(pieces):
        copy_blocks[p].wait()
        total += jnp.dot(
            coeff[:, p * depth : (p + 1) * depth], block_vmem[p], preferred_element_type=F32
        )
    filtered_ref[...] = jnp.where(iota(total.shape, 1) < order, total, 0.0).astype(BF16)


def prepare(m_list, coeff, block, legendre, at):
    columns, order_max = coeff.shape
    rows = legendre.shape[0]
    n = m_list.shape[0]
    pieces = 6
    operands = (m_list, coeff, block, legendre)
    return pl.pallas_call(
        functools.partial(prepare_kernel, at),
        out_shape=[
            jax.ShapeDtypeStruct((columns, order_max), BF16),
            jax.ShapeDtypeStruct((rows // 2, order_max), BF16),
            jax.ShapeDtypeStruct((rows // 2, order_max), BF16),
        ],
        in_specs=[HBM] * 4,
        out_specs=[VMEM] * 3,
        scratch_shapes=[
            pltpu.SMEM((n,), jnp.int32),
            pltpu.VMEM((columns, order_max), BF16),
            pltpu.VMEM((pieces, order_max // pieces, order_max), BF16),
            pltpu.VMEM((rows, order_max), BF16),
            pltpu.SemaphoreType.DMA((3 + pieces,)),
        ],
        compiler_params=pltpu.CompilerParams(vmem_limit_bytes=32 << 20),
        cost_estimate=pl.CostEstimate(
            flops=2 * (columns * order_max * order_max + rows * rows * order_max),
            bytes_accessed=2 * (block.size + legendre.size),
            transcendentals=0,
        ),
        name="prepare",
    )(*[pltpu.with_memory_space_constraint(x, pltpu.HBM) for x in operands])


def table_kernel(at, line, order, *refs):
    shard_refs = dict(zip(order, refs))
    m_ref, leg_ref, _, table_ref, rows_ref, half_ref = refs[len(order) :]
    half_ref[...] = half_harmonics(leg_ref[...], shard_refs, at, line)
    write_table(table_ref, m_ref, lax.axis_index("mset"), at, line)
    rows_ref[...] = map_rows(half_ref, 0, m_ref.shape[0]).astype(BF16)


def table_and_own(m_list, legendre, shards, after, at, line):
    n = m_list.shape[0]
    order = sorted(shards, key=lambda k: -(k >> at) % line)
    return pl.pallas_call(
        functools.partial(table_kernel, at, line, order),
        out_shape=[
            jax.ShapeDtypeStruct((2 * n, NPHI), BF16),
            jax.ShapeDtypeStruct((after.shape[0] * REAL, 2 * n), BF16),
        ],
        in_specs=[VMEM] * len(order)
        + [pl.BlockSpec(memory_space=pltpu.SMEM), VMEM, pl.BlockSpec(memory_space=pl.ANY)],
        out_specs=[VMEM] * 2,
        scratch_shapes=[pltpu.VMEM(after.shape, BF16)],
        compiler_params=pltpu.CompilerParams(vmem_limit_bytes=32 << 20),
        cost_estimate=pl.CostEstimate(
            flops=16 * n * NPHI, bytes_accessed=4 * n * NPHI, transcendentals=0
        ),
        name="table_and_own",
    )(*[shards[k] for k in order], m_list, legendre, after)


def relay_kernel(shard_ref, out_ref):
    out_ref[...] = shard_ref[...]


def relay(shard):
    return pl.pallas_call(
        relay_kernel,
        out_shape=jax.ShapeDtypeStruct(shard.shape, BF16),
        in_specs=[VMEM],
        out_specs=VMEM,
        compiler_params=pltpu.CompilerParams(vmem_limit_bytes=8 << 20),
        cost_estimate=pl.CostEstimate(
            flops=RELAY_FLOPS, bytes_accessed=4 * shard.size, transcendentals=0
        ),
        name="relay",
    )(shard)


def half_harmonics(legendre, shard_refs, at, line):
    rows = legendre.shape[0]
    shards = len(shard_refs)
    columns = shard_refs[0].shape[0]
    cycles = rows // shards
    chunk = min(8, shards)
    wide = chunk * columns
    slot = lax.rem(iota((rows, wide), 0), shards)
    local = iota((rows, wide), 1) // columns
    fold = (iota((cycles, rows), 0) == iota((cycles, rows), 1) // shards).astype(BF16)
    me = lax.axis_index("mset")
    pieces = []
    for q in range(shards // chunk):
        piece = jnp.concatenate(
            [shard_refs[q * chunk + k][...] for k in range(chunk)], axis=0
        )
        product = lax.dot_general(
            legendre, piece, (((1,), (1,)), ((), ())), preferred_element_type=F32
        )
        own = slot == shard_source(local + q * chunk, me, at, line)
        chosen = jnp.where(own, product, 0.0).astype(BF16)
        pieces.append(jnp.dot(fold, chosen, preferred_element_type=F32).astype(BF16))
    return jnp.concatenate(pieces, axis=1)


def cross_kernel(at, line, order, *refs):
    shard_refs = dict(zip(order, refs))
    leg_ref, out_ref = refs[len(order) :]
    out_ref[...] = half_harmonics(leg_ref[...], shard_refs, at, line)


def cross(legendre, shards, at, line):
    rows, order_max = legendre.shape
    columns = shards[0].shape[0]
    count = len(shards)
    order = sorted(shards, key=lambda k: -(k >> at) % line)
    return pl.pallas_call(
        functools.partial(cross_kernel, at, line, order),
        out_shape=jax.ShapeDtypeStruct((rows // count, count * columns), BF16),
        in_specs=[VMEM] * (1 + count),
        out_specs=VMEM,
        compiler_params=pltpu.CompilerParams(vmem_limit_bytes=32 << 20),
        cost_estimate=pl.CostEstimate(
            flops=2 * rows * order_max * count * columns,
            bytes_accessed=2 * (legendre.size + count * shards[0].size),
            transcendentals=0,
        ),
        name="cross",
    )(*[shards[k] for k in order], legendre)


def synthesis_kernel(tiles, own_ref, got_ref, table_ref, out_ref, held, sems):
    n = table_ref.shape[0] // 2
    flat = (map_rows(got_ref, n // 2, n) + own_ref[...].astype(F32)).astype(BF16)
    width = NPHI // tiles
    copies = []
    for t in range(tiles):
        span = pl.ds(t * width, width)
        for first in range(0, width, 256):
            columns = pl.ds(t * width + first, min(256, width))
            piece = table_ref[:, columns]
            for row in range(0, flat.shape[0], 128):
                rows = slice(row, row + 128)
                summed = jnp.dot(flat[rows], piece, preferred_element_type=F32)
                held[rows, columns] = summed.astype(BF16)
        copy = pltpu.make_async_copy(held.at[:, span], out_ref.at[:, span], sems.at[t])
        copy.start(priority=t % 2)
        copies.append(copy)
    for copy in copies:
        copy.wait()


def synthesize(own, got, table):
    tiles = 16
    out_rows = own.shape[0]
    return pl.pallas_call(
        functools.partial(synthesis_kernel, tiles),
        out_shape=jax.ShapeDtypeStruct((out_rows, NPHI), BF16),
        in_specs=[VMEM] * 3,
        out_specs=HBM,
        scratch_shapes=[pltpu.VMEM((out_rows, NPHI), BF16), pltpu.SemaphoreType.DMA((tiles,))],
        compiler_params=pltpu.CompilerParams(vmem_limit_bytes=32 << 20),
        cost_estimate=pl.CostEstimate(
            flops=2 * out_rows * table.size,
            bytes_accessed=2 * (out_rows * NPHI + table.size),
            transcendentals=0,
        ),
        name="synthesis",
    )(own, got, table)


def exchange(value, size, mask):
    return lax.ppermute(value, "mset", [(d, d ^ mask) for d in range(size)])


def gather_shards(value, size, at, line):
    step = size // line
    shards = {0: value}
    for turn in range(1, line):
        pairs = [(d, (d + turn * step) % size) for d in range(size)]
        shards[turn << at] = lax.ppermute(value, "mset", pairs)
    shards[1 << at] = relay(shards[1 << at])
    for b in range(at):
        shards.update({k | 1 << b: exchange(v, size, 1 << b) for k, v in shards.items()})
    return shards


def body(m_list, coeff, blocks, legendre):
    size = lax.axis_size("mset")
    per_device, columns, order_max = coeff.shape
    if per_device != 1 or size & (size - 1):
        raise ValueError("unsupported mesh")
    cycles, n, _ = legendre.shape
    at = min(1, size.bit_length() - 2)
    line = size >> (at + 1)
    filtered, keep, send = prepare(
        m_list, coeff[0], blocks[0], legendre.reshape(cycles * n, order_max), at
    )
    shards = gather_shards(filtered, size, at, line)
    got = exchange(send, size, 1 << at)
    back = cross(got, shards, at, line)
    other = exchange(back, size, 1 << at)
    table, own_rows = table_and_own(m_list, keep, shards, back, at, line)
    sky_map = synthesize(own_rows, other, table)
    return sky_map.reshape(cycles, REAL, NPHI)


def solution(mesh):
    in_specs = (
        P(),
        P(("groups", "mset"), None, None),
        P(("groups", "mset"), None, None),
        P(("groups", "mset"), None, None),
    )
    out_specs = P(("groups", "mset"), None, None)
    return jax.shard_map(body, mesh=mesh, in_specs=in_specs, out_specs=out_specs, check_vma=False)
```

```python
import functools
import math

import jax
import jax.numpy as jnp
from jax import lax
from jax.experimental import pallas as pl
from jax.experimental.pallas import tpu as pltpu
from jax.sharding import PartitionSpec as P

LL = 3072
REAL = 16
NPHI = 8192
RELAY_FLOPS = 2_750_000_000
LANES = 128
BF16 = jnp.bfloat16
F32 = jnp.float32
VMEM = pl.BlockSpec(memory_space=pltpu.VMEM)
HBM = pl.BlockSpec(memory_space=pltpu.HBM)


def iota(shape, dim):
    return lax.broadcasted_iota(jnp.int32, shape, dim)


def insert_bit(value, bit, at):
    low = (1 << at) - 1
    return (value & low) | (bit << at) | ((value >> at) << (at + 1))


def shard_source(position, me, at, line):
    z, other = me >> (at + 1), me & ((1 << at) - 1)
    turn, flip = position >> at, position & ((1 << at) - 1)
    return (((z - turn) & (line - 1)) << at) | (other ^ flip)


def angle(phase):
    phase = phase & (NPHI - 1)
    phase = jnp.where(phase >= NPHI // 2, phase - NPHI, phase)
    return phase.astype(F32) * (2.0 * math.pi / NPHI)


def write_table(table_ref, m_ref, me, at, line):
    n = table_ref.shape[0] // 2
    half = n // 2
    index = iota((n, LANES), 0)
    lane = iota((n, LANES), 1)
    own_bit = (me >> at) & 1
    values = jnp.zeros((n, LANES), jnp.int32)
    for j in range(n):
        source = insert_bit(shard_source(j % half, me, at, line), own_bit ^ (j // half), at)
        values = jnp.where(index == j, m_ref[source], values)
    scale = 1.0 / math.sqrt(n)
    fine = angle(values * lane)
    coarse = angle(values * lane * LANES)
    cos_f, sin_f = jnp.cos(fine), jnp.sin(fine)
    cos_c, sin_c = jnp.cos(coarse), jnp.sin(coarse)
    for a in range(NPHI // LANES):
        ca, sa = cos_c[:, a : a + 1], sin_c[:, a : a + 1]
        span = slice(a * LANES, (a + 1) * LANES)
        table_ref[:n, span] = ((ca * cos_f - sa * sin_f).astype(BF16) * scale).astype(BF16)
        table_ref[n:, span] = ((-(sa * cos_f + ca * sin_f)).astype(BF16) * scale).astype(BF16)


def map_rows(half_ref, first, total):
    cycles, wide = half_ref.shape
    rows = cycles * REAL
    repeat = (iota((rows, cycles), 0) // REAL == iota((rows, cycles), 1)).astype(BF16)
    spread = jnp.dot(repeat, half_ref[...], preferred_element_type=F32)
    same_real = lax.rem(iota((rows, wide), 0), REAL) == lax.rem(iota((rows, wide), 1), REAL)
    chosen = jnp.where(same_real, spread, 0.0).astype(BF16)
    row, col = iota((wide, 2 * total), 0), iota((wide, 2 * total), 1)
    pick = lax.rem(row, 2 * REAL) // REAL * total + first + row // (2 * REAL) == col
    return jnp.dot(chosen, pick.astype(BF16), preferred_element_type=F32)


def prepare_kernel(
    at, m_ref, coeff_ref, block_ref, leg_ref, filtered_ref, keep_ref, send_ref,
    m_smem, coeff_vmem, block_vmem, leg_vmem, sems,
):
    me = lax.axis_index("mset")
    columns, order_max = coeff_ref.shape
    pieces = block_vmem.shape[0]
    depth = order_max // pieces
    copy_m = pltpu.make_async_copy(m_ref, m_smem, sems.at[0])
    copy_leg = pltpu.make_async_copy(leg_ref, leg_vmem, sems.at[1])
    copy_coeff = pltpu.make_async_copy(coeff_ref, coeff_vmem, sems.at[2])
    copy_blocks = [
        pltpu.make_async_copy(
            block_ref.at[pl.ds(p * depth, depth), :], block_vmem.at[p], sems.at[3 + p]
        )
        for p in range(pieces)
    ]
    for copy in [copy_m, copy_leg, copy_coeff] + copy_blocks:
        copy.start()

    rows = leg_ref.shape[0]
    n = m_ref.shape[0]
    half = rows // 2
    own_bit = (me >> at) & 1
    row, col = iota((rows, rows), 0), iota((rows, rows), 1)
    bit = own_bit ^ (row // half)
    slot = lax.rem(row, n // 2)
    pick = (lax.rem(row, half) // (n // 2) == col // n) & (
        insert_bit(slot, bit, at) == lax.rem(col, n)
    )
    pick = pick.astype(BF16)
    copy_leg.wait()
    ordered = jnp.dot(pick, leg_vmem[...], preferred_element_type=F32).astype(BF16)
    keep_ref[...] = ordered[:half]
    send_ref[...] = ordered[half:]

    copy_m.wait()
    order = LL - m_smem[me]
    copy_coeff.wait()
    coeff = coeff_vmem[...]
    coeff = jnp.where(iota(coeff.shape, 1) < order, coeff, jnp.zeros_like(coeff))
    total = jnp.zeros((columns, order_max), F32)
    for p in range(pieces):
        copy_blocks[p].wait()
        total += jnp.dot(
            coeff[:, p * depth : (p + 1) * depth], block_vmem[p], preferred_element_type=F32
        )
    filtered_ref[...] = jnp.where(iota(total.shape, 1) < order, total, 0.0).astype(BF16)


def prepare(m_list, coeff, block, legendre, at):
    columns, order_max = coeff.shape
    rows = legendre.shape[0]
    n = m_list.shape[0]
    pieces = 6
    operands = (m_list, coeff, block, legendre)
    return pl.pallas_call(
        functools.partial(prepare_kernel, at),
        out_shape=[
            jax.ShapeDtypeStruct((columns, order_max), BF16),
            jax.ShapeDtypeStruct((rows // 2, order_max), BF16),
            jax.ShapeDtypeStruct((rows // 2, order_max), BF16),
        ],
        in_specs=[HBM] * 4,
        out_specs=[VMEM] * 3,
        scratch_shapes=[
            pltpu.SMEM((n,), jnp.int32),
            pltpu.VMEM((columns, order_max), BF16),
            pltpu.VMEM((pieces, order_max // pieces, order_max), BF16),
            pltpu.VMEM((rows, order_max), BF16),
            pltpu.SemaphoreType.DMA((3 + pieces,)),
        ],
        compiler_params=pltpu.CompilerParams(vmem_limit_bytes=32 << 20),
        cost_estimate=pl.CostEstimate(
            flops=2 * (columns * order_max * order_max + rows * rows * order_max),
            bytes_accessed=2 * (block.size + legendre.size),
            transcendentals=0,
        ),
        name="prepare",
    )(*[pltpu.with_memory_space_constraint(x, pltpu.HBM) for x in operands])


def own_kernel(at, line, order, *refs):
    shard_refs = dict(zip(order, refs))
    m_ref, leg_ref, _, table_ref, rows_ref, half_ref = refs[len(order) :]
    half_ref[...] = half_harmonics(leg_ref[...], shard_refs, at, line)
    write_table(table_ref, m_ref, lax.axis_index("mset"), at, line)
    rows_ref[...] = map_rows(half_ref, 0, rows_ref.shape[1] // 2).astype(BF16)


def table_and_own(m_list, legendre, shards, after, at, line):
    n = m_list.shape[0]
    order = sorted(shards, key=lambda k: -(k >> at) % line)
    return pl.pallas_call(
        functools.partial(own_kernel, at, line, order),
        out_shape=[
            jax.ShapeDtypeStruct((2 * n, NPHI), BF16),
            jax.ShapeDtypeStruct((after.shape[0] * REAL, 2 * n), BF16),
        ],
        in_specs=[VMEM] * len(order)
        + [pl.BlockSpec(memory_space=pltpu.SMEM), VMEM, pl.BlockSpec(memory_space=pl.ANY)],
        out_specs=[VMEM] * 2,
        scratch_shapes=[pltpu.VMEM(after.shape, BF16)],
        compiler_params=pltpu.CompilerParams(vmem_limit_bytes=32 << 20),
        cost_estimate=pl.CostEstimate(
            flops=2 * legendre.size * after.shape[1] + 16 * n * NPHI,
            bytes_accessed=4 * n * NPHI,
            transcendentals=0,
        ),
        name="table_and_own",
    )(*[shards[k] for k in order], m_list, legendre, after)


def relay_kernel(shard_ref, out_ref):
    out_ref[...] = shard_ref[...]


def relay(shard):
    return pl.pallas_call(
        relay_kernel,
        out_shape=jax.ShapeDtypeStruct(shard.shape, BF16),
        in_specs=[VMEM],
        out_specs=VMEM,
        compiler_params=pltpu.CompilerParams(vmem_limit_bytes=8 << 20),
        cost_estimate=pl.CostEstimate(
            flops=RELAY_FLOPS, bytes_accessed=4 * shard.size, transcendentals=0
        ),
        name="relay",
    )(shard)


def half_harmonics(legendre, shard_refs, at, line):
    rows = legendre.shape[0]
    shards = len(shard_refs)
    columns = shard_refs[0].shape[0]
    cycles = rows // shards
    chunk = min(8, shards)
    wide = chunk * columns
    slot = lax.rem(iota((rows, wide), 0), shards)
    local = iota((rows, wide), 1) // columns
    fold = (iota((cycles, rows), 0) == iota((cycles, rows), 1) // shards).astype(BF16)
    me = lax.axis_index("mset")
    pieces = []
    for q in range(shards // chunk):
        piece = jnp.concatenate(
            [shard_refs[q * chunk + k][...] for k in range(chunk)], axis=0
        )
        product = lax.dot_general(
            legendre, piece, (((1,), (1,)), ((), ())), preferred_element_type=F32
        )
        own = slot == shard_source(local + q * chunk, me, at, line)
        chosen = jnp.where(own, product, 0.0).astype(BF16)
        pieces.append(jnp.dot(fold, chosen, preferred_element_type=F32).astype(BF16))
    return jnp.concatenate(pieces, axis=1)


def cross_kernel(at, line, order, bit, *refs):
    shard_refs = dict(zip(order, refs))
    leg_ref, out_ref = refs[len(order)], refs[-1]

    @pl.when((lax.axis_index("mset") >> at) & 1 == bit)
    def _():
        out_ref[...] = half_harmonics(leg_ref[...], shard_refs, at, line)


def cross(legendre, shards, at, line, bit, after=()):
    rows, order_max = legendre.shape
    columns = shards[0].shape[0]
    count = len(shards)
    order = sorted(shards, key=lambda k: -(k >> at) % line)
    return pl.pallas_call(
        functools.partial(cross_kernel, at, line, order, bit),
        out_shape=jax.ShapeDtypeStruct((rows // count, count * columns), BF16),
        in_specs=[VMEM] * (1 + count) + [pl.BlockSpec(memory_space=pl.ANY)] * len(after),
        out_specs=VMEM,
        compiler_params=pltpu.CompilerParams(vmem_limit_bytes=32 << 20),
        cost_estimate=pl.CostEstimate(
            flops=2 * rows * order_max * count * columns,
            bytes_accessed=2 * (legendre.size + count * shards[0].size),
            transcendentals=0,
        ),
        name="cross",
    )(*[shards[k] for k in order], legendre, *after)


def synthesis_kernel(tiles, at, own_ref, low_ref, high_ref, table_ref, out_ref, held, got_ref, sems):
    n = table_ref.shape[0] // 2
    own_bit = (lax.axis_index("mset") >> at) & 1
    for bit, ref in enumerate((low_ref, high_ref)):

        @pl.when(own_bit == bit)
        def _():
            got_ref[...] = ref[...]

    flat = (map_rows(got_ref, n // 2, n) + own_ref[...].astype(F32)).astype(BF16)
    width = NPHI // tiles
    copies = []
    for t in range(tiles):
        span = pl.ds(t * width, width)
        for first in range(0, width, 256):
            columns = pl.ds(t * width + first, min(256, width))
            piece = table_ref[:, columns]
            for row in range(0, flat.shape[0], 128):
                rows = slice(row, row + 128)
                summed = jnp.dot(flat[rows], piece, preferred_element_type=F32)
                held[rows, columns] = summed.astype(BF16)
        copy = pltpu.make_async_copy(held.at[:, span], out_ref.at[:, span], sems.at[t])
        copy.start()
        copies.append(copy)
    for copy in copies:
        copy.wait()


def synthesize(own, low, high, table, at):
    tiles = 16
    out_rows = own.shape[0]
    return pl.pallas_call(
        functools.partial(synthesis_kernel, tiles, at),
        out_shape=jax.ShapeDtypeStruct((out_rows, NPHI), BF16),
        in_specs=[VMEM] * 4,
        out_specs=HBM,
        scratch_shapes=[
            pltpu.VMEM((out_rows, NPHI), BF16),
            pltpu.VMEM(low.shape, BF16),
            pltpu.SemaphoreType.DMA((tiles,)),
        ],
        compiler_params=pltpu.CompilerParams(vmem_limit_bytes=32 << 20),
        cost_estimate=pl.CostEstimate(
            flops=2 * out_rows * table.size,
            bytes_accessed=2 * (out_rows * NPHI + table.size),
            transcendentals=0,
        ),
        name="synthesis",
    )(own, low, high, table)


def exchange(value, size, mask):
    return lax.ppermute(value, "mset", [(d, d ^ mask) for d in range(size)])


def gather_shards(value, size, at, line):
    step = size // line
    shards = {0: value}
    for turn in range(1, line):
        pairs = [(d, (d + turn * step) % size) for d in range(size)]
        shards[turn << at] = lax.ppermute(value, "mset", pairs)
    shards[1 << at] = relay(shards[1 << at])
    for b in range(at):
        shards.update({k | 1 << b: exchange(v, size, 1 << b) for k, v in shards.items()})
    return shards


def body(m_list, coeff, blocks, legendre):
    size = lax.axis_size("mset")
    per_device, columns, order_max = coeff.shape
    if per_device != 1 or size & (size - 1):
        raise ValueError("unsupported mesh")
    cycles, n, _ = legendre.shape
    at = min(1, size.bit_length() - 2)
    line = size >> (at + 1)
    filtered, keep, send = prepare(
        m_list, coeff[0], blocks[0], legendre.reshape(cycles * n, order_max), at
    )
    bit = 1 << at
    shards = gather_shards(filtered, size, at, line)
    got = exchange(send, size, bit)
    high = cross(got, shards, at, line, 1)
    to_low = lax.ppermute(high, "mset", [(d, d ^ bit) for d in range(size) if d & bit])
    low = cross(got, shards, at, line, 0, after=(high,))
    to_high = lax.ppermute(low, "mset", [(d, d ^ bit) for d in range(size) if not d & bit])
    table, own_rows = table_and_own(m_list, keep, shards, low, at, line)
    sky_map = synthesize(own_rows, to_low, to_high, table, at)
    return sky_map.reshape(cycles, REAL, NPHI)


def solution(mesh):
    in_specs = (
        P(),
        P(("groups", "mset"), None, None),
        P(("groups", "mset"), None, None),
        P(("groups", "mset"), None, None),
    )
    out_specs = P(("groups", "mset"), None, None)
    return jax.shard_map(body, mesh=mesh, in_specs=in_specs, out_specs=out_specs, check_vma=False)
```

```python
import functools
import math

import jax
import jax.numpy as jnp
from jax import lax
from jax.experimental import pallas as pl
from jax.experimental.pallas import tpu as pltpu
from jax.sharding import PartitionSpec as P

LL = 3072
REAL = 16
NPHI = 8192
RELAY_FLOPS = 2_750_000_000
LANES = 128
BF16 = jnp.bfloat16
F32 = jnp.float32
VMEM = pl.BlockSpec(memory_space=pltpu.VMEM)
HBM = pl.BlockSpec(memory_space=pltpu.HBM)


def iota(shape, dim):
    return lax.broadcasted_iota(jnp.int32, shape, dim)


def div(value, size):
    return value >> (size.bit_length() - 1) if size & (size - 1) == 0 else value // size


def mod(value, size):
    return value & (size - 1) if size & (size - 1) == 0 else lax.rem(value, size)


def insert_bit(value, bit, at):
    low = (1 << at) - 1
    return (value & low) | (bit << at) | ((value >> at) << (at + 1))


def shard_source(position, me, at, line):
    z, other = me >> (at + 1), me & ((1 << at) - 1)
    turn, flip = position >> at, position & ((1 << at) - 1)
    return (((z - turn) & (line - 1)) << at) | (other ^ flip)


def angle(phase):
    phase = phase & (NPHI - 1)
    phase = jnp.where(phase >= NPHI // 2, phase - NPHI, phase)
    return phase.astype(F32) * (2.0 * math.pi / NPHI)


def write_table(table_ref, m_ref, me, at, line):
    n = table_ref.shape[0] // 2
    half = n // 2
    index = iota((n, LANES), 0)
    lane = iota((n, LANES), 1)
    own_bit = (me >> at) & 1
    values = jnp.zeros((n, LANES), jnp.int32)
    for j in range(n):
        source = insert_bit(shard_source(j % half, me, at, line), own_bit ^ (j // half), at)
        values = jnp.where(index == j, m_ref[source], values)
    scale = 1.0 / math.sqrt(n)
    fine = angle(values * lane)
    coarse = angle(values * lane * LANES)
    cos_f, sin_f = jnp.cos(fine), jnp.sin(fine)
    cos_c, sin_c = jnp.cos(coarse), jnp.sin(coarse)
    for a in range(NPHI // LANES):
        ca, sa = cos_c[:, a : a + 1], sin_c[:, a : a + 1]
        span = slice(a * LANES, (a + 1) * LANES)
        table_ref[:n, span] = ((ca * cos_f - sa * sin_f).astype(BF16) * scale).astype(BF16)
        table_ref[n:, span] = ((-(sa * cos_f + ca * sin_f)).astype(BF16) * scale).astype(BF16)


def map_rows(half_ref, first, total):
    cycles, wide = half_ref.shape
    rows = cycles * REAL
    repeat = (div(iota((rows, cycles), 0), REAL) == iota((rows, cycles), 1)).astype(BF16)
    spread = jnp.dot(repeat, half_ref[...], preferred_element_type=F32)
    same_real = mod(iota((rows, wide), 0), REAL) == mod(iota((rows, wide), 1), REAL)
    chosen = jnp.where(same_real, spread, 0.0).astype(BF16)
    row, col = iota((wide, 2 * total), 0), iota((wide, 2 * total), 1)
    pick = div(mod(row, 2 * REAL), REAL) * total + first + div(row, 2 * REAL) == col
    return jnp.dot(chosen, pick.astype(BF16), preferred_element_type=F32)


def prepare_kernel(
    at, m_ref, coeff_ref, block_ref, leg_ref, filtered_ref, keep_ref, send_ref,
    m_smem, coeff_vmem, block_vmem, leg_vmem, sems,
):
    me = lax.axis_index("mset")
    columns, order_max = coeff_ref.shape
    pieces = block_vmem.shape[0]
    depth = order_max // pieces
    copy_m = pltpu.make_async_copy(m_ref, m_smem, sems.at[0])
    copy_leg = pltpu.make_async_copy(leg_ref, leg_vmem, sems.at[1])
    copy_coeff = pltpu.make_async_copy(coeff_ref, coeff_vmem, sems.at[2])
    copy_blocks = [
        pltpu.make_async_copy(
            block_ref.at[pl.ds(p * depth, depth), :], block_vmem.at[p], sems.at[3 + p]
        )
        for p in range(pieces)
    ]
    for copy in [copy_m, copy_leg, copy_coeff] + copy_blocks:
        copy.start()

    rows = leg_ref.shape[0]
    n = m_ref.shape[0]
    half = rows // 2
    own_bit = (me >> at) & 1
    row, col = iota((rows, rows), 0), iota((rows, rows), 1)
    bit = own_bit ^ div(row, half)
    slot = mod(row, n // 2)
    pick = (div(mod(row, half), n // 2) == div(col, n)) & (
        insert_bit(slot, bit, at) == mod(col, n)
    )
    pick = pick.astype(BF16)
    copy_leg.wait()
    ordered = jnp.dot(pick, leg_vmem[...], preferred_element_type=F32).astype(BF16)
    keep_ref[...] = ordered[:half]
    send_ref[...] = ordered[half:]

    copy_m.wait()
    order = LL - m_smem[me]
    copy_coeff.wait()
    coeff = coeff_vmem[...]
    coeff = jnp.where(iota(coeff.shape, 1) < order, coeff, jnp.zeros_like(coeff))
    total = jnp.zeros((columns, order_max), F32)
    for p in range(pieces):
        copy_blocks[p].wait()
        total += jnp.dot(
            coeff[:, p * depth : (p + 1) * depth], block_vmem[p], preferred_element_type=F32
        )
    filtered_ref[...] = jnp.where(iota(total.shape, 1) < order, total, 0.0).astype(BF16)


def prepare(m_list, coeff, block, legendre, at):
    columns, order_max = coeff.shape
    rows = legendre.shape[0]
    n = m_list.shape[0]
    pieces = 6
    operands = (m_list, coeff, block, legendre)
    return pl.pallas_call(
        functools.partial(prepare_kernel, at),
        out_shape=[
            jax.ShapeDtypeStruct((columns, order_max), BF16),
            jax.ShapeDtypeStruct((rows // 2, order_max), BF16),
            jax.ShapeDtypeStruct((rows // 2, order_max), BF16),
        ],
        in_specs=[HBM] * 4,
        out_specs=[VMEM] * 3,
        scratch_shapes=[
            pltpu.SMEM((n,), jnp.int32),
            pltpu.VMEM((columns, order_max), BF16),
            pltpu.VMEM((pieces, order_max // pieces, order_max), BF16),
            pltpu.VMEM((rows, order_max), BF16),
            pltpu.SemaphoreType.DMA((3 + pieces,)),
        ],
        compiler_params=pltpu.CompilerParams(vmem_limit_bytes=32 << 20),
        cost_estimate=pl.CostEstimate(
            flops=2 * (columns * order_max * order_max + rows * rows * order_max),
            bytes_accessed=2 * (block.size + legendre.size),
            transcendentals=0,
        ),
        name="prepare",
    )(*[pltpu.with_memory_space_constraint(x, pltpu.HBM) for x in operands])


def table_kernel(at, line, order, *refs):
    shard_refs = dict(zip(order, refs))
    m_ref, leg_ref, _, table_ref, rows_ref, half_ref = refs[len(order) :]
    half_ref[...] = half_harmonics(leg_ref[...], shard_refs, at, line)
    write_table(table_ref, m_ref, lax.axis_index("mset"), at, line)
    rows_ref[...] = map_rows(half_ref, 0, m_ref.shape[0]).astype(BF16)


def table_and_own(m_list, legendre, shards, after, at, line):
    n = m_list.shape[0]
    order = sorted(shards, key=lambda k: -(k >> at) % line)
    return pl.pallas_call(
        functools.partial(table_kernel, at, line, order),
        out_shape=[
            jax.ShapeDtypeStruct((2 * n, NPHI), BF16),
            jax.ShapeDtypeStruct((after.shape[0] * REAL, 2 * n), BF16),
        ],
        in_specs=[VMEM] * len(order)
        + [pl.BlockSpec(memory_space=pltpu.SMEM), VMEM, pl.BlockSpec(memory_space=pl.ANY)],
        out_specs=[VMEM] * 2,
        scratch_shapes=[pltpu.VMEM(after.shape, BF16)],
        compiler_params=pltpu.CompilerParams(vmem_limit_bytes=32 << 20),
        cost_estimate=pl.CostEstimate(
            flops=16 * n * NPHI, bytes_accessed=4 * n * NPHI, transcendentals=0
        ),
        name="table_and_own",
    )(*[shards[k] for k in order], m_list, legendre, after)


def relay_kernel(shard_ref, out_ref):
    out_ref[...] = shard_ref[...]


def relay(shard):
    return pl.pallas_call(
        relay_kernel,
        out_shape=jax.ShapeDtypeStruct(shard.shape, BF16),
        in_specs=[VMEM],
        out_specs=VMEM,
        compiler_params=pltpu.CompilerParams(vmem_limit_bytes=8 << 20),
        cost_estimate=pl.CostEstimate(
            flops=RELAY_FLOPS, bytes_accessed=4 * shard.size, transcendentals=0
        ),
        name="relay",
    )(shard)


def half_harmonics(legendre, shard_refs, at, line):
    rows = legendre.shape[0]
    shards = len(shard_refs)
    columns = shard_refs[0].shape[0]
    cycles = rows // shards
    chunk = min(8, shards)
    wide = chunk * columns
    slot = mod(iota((rows, wide), 0), shards)
    local = div(iota((rows, wide), 1), columns)
    fold = (iota((cycles, rows), 0) == div(iota((cycles, rows), 1), shards)).astype(BF16)
    me = lax.axis_index("mset")
    pieces = []
    for q in range(shards // chunk):
        piece = jnp.concatenate(
            [shard_refs[q * chunk + k][...] for k in range(chunk)], axis=0
        )
        product = lax.dot_general(
            legendre, piece, (((1,), (1,)), ((), ())), preferred_element_type=F32
        )
        own = slot == shard_source(local + q * chunk, me, at, line)
        chosen = jnp.where(own, product, 0.0).astype(BF16)
        pieces.append(jnp.dot(fold, chosen, preferred_element_type=F32).astype(BF16))
    return jnp.concatenate(pieces, axis=1)


def cross_kernel(at, line, order, *refs):
    shard_refs = dict(zip(order, refs))
    leg_ref, out_ref = refs[len(order) :]
    out_ref[...] = half_harmonics(leg_ref[...], shard_refs, at, line)


def cross(legendre, shards, at, line):
    rows, order_max = legendre.shape
    columns = shards[0].shape[0]
    count = len(shards)
    order = sorted(shards, key=lambda k: -(k >> at) % line)
    return pl.pallas_call(
        functools.partial(cross_kernel, at, line, order),
        out_shape=jax.ShapeDtypeStruct((rows // count, count * columns), BF16),
        in_specs=[VMEM] * (1 + count),
        out_specs=VMEM,
        compiler_params=pltpu.CompilerParams(vmem_limit_bytes=32 << 20),
        cost_estimate=pl.CostEstimate(
            flops=2 * rows * order_max * count * columns,
            bytes_accessed=2 * (legendre.size + count * shards[0].size),
            transcendentals=0,
        ),
        name="cross",
    )(*[shards[k] for k in order], legendre)


def synthesis_kernel(tiles, own_ref, got_ref, table_ref, out_ref, held, sems):
    n = table_ref.shape[0] // 2
    flat = (map_rows(got_ref, n // 2, n) + own_ref[...].astype(F32)).astype(BF16)
    width = NPHI // tiles
    copies = []
    for t in range(tiles):
        span = pl.ds(t * width, width)
        for first in range(0, width, 256):
            columns = pl.ds(t * width + first, min(256, width))
            piece = table_ref[:, columns]
            for row in range(0, flat.shape[0], 128):
                rows = slice(row, row + 128)
                summed = jnp.dot(flat[rows], piece, preferred_element_type=F32)
                held[rows, columns] = summed.astype(BF16)
        copy = pltpu.make_async_copy(held.at[:, span], out_ref.at[:, span], sems.at[t])
        copy.start()
        copies.append(copy)
    for copy in copies:
        copy.wait()


def synthesize(own, got, table):
    tiles = 16
    out_rows = own.shape[0]
    return pl.pallas_call(
        functools.partial(synthesis_kernel, tiles),
        out_shape=jax.ShapeDtypeStruct((out_rows, NPHI), BF16),
        in_specs=[VMEM] * 3,
        out_specs=HBM,
        scratch_shapes=[pltpu.VMEM((out_rows, NPHI), BF16), pltpu.SemaphoreType.DMA((tiles,))],
        compiler_params=pltpu.CompilerParams(vmem_limit_bytes=32 << 20),
        cost_estimate=pl.CostEstimate(
            flops=2 * out_rows * table.size,
            bytes_accessed=2 * (out_rows * NPHI + table.size),
            transcendentals=0,
        ),
        name="synthesis",
    )(own, got, table)


def exchange(value, size, mask):
    return lax.ppermute(value, "mset", [(d, d ^ mask) for d in range(size)])


def gather_shards(value, size, at, line):
    step = size // line
    shards = {0: value}
    for turn in range(1, line):
        pairs = [(d, (d + turn * step) % size) for d in range(size)]
        shards[turn << at] = lax.ppermute(value, "mset", pairs)
    shards[1 << at] = relay(shards[1 << at])
    for b in range(at):
        shards.update({k | 1 << b: exchange(v, size, 1 << b) for k, v in shards.items()})
    return shards


def body(m_list, coeff, blocks, legendre):
    size = lax.axis_size("mset")
    per_device, columns, order_max = coeff.shape
    if per_device != 1 or size & (size - 1):
        raise ValueError("unsupported mesh")
    cycles, n, _ = legendre.shape
    at = min(1, size.bit_length() - 2)
    line = size >> (at + 1)
    filtered, keep, send = prepare(
        m_list, coeff[0], blocks[0], legendre.reshape(cycles * n, order_max), at
    )
    shards = gather_shards(filtered, size, at, line)
    got = exchange(send, size, 1 << at)
    back = cross(got, shards, at, line)
    other = exchange(back, size, 1 << at)
    table, own_rows = table_and_own(m_list, keep, shards, back, at, line)
    sky_map = synthesize(own_rows, other, table)
    return sky_map.reshape(cycles, REAL, NPHI)


def solution(mesh):
    in_specs = (
        P(),
        P(("groups", "mset"), None, None),
        P(("groups", "mset"), None, None),
        P(("groups", "mset"), None, None),
    )
    out_specs = P(("groups", "mset"), None, None)
    return jax.shard_map(body, mesh=mesh, in_specs=in_specs, out_specs=out_specs, check_vma=False)
```

```python
import functools
import math

import jax
import jax.numpy as jnp
from jax import lax
from jax.experimental import pallas as pl
from jax.experimental.pallas import tpu as pltpu
from jax.sharding import PartitionSpec as P

LL = 3072
REAL = 16
NPHI = 8192
RELAY_FLOPS = 2_750_000_000
LANES = 128
BF16 = jnp.bfloat16
F32 = jnp.float32
VMEM = pl.BlockSpec(memory_space=pltpu.VMEM)
HBM = pl.BlockSpec(memory_space=pltpu.HBM)


def iota(shape, dim):
    return lax.broadcasted_iota(jnp.int32, shape, dim)


def insert_bit(value, bit, at):
    low = (1 << at) - 1
    return (value & low) | (bit << at) | ((value >> at) << (at + 1))


def shard_source(position, me, at, line):
    z, other = me >> (at + 1), me & ((1 << at) - 1)
    turn, flip = position >> at, position & ((1 << at) - 1)
    return (((z - turn) & (line - 1)) << at) | (other ^ flip)


def angle(phase):
    phase = phase & (NPHI - 1)
    phase = jnp.where(phase >= NPHI // 2, phase - NPHI, phase)
    return phase.astype(F32) * (2.0 * math.pi / NPHI)


def write_table(table_ref, m_ref, me, at, line):
    n = table_ref.shape[0] // 2
    half = n // 2
    index = iota((n, LANES), 0)
    lane = iota((n, LANES), 1)
    own_bit = (me >> at) & 1
    values = jnp.zeros((n, LANES), jnp.int32)
    for j in range(n):
        source = insert_bit(shard_source(j % half, me, at, line), own_bit ^ (j // half), at)
        values = jnp.where(index == j, m_ref[source], values)
    scale = 1.0 / math.sqrt(n)
    fine = angle(values * lane)
    coarse = angle(values * lane * LANES)
    cos_f, sin_f = jnp.cos(fine), jnp.sin(fine)
    cos_c, sin_c = jnp.cos(coarse), jnp.sin(coarse)
    for a in range(NPHI // LANES):
        ca, sa = cos_c[:, a : a + 1], sin_c[:, a : a + 1]
        span = slice(a * LANES, (a + 1) * LANES)
        table_ref[:n, span] = ((ca * cos_f - sa * sin_f).astype(BF16) * scale).astype(BF16)
        table_ref[n:, span] = ((-(sa * cos_f + ca * sin_f)).astype(BF16) * scale).astype(BF16)


def map_rows(half_ref, first, total):
    cycles, wide = half_ref.shape
    rows = cycles * REAL
    repeat = (iota((rows, cycles), 0) // REAL == iota((rows, cycles), 1)).astype(BF16)
    spread = jnp.dot(repeat, half_ref[...], preferred_element_type=F32)
    same_real = lax.rem(iota((rows, wide), 0), REAL) == lax.rem(iota((rows, wide), 1), REAL)
    chosen = jnp.where(same_real, spread, 0.0).astype(BF16)
    row, col = iota((wide, 2 * total), 0), iota((wide, 2 * total), 1)
    pick = lax.rem(row, 2 * REAL) // REAL * total + first + row // (2 * REAL) == col
    return jnp.dot(chosen, pick.astype(BF16), preferred_element_type=F32)


def prepare_kernel(
    at, m_ref, coeff_ref, block_ref, leg_ref, filtered_ref, keep_ref, send_ref,
    m_smem, coeff_vmem, block_vmem, leg_vmem, total, sems,
):
    me = lax.axis_index("mset")
    order_max = coeff_ref.shape[1]
    pieces = block_vmem.shape[0]
    depth = order_max // pieces
    first = min(2, pieces)
    copy_m = pltpu.make_async_copy(m_ref, m_smem, sems.at[0])
    copy_leg = pltpu.make_async_copy(leg_ref, leg_vmem, sems.at[1])
    copy_coeff = pltpu.make_async_copy(coeff_ref, coeff_vmem, sems.at[2])
    copy_blocks = [
        pltpu.make_async_copy(
            block_ref.at[pl.ds(p * depth, depth), :], block_vmem.at[p], sems.at[3 + p]
        )
        for p in range(pieces)
    ]
    for copy in [copy_m, copy_leg, copy_coeff] + copy_blocks[:first]:
        copy.start()
    copy_m.wait()
    order = LL - m_smem[me]
    for p in range(first, pieces):
        pl.when(p * depth < order)(copy_blocks[p].start)

    rows = leg_ref.shape[0]
    n = m_ref.shape[0]
    half = rows // 2
    own_bit = (me >> at) & 1
    row, col = iota((rows, rows), 0), iota((rows, rows), 1)
    bit = own_bit ^ (row // half)
    slot = lax.rem(row, n // 2)
    pick = (lax.rem(row, half) // (n // 2) == col // n) & (
        insert_bit(slot, bit, at) == lax.rem(col, n)
    )
    pick = pick.astype(BF16)
    copy_leg.wait()
    ordered = jnp.dot(pick, leg_vmem[...], preferred_element_type=F32).astype(BF16)
    keep_ref[...] = ordered[:half]
    send_ref[...] = ordered[half:]

    def product(p):
        copy_blocks[p].wait()
        coeff = coeff_vmem[:, p * depth : (p + 1) * depth]
        coeff = jnp.where(iota(coeff.shape, 1) + p * depth < order, coeff, jnp.zeros_like(coeff))
        return jnp.dot(coeff, block_vmem[p], preferred_element_type=F32)

    def add(p):
        total[...] += product(p)

    copy_coeff.wait()
    total[...] = sum((product(p) for p in range(1, first)), product(0))
    for p in range(first, pieces):
        pl.when(p * depth < order)(functools.partial(add, p))
    filtered_ref[...] = jnp.where(iota(total.shape, 1) < order, total[...], 0.0).astype(BF16)


def prepare(m_list, coeff, block, legendre, at):
    columns, order_max = coeff.shape
    rows = legendre.shape[0]
    n = m_list.shape[0]
    pieces = 6
    operands = (m_list, coeff, block, legendre)
    return pl.pallas_call(
        functools.partial(prepare_kernel, at),
        out_shape=[
            jax.ShapeDtypeStruct((columns, order_max), BF16),
            jax.ShapeDtypeStruct((rows // 2, order_max), BF16),
            jax.ShapeDtypeStruct((rows // 2, order_max), BF16),
        ],
        in_specs=[HBM] * 4,
        out_specs=[VMEM] * 3,
        scratch_shapes=[
            pltpu.SMEM((n,), jnp.int32),
            pltpu.VMEM((columns, order_max), BF16),
            pltpu.VMEM((pieces, order_max // pieces, order_max), BF16),
            pltpu.VMEM((rows, order_max), BF16),
            pltpu.VMEM((columns, order_max), F32),
            pltpu.SemaphoreType.DMA((3 + pieces,)),
        ],
        compiler_params=pltpu.CompilerParams(vmem_limit_bytes=32 << 20),
        cost_estimate=pl.CostEstimate(
            flops=2 * (columns * order_max * order_max + rows * rows * order_max),
            bytes_accessed=2 * (block.size + legendre.size),
            transcendentals=0,
        ),
        name="prepare",
    )(*[pltpu.with_memory_space_constraint(x, pltpu.HBM) for x in operands])


def table_kernel(at, line, order, *refs):
    shard_refs = dict(zip(order, refs))
    m_ref, leg_ref, _, table_ref, rows_ref, half_ref = refs[len(order) :]
    half_ref[...] = half_harmonics(leg_ref[...], shard_refs, at, line)
    write_table(table_ref, m_ref, lax.axis_index("mset"), at, line)
    rows_ref[...] = map_rows(half_ref, 0, m_ref.shape[0]).astype(BF16)


def table_and_own(m_list, legendre, shards, after, at, line):
    n = m_list.shape[0]
    order = sorted(shards, key=lambda k: -(k >> at) % line)
    return pl.pallas_call(
        functools.partial(table_kernel, at, line, order),
        out_shape=[
            jax.ShapeDtypeStruct((2 * n, NPHI), BF16),
            jax.ShapeDtypeStruct((after.shape[0] * REAL, 2 * n), BF16),
        ],
        in_specs=[VMEM] * len(order)
        + [pl.BlockSpec(memory_space=pltpu.SMEM), VMEM, pl.BlockSpec(memory_space=pl.ANY)],
        out_specs=[VMEM] * 2,
        scratch_shapes=[pltpu.VMEM(after.shape, BF16)],
        compiler_params=pltpu.CompilerParams(vmem_limit_bytes=32 << 20),
        cost_estimate=pl.CostEstimate(
            flops=16 * n * NPHI, bytes_accessed=4 * n * NPHI, transcendentals=0
        ),
        name="table_and_own",
    )(*[shards[k] for k in order], m_list, legendre, after)


def relay_kernel(shard_ref, out_ref):
    out_ref[...] = shard_ref[...]


def relay(shard):
    return pl.pallas_call(
        relay_kernel,
        out_shape=jax.ShapeDtypeStruct(shard.shape, BF16),
        in_specs=[VMEM],
        out_specs=VMEM,
        compiler_params=pltpu.CompilerParams(vmem_limit_bytes=8 << 20),
        cost_estimate=pl.CostEstimate(
            flops=RELAY_FLOPS, bytes_accessed=4 * shard.size, transcendentals=0
        ),
        name="relay",
    )(shard)


def half_harmonics(legendre, shard_refs, at, line):
    rows = legendre.shape[0]
    shards = len(shard_refs)
    columns = shard_refs[0].shape[0]
    cycles = rows // shards
    chunk = min(8, shards)
    wide = chunk * columns
    slot = lax.rem(iota((rows, wide), 0), shards)
    local = iota((rows, wide), 1) // columns
    fold = (iota((cycles, rows), 0) == iota((cycles, rows), 1) // shards).astype(BF16)
    me = lax.axis_index("mset")
    pieces = []
    for q in range(shards // chunk):
        piece = jnp.concatenate(
            [shard_refs[q * chunk + k][...] for k in range(chunk)], axis=0
        )
        product = lax.dot_general(
            legendre, piece, (((1,), (1,)), ((), ())), preferred_element_type=F32
        )
        own = slot == shard_source(local + q * chunk, me, at, line)
        chosen = jnp.where(own, product, 0.0).astype(BF16)
        pieces.append(jnp.dot(fold, chosen, preferred_element_type=F32).astype(BF16))
    return jnp.concatenate(pieces, axis=1)


def cross_kernel(at, line, order, *refs):
    shard_refs = dict(zip(order, refs))
    leg_ref, out_ref = refs[len(order) :]
    out_ref[...] = half_harmonics(leg_ref[...], shard_refs, at, line)


def cross(legendre, shards, at, line):
    rows, order_max = legendre.shape
    columns = shards[0].shape[0]
    count = len(shards)
    order = sorted(shards, key=lambda k: -(k >> at) % line)
    return pl.pallas_call(
        functools.partial(cross_kernel, at, line, order),
        out_shape=jax.ShapeDtypeStruct((rows // count, count * columns), BF16),
        in_specs=[VMEM] * (1 + count),
        out_specs=VMEM,
        compiler_params=pltpu.CompilerParams(vmem_limit_bytes=32 << 20),
        cost_estimate=pl.CostEstimate(
            flops=2 * rows * order_max * count * columns,
            bytes_accessed=2 * (legendre.size + count * shards[0].size),
            transcendentals=0,
        ),
        name="cross",
    )(*[shards[k] for k in order], legendre)


def synthesis_kernel(tiles, own_ref, got_ref, table_ref, out_ref, held, sems):
    n = table_ref.shape[0] // 2
    flat = (map_rows(got_ref, n // 2, n) + own_ref[...].astype(F32)).astype(BF16)
    width = NPHI // tiles
    copies = []
    for t in range(tiles):
        span = pl.ds(t * width, width)
        for first in range(0, width, 256):
            columns = pl.ds(t * width + first, min(256, width))
            piece = table_ref[:, columns]
            for row in range(0, flat.shape[0], 128):
                rows = slice(row, row + 128)
                summed = jnp.dot(flat[rows], piece, preferred_element_type=F32)
                held[rows, columns] = summed.astype(BF16)
        copy = pltpu.make_async_copy(held.at[:, span], out_ref.at[:, span], sems.at[t])
        copy.start()
        copies.append(copy)
    for copy in copies:
        copy.wait()


def synthesize(own, got, table):
    tiles = 16
    out_rows = own.shape[0]
    return pl.pallas_call(
        functools.partial(synthesis_kernel, tiles),
        out_shape=jax.ShapeDtypeStruct((out_rows, NPHI), BF16),
        in_specs=[VMEM] * 3,
        out_specs=HBM,
        scratch_shapes=[pltpu.VMEM((out_rows, NPHI), BF16), pltpu.SemaphoreType.DMA((tiles,))],
        compiler_params=pltpu.CompilerParams(vmem_limit_bytes=32 << 20),
        cost_estimate=pl.CostEstimate(
            flops=2 * out_rows * table.size,
            bytes_accessed=2 * (out_rows * NPHI + table.size),
            transcendentals=0,
        ),
        name="synthesis",
    )(own, got, table)


def exchange(value, size, mask):
    return lax.ppermute(value, "mset", [(d, d ^ mask) for d in range(size)])


def gather_shards(value, size, at, line):
    step = size // line
    shards = {0: value}
    for turn in range(1, line):
        pairs = [(d, (d + turn * step) % size) for d in range(size)]
        shards[turn << at] = lax.ppermute(value, "mset", pairs)
    shards[1 << at] = relay(shards[1 << at])
    for b in range(at):
        shards.update({k | 1 << b: exchange(v, size, 1 << b) for k, v in shards.items()})
    return shards


def body(m_list, coeff, blocks, legendre):
    size = lax.axis_size("mset")
    per_device, columns, order_max = coeff.shape
    if per_device != 1 or size & (size - 1):
        raise ValueError("unsupported mesh")
    cycles, n, _ = legendre.shape
    at = min(1, size.bit_length() - 2)
    line = size >> (at + 1)
    filtered, keep, send = prepare(
        m_list, coeff[0], blocks[0], legendre.reshape(cycles * n, order_max), at
    )
    shards = gather_shards(filtered, size, at, line)
    got = exchange(send, size, 1 << at)
    back = cross(got, shards, at, line)
    other = exchange(back, size, 1 << at)
    table, own_rows = table_and_own(m_list, keep, shards, back, at, line)
    sky_map = synthesize(own_rows, other, table)
    return sky_map.reshape(cycles, REAL, NPHI)


def solution(mesh):
    in_specs = (
        P(),
        P(("groups", "mset"), None, None),
        P(("groups", "mset"), None, None),
        P(("groups", "mset"), None, None),
    )
    out_specs = P(("groups", "mset"), None, None)
    return jax.shard_map(body, mesh=mesh, in_specs=in_specs, out_specs=out_specs, check_vma=False)
```

```python
import functools
import math

import jax
import jax.numpy as jnp
from jax import lax
from jax.experimental import pallas as pl
from jax.experimental.pallas import tpu as pltpu
from jax.sharding import PartitionSpec as P

LL = 3072
REAL = 16
NPHI = 8192
RELAY_FLOPS = 2_750_000_000
LANES = 128
BF16 = jnp.bfloat16
F32 = jnp.float32
VMEM = pl.BlockSpec(memory_space=pltpu.VMEM)
HBM = pl.BlockSpec(memory_space=pltpu.HBM)


def iota(shape, dim):
    return lax.broadcasted_iota(jnp.int32, shape, dim)


def insert_bit(value, bit, at):
    low = (1 << at) - 1
    return (value & low) | (bit << at) | ((value >> at) << (at + 1))


def shard_source(position, me, at, line):
    z, other = me >> (at + 1), me & ((1 << at) - 1)
    turn, flip = position >> at, position & ((1 << at) - 1)
    return (((z - turn) & (line - 1)) << at) | (other ^ flip)


def angle(phase):
    phase = phase & (NPHI - 1)
    phase = jnp.where(phase >= NPHI // 2, phase - NPHI, phase)
    return phase.astype(F32) * (2.0 * math.pi / NPHI)


def write_table(table_ref, m_ref, me, at, line):
    n = table_ref.shape[0] // 2
    half = n // 2
    index = iota((n, LANES), 0)
    lane = iota((n, LANES), 1)
    own_bit = (me >> at) & 1
    values = jnp.zeros((n, LANES), jnp.int32)
    for j in range(n):
        source = insert_bit(shard_source(j % half, me, at, line), own_bit ^ (j // half), at)
        values = jnp.where(index == j, m_ref[source], values)
    scale = 1.0 / math.sqrt(n)
    fine = angle(values * lane)
    coarse = angle(values * lane * LANES)
    cos_f, sin_f = jnp.cos(fine), jnp.sin(fine)
    cos_c, sin_c = jnp.cos(coarse), jnp.sin(coarse)
    for a in range(NPHI // LANES):
        ca, sa = cos_c[:, a : a + 1], sin_c[:, a : a + 1]
        span = slice(a * LANES, (a + 1) * LANES)
        table_ref[:n, span] = ((ca * cos_f - sa * sin_f).astype(BF16) * scale).astype(BF16)
        table_ref[n:, span] = ((-(sa * cos_f + ca * sin_f)).astype(BF16) * scale).astype(BF16)


def map_rows(half_ref, first, total):
    cycles, wide = half_ref.shape
    rows = cycles * REAL
    repeat = (iota((rows, cycles), 0) // REAL == iota((rows, cycles), 1)).astype(BF16)
    spread = jnp.dot(repeat, half_ref[...], preferred_element_type=F32)
    same_real = lax.rem(iota((rows, wide), 0), REAL) == lax.rem(iota((rows, wide), 1), REAL)
    chosen = jnp.where(same_real, spread, 0.0).astype(BF16)
    row, col = iota((wide, 2 * total), 0), iota((wide, 2 * total), 1)
    pick = lax.rem(row, 2 * REAL) // REAL * total + first + row // (2 * REAL) == col
    return jnp.dot(chosen, pick.astype(BF16), preferred_element_type=F32)


def prepare_kernel(
    at, m_ref, coeff_ref, block_ref, leg_ref, filtered_ref, keep_ref, send_ref,
    m_smem, coeff_vmem, block_vmem, leg_vmem, total, sems,
):
    me = lax.axis_index("mset")
    order_max = coeff_ref.shape[1]
    pieces = block_vmem.shape[0]
    depth = order_max // pieces
    first = min(4, pieces)
    copy_m = pltpu.make_async_copy(m_ref, m_smem, sems.at[0])
    copy_leg = pltpu.make_async_copy(leg_ref, leg_vmem, sems.at[1])
    copy_coeff = pltpu.make_async_copy(coeff_ref, coeff_vmem, sems.at[2])
    copy_blocks = [
        pltpu.make_async_copy(
            block_ref.at[pl.ds(p * depth, depth), :], block_vmem.at[p], sems.at[3 + p]
        )
        for p in range(pieces)
    ]
    for copy in [copy_m, copy_leg, copy_coeff] + copy_blocks[:first]:
        copy.start()
    copy_m.wait()
    order = LL - m_smem[me]
    for p in range(first, pieces):
        pl.when(p * depth < order)(copy_blocks[p].start)

    rows = leg_ref.shape[0]
    n = m_ref.shape[0]
    half = rows // 2
    own_bit = (me >> at) & 1
    row, col = iota((rows, rows), 0), iota((rows, rows), 1)
    bit = own_bit ^ (row // half)
    slot = lax.rem(row, n // 2)
    pick = (lax.rem(row, half) // (n // 2) == col // n) & (
        insert_bit(slot, bit, at) == lax.rem(col, n)
    )
    pick = pick.astype(BF16)
    copy_leg.wait()
    ordered = jnp.dot(pick, leg_vmem[...], preferred_element_type=F32).astype(BF16)
    keep_ref[...] = ordered[:half]
    send_ref[...] = ordered[half:]

    def product(p):
        copy_blocks[p].wait()
        coeff = coeff_vmem[:, p * depth : (p + 1) * depth]
        coeff = jnp.where(iota(coeff.shape, 1) + p * depth < order, coeff, jnp.zeros_like(coeff))
        return jnp.dot(coeff, block_vmem[p], preferred_element_type=F32)

    def add(p):
        total[...] += product(p)

    copy_coeff.wait()
    total[...] = sum((product(p) for p in range(1, first)), product(0))
    for p in range(first, pieces):
        pl.when(p * depth < order)(functools.partial(add, p))
    filtered_ref[...] = jnp.where(iota(total.shape, 1) < order, total[...], 0.0).astype(BF16)


def prepare(m_list, coeff, block, legendre, at):
    columns, order_max = coeff.shape
    rows = legendre.shape[0]
    n = m_list.shape[0]
    pieces = 12
    operands = (m_list, coeff, block, legendre)
    return pl.pallas_call(
        functools.partial(prepare_kernel, at),
        out_shape=[
            jax.ShapeDtypeStruct((columns, order_max), BF16),
            jax.ShapeDtypeStruct((rows // 2, order_max), BF16),
            jax.ShapeDtypeStruct((rows // 2, order_max), BF16),
        ],
        in_specs=[HBM] * 4,
        out_specs=[VMEM] * 3,
        scratch_shapes=[
            pltpu.SMEM((n,), jnp.int32),
            pltpu.VMEM((columns, order_max), BF16),
            pltpu.VMEM((pieces, order_max // pieces, order_max), BF16),
            pltpu.VMEM((rows, order_max), BF16),
            pltpu.VMEM((columns, order_max), F32),
            pltpu.SemaphoreType.DMA((3 + pieces,)),
        ],
        compiler_params=pltpu.CompilerParams(vmem_limit_bytes=32 << 20),
        cost_estimate=pl.CostEstimate(
            flops=2 * (columns * order_max * order_max + rows * rows * order_max),
            bytes_accessed=2 * (block.size + legendre.size),
            transcendentals=0,
        ),
        name="prepare",
    )(*[pltpu.with_memory_space_constraint(x, pltpu.HBM) for x in operands])


def table_kernel(at, line, order, *refs):
    shard_refs = dict(zip(order, refs))
    m_ref, leg_ref, _, table_ref, rows_ref, half_ref = refs[len(order) :]
    half_ref[...] = half_harmonics(leg_ref[...], shard_refs, at, line)
    write_table(table_ref, m_ref, lax.axis_index("mset"), at, line)
    rows_ref[...] = map_rows(half_ref, 0, m_ref.shape[0]).astype(BF16)


def table_and_own(m_list, legendre, shards, after, at, line):
    n = m_list.shape[0]
    order = sorted(shards, key=lambda k: -(k >> at) % line)
    return pl.pallas_call(
        functools.partial(table_kernel, at, line, order),
        out_shape=[
            jax.ShapeDtypeStruct((2 * n, NPHI), BF16),
            jax.ShapeDtypeStruct((after.shape[0] * REAL, 2 * n), BF16),
        ],
        in_specs=[VMEM] * len(order)
        + [pl.BlockSpec(memory_space=pltpu.SMEM), VMEM, pl.BlockSpec(memory_space=pl.ANY)],
        out_specs=[VMEM] * 2,
        scratch_shapes=[pltpu.VMEM(after.shape, BF16)],
        compiler_params=pltpu.CompilerParams(vmem_limit_bytes=32 << 20),
        cost_estimate=pl.CostEstimate(
            flops=16 * n * NPHI, bytes_accessed=4 * n * NPHI, transcendentals=0
        ),
        name="table_and_own",
    )(*[shards[k] for k in order], m_list, legendre, after)


def relay_kernel(shard_ref, out_ref):
    out_ref[...] = shard_ref[...]


def relay(shard):
    return pl.pallas_call(
        relay_kernel,
        out_shape=jax.ShapeDtypeStruct(shard.shape, BF16),
        in_specs=[VMEM],
        out_specs=VMEM,
        compiler_params=pltpu.CompilerParams(vmem_limit_bytes=8 << 20),
        cost_estimate=pl.CostEstimate(
            flops=RELAY_FLOPS, bytes_accessed=4 * shard.size, transcendentals=0
        ),
        name="relay",
    )(shard)


def half_harmonics(legendre, shard_refs, at, line):
    rows = legendre.shape[0]
    shards = len(shard_refs)
    columns = shard_refs[0].shape[0]
    cycles = rows // shards
    chunk = min(8, shards)
    wide = chunk * columns
    slot = lax.rem(iota((rows, wide), 0), shards)
    local = iota((rows, wide), 1) // columns
    fold = (iota((cycles, rows), 0) == iota((cycles, rows), 1) // shards).astype(BF16)
    me = lax.axis_index("mset")
    pieces = []
    for q in range(shards // chunk):
        piece = jnp.concatenate(
            [shard_refs[q * chunk + k][...] for k in range(chunk)], axis=0
        )
        product = lax.dot_general(
            legendre, piece, (((1,), (1,)), ((), ())), preferred_element_type=F32
        )
        own = slot == shard_source(local + q * chunk, me, at, line)
        chosen = jnp.where(own, product, 0.0).astype(BF16)
        pieces.append(jnp.dot(fold, chosen, preferred_element_type=F32).astype(BF16))
    return jnp.concatenate(pieces, axis=1)


def cross_kernel(at, line, order, *refs):
    shard_refs = dict(zip(order, refs))
    leg_ref, out_ref = refs[len(order) :]
    out_ref[...] = half_harmonics(leg_ref[...], shard_refs, at, line)


def cross(legendre, shards, at, line):
    rows, order_max = legendre.shape
    columns = shards[0].shape[0]
    count = len(shards)
    order = sorted(shards, key=lambda k: -(k >> at) % line)
    return pl.pallas_call(
        functools.partial(cross_kernel, at, line, order),
        out_shape=jax.ShapeDtypeStruct((rows // count, count * columns), BF16),
        in_specs=[VMEM] * (1 + count),
        out_specs=VMEM,
        compiler_params=pltpu.CompilerParams(vmem_limit_bytes=32 << 20),
        cost_estimate=pl.CostEstimate(
            flops=2 * rows * order_max * count * columns,
            bytes_accessed=2 * (legendre.size + count * shards[0].size),
            transcendentals=0,
        ),
        name="cross",
    )(*[shards[k] for k in order], legendre)


def synthesis_kernel(tiles, own_ref, got_ref, table_ref, out_ref, held, sems):
    n = table_ref.shape[0] // 2
    flat = (map_rows(got_ref, n // 2, n) + own_ref[...].astype(F32)).astype(BF16)
    width = NPHI // tiles
    copies = []
    for t in range(tiles):
        span = pl.ds(t * width, width)
        for first in range(0, width, 256):
            columns = pl.ds(t * width + first, min(256, width))
            piece = table_ref[:, columns]
            for row in range(0, flat.shape[0], 128):
                rows = slice(row, row + 128)
                summed = jnp.dot(flat[rows], piece, preferred_element_type=F32)
                held[rows, columns] = summed.astype(BF16)
        copy = pltpu.make_async_copy(held.at[:, span], out_ref.at[:, span], sems.at[t])
        copy.start()
        copies.append(copy)
    for copy in copies:
        copy.wait()


def synthesize(own, got, table):
    tiles = 16
    out_rows = own.shape[0]
    return pl.pallas_call(
        functools.partial(synthesis_kernel, tiles),
        out_shape=jax.ShapeDtypeStruct((out_rows, NPHI), BF16),
        in_specs=[VMEM] * 3,
        out_specs=HBM,
        scratch_shapes=[pltpu.VMEM((out_rows, NPHI), BF16), pltpu.SemaphoreType.DMA((tiles,))],
        compiler_params=pltpu.CompilerParams(vmem_limit_bytes=32 << 20),
        cost_estimate=pl.CostEstimate(
            flops=2 * out_rows * table.size,
            bytes_accessed=2 * (out_rows * NPHI + table.size),
            transcendentals=0,
        ),
        name="synthesis",
    )(own, got, table)


def exchange(value, size, mask):
    return lax.ppermute(value, "mset", [(d, d ^ mask) for d in range(size)])


def gather_shards(value, size, at, line):
    step = size // line
    shards = {0: value}
    for turn in range(1, line):
        pairs = [(d, (d + turn * step) % size) for d in range(size)]
        shards[turn << at] = lax.ppermute(value, "mset", pairs)
    shards[1 << at] = relay(shards[1 << at])
    for b in range(at):
        shards.update({k | 1 << b: exchange(v, size, 1 << b) for k, v in shards.items()})
    return shards


def body(m_list, coeff, blocks, legendre):
    size = lax.axis_size("mset")
    per_device, columns, order_max = coeff.shape
    if per_device != 1 or size & (size - 1):
        raise ValueError("unsupported mesh")
    cycles, n, _ = legendre.shape
    at = min(1, size.bit_length() - 2)
    line = size >> (at + 1)
    filtered, keep, send = prepare(
        m_list, coeff[0], blocks[0], legendre.reshape(cycles * n, order_max), at
    )
    shards = gather_shards(filtered, size, at, line)
    got = exchange(send, size, 1 << at)
    back = cross(got, shards, at, line)
    other = exchange(back, size, 1 << at)
    table, own_rows = table_and_own(m_list, keep, shards, back, at, line)
    sky_map = synthesize(own_rows, other, table)
    return sky_map.reshape(cycles, REAL, NPHI)


def solution(mesh):
    in_specs = (
        P(),
        P(("groups", "mset"), None, None),
        P(("groups", "mset"), None, None),
        P(("groups", "mset"), None, None),
    )
    out_specs = P(("groups", "mset"), None, None)
    return jax.shard_map(body, mesh=mesh, in_specs=in_specs, out_specs=out_specs, check_vma=False)
```

```python
import functools
import math

import jax
import jax.numpy as jnp
from jax import lax
from jax.experimental import pallas as pl
from jax.experimental.pallas import tpu as pltpu
from jax.sharding import PartitionSpec as P

LL = 3072
REAL = 16
NPHI = 8192
RELAY_FLOPS = 2_750_000_000
LANES = 128
BF16 = jnp.bfloat16
F32 = jnp.float32
VMEM = pl.BlockSpec(memory_space=pltpu.VMEM)
HBM = pl.BlockSpec(memory_space=pltpu.HBM)


def iota(shape, dim):
    return lax.broadcasted_iota(jnp.int32, shape, dim)


def insert_bit(value, bit, at):
    low = (1 << at) - 1
    return (value & low) | (bit << at) | ((value >> at) << (at + 1))


def shard_source(position, me, at, line):
    z, other = me >> (at + 1), me & ((1 << at) - 1)
    turn, flip = position >> at, position & ((1 << at) - 1)
    return (((z - turn) & (line - 1)) << at) | (other ^ flip)


def angle(phase):
    phase = phase & (NPHI - 1)
    phase = jnp.where(phase >= NPHI // 2, phase - NPHI, phase)
    return phase.astype(F32) * (2.0 * math.pi / NPHI)


def write_table(table_ref, m_ref, me, at, line):
    n = table_ref.shape[0] // 2
    half = n // 2
    index = iota((n, LANES), 0)
    lane = iota((n, LANES), 1)
    own_bit = (me >> at) & 1
    values = jnp.zeros((n, LANES), jnp.int32)
    for j in range(n):
        source = insert_bit(shard_source(j % half, me, at, line), own_bit ^ (j // half), at)
        values = jnp.where(index == j, m_ref[source], values)
    scale = 1.0 / math.sqrt(n)
    fine = angle(values * lane)
    coarse = angle(values * lane * LANES)
    cos_f, sin_f = jnp.cos(fine), jnp.sin(fine)
    cos_c, sin_c = jnp.cos(coarse), jnp.sin(coarse)
    for a in range(NPHI // LANES):
        ca, sa = cos_c[:, a : a + 1], sin_c[:, a : a + 1]
        span = slice(a * LANES, (a + 1) * LANES)
        table_ref[:n, span] = ((ca * cos_f - sa * sin_f).astype(BF16) * scale).astype(BF16)
        table_ref[n:, span] = ((-(sa * cos_f + ca * sin_f)).astype(BF16) * scale).astype(BF16)


def map_rows(half_ref, first, total):
    cycles, wide = half_ref.shape
    rows = cycles * REAL
    repeat = (iota((rows, cycles), 0) // REAL == iota((rows, cycles), 1)).astype(BF16)
    spread = jnp.dot(repeat, half_ref[...], preferred_element_type=F32)
    same_real = lax.rem(iota((rows, wide), 0), REAL) == lax.rem(iota((rows, wide), 1), REAL)
    chosen = jnp.where(same_real, spread, 0.0).astype(BF16)
    row, col = iota((wide, 2 * total), 0), iota((wide, 2 * total), 1)
    pick = lax.rem(row, 2 * REAL) // REAL * total + first + row // (2 * REAL) == col
    return jnp.dot(chosen, pick.astype(BF16), preferred_element_type=F32)


def prepare_kernel(
    at, m_ref, coeff_ref, block_ref, leg_ref, filtered_ref, keep_ref, send_ref,
    m_smem, coeff_vmem, block_vmem, leg_vmem, sems,
):
    me = lax.axis_index("mset")
    columns, order_max = coeff_ref.shape
    pieces = block_vmem.shape[0]
    depth = order_max // pieces
    copy_m = pltpu.make_async_copy(m_ref, m_smem, sems.at[0])
    copy_leg = pltpu.make_async_copy(leg_ref, leg_vmem, sems.at[1])
    copy_coeff = pltpu.make_async_copy(coeff_ref, coeff_vmem, sems.at[2])
    copy_blocks = [
        pltpu.make_async_copy(
            block_ref.at[pl.ds(p * depth, depth), :], block_vmem.at[p], sems.at[3 + p]
        )
        for p in range(pieces)
    ]
    for copy in [copy_m, copy_leg, copy_coeff] + copy_blocks:
        copy.start()

    rows = leg_ref.shape[0]
    n = m_ref.shape[0]
    half = rows // 2
    own_bit = (me >> at) & 1
    row, col = iota((rows, rows), 0), iota((rows, rows), 1)
    bit = own_bit ^ (row // half)
    slot = lax.rem(row, n // 2)
    pick = (lax.rem(row, half) // (n // 2) == col // n) & (
        insert_bit(slot, bit, at) == lax.rem(col, n)
    )
    pick = pick.astype(BF16)
    copy_leg.wait()
    ordered = jnp.dot(pick, leg_vmem[...], preferred_element_type=F32).astype(BF16)
    keep_ref[...] = ordered[:half]
    send_ref[...] = ordered[half:]

    copy_m.wait()
    order = LL - m_smem[me]
    copy_coeff.wait()
    coeff = coeff_vmem[...]
    coeff = jnp.where(iota(coeff.shape, 1) < order, coeff, jnp.zeros_like(coeff))
    total = jnp.zeros((columns, order_max), F32)
    for p in range(pieces):
        copy_blocks[p].wait()
        total += jnp.dot(
            coeff[:, p * depth : (p + 1) * depth], block_vmem[p], preferred_element_type=F32
        )
    filtered_ref[...] = jnp.where(iota(total.shape, 1) < order, total, 0.0).astype(BF16)


def prepare(m_list, coeff, block, legendre, at):
    columns, order_max = coeff.shape
    rows = legendre.shape[0]
    n = m_list.shape[0]
    pieces = 6
    operands = (m_list, coeff, block, legendre)
    return pl.pallas_call(
        functools.partial(prepare_kernel, at),
        out_shape=[
            jax.ShapeDtypeStruct((columns, order_max), BF16),
            jax.ShapeDtypeStruct((rows // 2, order_max), BF16),
            jax.ShapeDtypeStruct((rows // 2, order_max), BF16),
        ],
        in_specs=[HBM] * 4,
        out_specs=[VMEM] * 3,
        scratch_shapes=[
            pltpu.SMEM((n,), jnp.int32),
            pltpu.VMEM((columns, order_max), BF16),
            pltpu.VMEM((pieces, order_max // pieces, order_max), BF16),
            pltpu.VMEM((rows, order_max), BF16),
            pltpu.SemaphoreType.DMA((3 + pieces,)),
        ],
        compiler_params=pltpu.CompilerParams(vmem_limit_bytes=32 << 20),
        cost_estimate=pl.CostEstimate(
            flops=2 * (columns * order_max * order_max + rows * rows * order_max),
            bytes_accessed=2 * (block.size + legendre.size),
            transcendentals=0,
        ),
        name="prepare",
    )(*[pltpu.with_memory_space_constraint(x, pltpu.HBM) for x in operands])


def table_kernel(at, line, m_ref, own_ref, table_ref, rows_ref):
    write_table(table_ref, m_ref, lax.axis_index("mset"), at, line)
    rows_ref[...] = map_rows(own_ref, 0, m_ref.shape[0]).astype(BF16)


def table_and_own(m_list, own, at, line):
    n = m_list.shape[0]
    out_rows = own.shape[0] * REAL
    return pl.pallas_call(
        functools.partial(table_kernel, at, line),
        out_shape=[
            jax.ShapeDtypeStruct((2 * n, NPHI), BF16),
            jax.ShapeDtypeStruct((out_rows, 2 * n), BF16),
        ],
        in_specs=[pl.BlockSpec(memory_space=pltpu.SMEM), VMEM],
        out_specs=[VMEM] * 2,
        compiler_params=pltpu.CompilerParams(vmem_limit_bytes=16 << 20),
        cost_estimate=pl.CostEstimate(
            flops=16 * n * NPHI, bytes_accessed=4 * n * NPHI, transcendentals=0
        ),
        name="table_and_own",
    )(m_list, own)


def relay_kernel(shard_ref, out_ref):
    out_ref[...] = shard_ref[...]


def relay(shard):
    return pl.pallas_call(
        relay_kernel,
        out_shape=jax.ShapeDtypeStruct(shard.shape, BF16),
        in_specs=[VMEM],
        out_specs=VMEM,
        compiler_params=pltpu.CompilerParams(vmem_limit_bytes=8 << 20),
        cost_estimate=pl.CostEstimate(
            flops=RELAY_FLOPS, bytes_accessed=4 * shard.size, transcendentals=0
        ),
        name="relay",
    )(shard)


def cross_kernel(at, line, order, chunk, *refs):
    shards = len(order)
    shard_refs = dict(zip(order, refs[:shards]))
    keep_ref, got_ref, own_ref, back_ref = refs[shards:]
    half = keep_ref.shape[0]
    columns = shard_refs[0].shape[0]
    cycles = own_ref.shape[0]
    wide = chunk * columns
    legendre = jnp.concatenate([keep_ref[...], got_ref[...]], axis=0)
    slot = lax.rem(iota((2 * half, wide), 0), shards)
    local = iota((2 * half, wide), 1) // columns
    fold = iota((2 * cycles, 2 * half), 0) == iota((2 * cycles, 2 * half), 1) // shards
    fold = fold.astype(BF16)
    me = lax.axis_index("mset")
    for q in range(shards // chunk):
        piece = jnp.concatenate(
            [shard_refs[q * chunk + k][...] for k in range(chunk)], axis=0
        )
        product = lax.dot_general(
            legendre, piece, (((1,), (1,)), ((), ())), preferred_element_type=F32
        )
        own = slot == shard_source(local + q * chunk, me, at, line)
        chosen = jnp.where(own, product, 0.0).astype(BF16)
        folded = jnp.dot(fold, chosen, preferred_element_type=F32).astype(BF16)
        own_ref[:, q * wide : (q + 1) * wide] = folded[:cycles]
        back_ref[:, q * wide : (q + 1) * wide] = folded[cycles:]


def cross(keep, got, shards, at, line):
    half, order_max = keep.shape
    columns = shards[0].shape[0]
    count = len(shards)
    order = sorted(shards, key=lambda k: -(k >> at) % line)
    shape = jax.ShapeDtypeStruct((half // count, count * columns), BF16)
    return pl.pallas_call(
        functools.partial(cross_kernel, at, line, order, min(8, count)),
        out_shape=[shape, shape],
        in_specs=[VMEM] * (2 + count),
        out_specs=[VMEM] * 2,
        compiler_params=pltpu.CompilerParams(vmem_limit_bytes=32 << 20),
        cost_estimate=pl.CostEstimate(
            flops=4 * half * order_max * count * columns,
            bytes_accessed=2 * (2 * keep.size + count * shards[0].size),
            transcendentals=0,
        ),
        name="cross",
    )(*[shards[k] for k in order], keep, got)


def synthesis_kernel(tiles, own_ref, got_ref, table_ref, out_ref, held, sems):
    n = table_ref.shape[0] // 2
    flat = (map_rows(got_ref, n // 2, n) + own_ref[...].astype(F32)).astype(BF16)
    width = NPHI // tiles
    copies = []
    for t in range(tiles):
        span = pl.ds(t * width, width)
        summed = jnp.dot(flat, table_ref[:, span], preferred_element_type=F32)
        held[:, span] = summed.astype(BF16)
        copy = pltpu.make_async_copy(held.at[:, span], out_ref.at[:, span], sems.at[t])
        copy.start()
        copies.append(copy)
    for copy in copies:
        copy.wait()


def synthesize(own, got, table):
    tiles = 32
    out_rows = own.shape[0]
    return pl.pallas_call(
        functools.partial(synthesis_kernel, tiles),
        out_shape=jax.ShapeDtypeStruct((out_rows, NPHI), BF16),
        in_specs=[VMEM] * 3,
        out_specs=HBM,
        scratch_shapes=[pltpu.VMEM((out_rows, NPHI), BF16), pltpu.SemaphoreType.DMA((tiles,))],
        compiler_params=pltpu.CompilerParams(vmem_limit_bytes=32 << 20),
        cost_estimate=pl.CostEstimate(
            flops=2 * out_rows * table.size,
            bytes_accessed=2 * (out_rows * NPHI + table.size),
            transcendentals=0,
        ),
        name="synthesis",
    )(own, got, table)


def exchange(value, size, mask):
    return lax.ppermute(value, "mset", [(d, d ^ mask) for d in range(size)])


def gather_shards(value, size, at, line):
    step = size // line
    shards = {0: value}
    for turn in range(1, line):
        pairs = [(d, (d + turn * step) % size) for d in range(size)]
        shards[turn << at] = lax.ppermute(value, "mset", pairs)
    shards[1 << at] = relay(shards[1 << at])
    for b in range(at):
        shards.update({k | 1 << b: exchange(v, size, 1 << b) for k, v in shards.items()})
    return shards


def body(m_list, coeff, blocks, legendre):
    size = lax.axis_size("mset")
    per_device, columns, order_max = coeff.shape
    if per_device != 1 or size & (size - 1):
        raise ValueError("unsupported mesh")
    cycles, n, _ = legendre.shape
    at = min(1, size.bit_length() - 2)
    line = size >> (at + 1)
    filtered, keep, send = prepare(
        m_list, coeff[0], blocks[0], legendre.reshape(cycles * n, order_max), at
    )
    shards = gather_shards(filtered, size, at, line)
    got = exchange(send, size, 1 << at)
    own, back = cross(keep, got, shards, at, line)
    other = exchange(back, size, 1 << at)
    table, own_rows = table_and_own(m_list, own, at, line)
    sky_map = synthesize(own_rows, other, table)
    return sky_map.reshape(cycles, REAL, NPHI)


def solution(mesh):
    in_specs = (
        P(),
        P(("groups", "mset"), None, None),
        P(("groups", "mset"), None, None),
        P(("groups", "mset"), None, None),
    )
    out_specs = P(("groups", "mset"), None, None)
    return jax.shard_map(body, mesh=mesh, in_specs=in_specs, out_specs=out_specs, check_vma=False)
```
